512 devices in a mesh: ctx: 64 (over z, x, core), head: 8 (over y).
Axes of the slice: x: 4, y: 8, z: 8, core: 2. Of those that a mesh axis runs over, the one named last changes fastest.
Arguments:
- queries: bfloat16 [16384, 64, 128], P(('ctx', 'head'))
- keys: bfloat16 [16384, 8, 128], P(('ctx', 'head'))
- values: bfloat16 [16384, 8, 128], P(('ctx', 'head')), may hold values from -6 to 6
- output_gradient: bfloat16 [16384, 64, 128], P(('ctx', 'head')), may hold values from -6 to 6
- kv_list: int32 [128, 8], replicated, may hold values from 0 to 127, as said below
- kv_type: int32 [128, 8], replicated, may hold values from 0 to 3, as said below
- session_id: int32 [16384], replicated, may hold values from 0 to 31, never falling along the last dimension, each value on 1 to 1024 neighbouring positions
Outputs:
- attended: bfloat16 [16384, 64, 128], P(('ctx', 'head'))
- query_gradient: bfloat16 [16384, 64, 128], P(('ctx', 'head'))
- key_grad: bfloat16 [16384, 8, 128], P(('ctx', 'head'))
- value_grad: bfloat16 [16384, 8, 128], P(('ctx', 'head'))
The draws below stay inside these ranges and needn't reach their ends.
Inputs may be any that keep to these rules, and one draw needn't show every extreme that they name: `kv_list`: entry 0 of query block i is block i, and it is the only listed block owned by the same index of ctx as block i. No list names a block twice. The query blocks of one index d of ctx (blocks d * 2 to d * 2 + 1) list at most one block owned by any other index of ctx, and every index but 0 lists exactly one block of index 0. Every query block from 2 on lists block 0 as entry 1. `kv_type`: entry 0 has type 0; entry 1 has type 1 where it names block 0.
All inputs are finite; a program needn't handle non-finite values.
Results may differ from the reference program's by a relative error of at most 0.029.
Values may be sent and summed in bfloat16 or wider, within the bound.
No kernel may reach another device: no remote copies, remote signals or barrier semaphores. Data moves between devices by JAX's collectives and lax.ppermute only.
A program may use at most 64 MiB of HBM per device.

```python
import math
import jax
import jax.numpy as jnp
import numpy as np
from jax import lax

QUERY_HEADS = 64
KEY_VALUE_HEADS = 8
HEAD_SIZE = 128
BLOCK_TOKENS = 128
BLK_DEV = 2
RAND = 6
LISTED_BLOCKS = 8
PACKED_TOKENS = 16384
MASK_BLOCKS = 128
NSESS = 32
SESS_MOST = 1024


def listed_blocks(key):
    device_count = MASK_BLOCKS // BLK_DEV

    def per_device(device_index):
        device_key = jax.random.fold_in(key, device_index)
        shuffled = jax.random.permutation(jax.random.fold_in(device_key, 1), device_count).astype(jnp.int32)
        candidates = jnp.arange(device_count, dtype=jnp.int32)
        barred = (candidates == device_index) | (candidates < 2)
        ranking = shuffled + device_count * barred.astype(jnp.int32)
        chosen = jnp.argsort(ranking)[:BLK_DEV * RAND].reshape(BLK_DEV, RAND).astype(jnp.int32)
        within = jax.random.randint(jax.random.fold_in(device_key, 2), (BLK_DEV, RAND), 0, BLK_DEV)
        random_blocks = chosen * BLK_DEV + within
        random_kinds = jax.random.randint(jax.random.fold_in(device_key, 3), (BLK_DEV, RAND), 1, 4)
        own_blocks = device_index * BLK_DEV + jnp.arange(BLK_DEV, dtype=jnp.int32)
        second_block = jnp.where(device_index == 0, BLK_DEV, 0) * jnp.ones((BLK_DEV,), jnp.int32)
        second_kind = jnp.where(device_index == 0, 2, 1) * jnp.ones((BLK_DEV,), jnp.int32)
        block_lists = jnp.concatenate([own_blocks[:, None], second_block[:, None], random_blocks], 1)
        kind_lists = jnp.concatenate([jnp.zeros((BLK_DEV, 1), jnp.int32), second_kind[:, None], random_kinds], 1)
        return (block_lists.astype(jnp.int32), kind_lists.astype(jnp.int32))
    block_lists, kind_lists = jax.vmap(per_device)(jnp.arange(device_count, dtype=jnp.int32))
    return (block_lists.reshape(MASK_BLOCKS, LISTED_BLOCKS), kind_lists.reshape(MASK_BLOCKS, LISTED_BLOCKS))


def draw_kv_list(key, part):
    shared_entries = listed_blocks(key)
    return shared_entries[0]


def draw_kv_type(key, part):
    shared_entries = listed_blocks(key)
    return shared_entries[1]


def draw_queries(key, part):
    key = jax.random.fold_in(key, 21)
    initial_sample = jnp.clip(jax.random.normal(key, (PACKED_TOKENS, QUERY_HEADS, HEAD_SIZE), jnp.float32), -6.0, 6.0)
    return initial_sample.astype(jnp.bfloat16)


def draw_keys(key, part):
    key = jax.random.fold_in(key, 22)
    initial_sample = jnp.clip(jax.random.normal(key, (PACKED_TOKENS, KEY_VALUE_HEADS, HEAD_SIZE), jnp.float32), -6.0, 6.0)
    return initial_sample.astype(jnp.bfloat16)


def steps_of(key, shape, split, smallest, largest):
    gain, own = 1.0, jax.random.fold_in(key, 6)
    for axis_at, parts in split:
        heights = jnp.exp(jax.random.uniform(jax.random.fold_in(own, axis_at), (parts,), jnp.float32, smallest / len(split), largest / len(split)))
        gain = gain * jnp.repeat(heights, shape[axis_at] // parts).reshape([-1 if axis == axis_at else 1 for axis in range(len(shape))])
    return gain


def split_up(number_of, total, bound, skew):
    portions = [(1 << 20) // math.isqrt(grade ** skew) + 1 for grade in range(2, number_of + 1)]
    rest, given = total - bound - (number_of - 1), [1] * (number_of - 1)
    while rest > 0:
        free = [i for i in range(number_of - 1) if given[i] < bound]
        whole, budget = sum([portions[i] for i in free]), rest
        for i in free:
            addition = min(bound - given[i], max(1, budget * portions[i] // whole), rest)
            given[i] = given[i] + addition
            rest = rest - addition
    return np.array([bound] + given)


def ragged_sizes(stream_key, number_of, total, most, slope):
    if number_of == 2:
        one = jax.random.randint(stream_key, (), max(1, total - most), min(most, total - 1) + 1)
        return jnp.stack([one, total - one])
    lengths = jnp.asarray(split_up(number_of, total, most, slope), jnp.int32)
    pairs = (number_of - 1) // 2
    source_of, sink = lengths[1:1 + 2 * pairs:2], lengths[2:2 + 2 * pairs:2]
    room = jnp.minimum(source_of - 1, most - sink)
    moved = jax.random.randint(jax.random.fold_in(stream_key, 1), (pairs,), 0, 1 << 20) % (room + 1)
    lengths = lengths.at[1:1 + 2 * pairs:2].set(source_of - moved).at[2:2 + 2 * pairs:2].set(sink + moved)
    return lengths[jax.random.permutation(jax.random.fold_in(stream_key, 2), number_of)]


def noise(rng, extent, spread, limit, shards=(), kind=jnp.bfloat16):
    array = spread * jax.random.normal(rng, extent, jnp.float32)
    if shards:
        array = array * steps_of(rng, extent, shards, -0.22, 0.18)
    return jnp.clip(array, -limit, limit).astype(kind)


def setup_inputs(seed: int = 0) -> dict:
    streams_of = jax.random.split(jax.random.key(seed), 8)
    return {
        "queries": draw_queries(jax.random.fold_in(streams_of[7], 71), 0),
        "keys": draw_keys(jax.random.fold_in(streams_of[7], 71), 0),
        "values": noise(streams_of[2], (PACKED_TOKENS, KEY_VALUE_HEADS, HEAD_SIZE), 1.0, 6.0, ((0, 512),)),
        "output_gradient": noise(streams_of[3], (PACKED_TOKENS, QUERY_HEADS, HEAD_SIZE), 1.0, 6.0, ((0, 512),)),
        "kv_list": draw_kv_list(jax.random.fold_in(streams_of[7], 71), 0),
        "kv_type": draw_kv_type(jax.random.fold_in(streams_of[7], 71), 0),
        "session_id": jnp.searchsorted(jnp.cumsum(ragged_sizes(streams_of[6], NSESS, PACKED_TOKENS, SESS_MOST, 1)), jnp.arange(PACKED_TOKENS), side="right").astype(jnp.int32),
    }


def visible(query_pos, key_pos, query_sess, key_sess, kind_rows, block_len):
    query_col = query_pos[:, None, None]
    key_grid = key_pos[None, :, :]
    same_session = query_sess[:, None, None] == key_sess[None, :, :]
    kind_grid = kind_rows[None, :, None]
    causal = (key_grid <= query_col) & same_session
    aligned = (key_grid % block_len) <= (query_col % block_len)
    allowed = jnp.where(kind_grid == 0, causal, jnp.where(kind_grid == 1, jnp.ones_like(causal), jnp.where(kind_grid == 2, same_session, aligned)))
    return allowed.reshape(query_pos.shape[0], -1)


def reference(queries, keys, values, output_gradient, kv_list, kv_type, session_id):
    group_width = QUERY_HEADS // KEY_VALUE_HEADS
    score_scale = HEAD_SIZE ** -0.5
    query_block_rows = queries.reshape(MASK_BLOCKS, BLOCK_TOKENS, KEY_VALUE_HEADS, group_width, HEAD_SIZE)
    gradient_block_rows = output_gradient.reshape(MASK_BLOCKS, BLOCK_TOKENS, KEY_VALUE_HEADS, group_width, HEAD_SIZE)
    key_block_rows = keys.reshape(MASK_BLOCKS, BLOCK_TOKENS, KEY_VALUE_HEADS, HEAD_SIZE)
    value_block_rows = values.reshape(MASK_BLOCKS, BLOCK_TOKENS, KEY_VALUE_HEADS, HEAD_SIZE)
    offsets = jnp.arange(BLOCK_TOKENS, dtype=jnp.int32)

    def step_block(running, block_index):
        key_running, value_running = running
        listed_entries = kv_list[block_index]
        query_pos = (block_index * BLOCK_TOKENS + offsets).astype(jnp.int32)
        key_pos = (listed_entries[:, None] * BLOCK_TOKENS + offsets[None, :]).astype(jnp.int32)
        allowed = visible(query_pos, key_pos, session_id[query_pos], session_id[key_pos], kv_type[block_index], BLOCK_TOKENS)
        key_piece = key_block_rows[listed_entries].reshape(LISTED_BLOCKS * BLOCK_TOKENS, KEY_VALUE_HEADS, HEAD_SIZE).astype(jnp.float32)
        value_piece = value_block_rows[listed_entries].reshape(LISTED_BLOCKS * BLOCK_TOKENS, KEY_VALUE_HEADS, HEAD_SIZE).astype(jnp.float32)
        query_piece = query_block_rows[block_index].astype(jnp.float32)
        gradient_piece = gradient_block_rows[block_index].astype(jnp.float32)
        scores = jnp.einsum("qkgd,skd->kgqs", query_piece, key_piece) * score_scale
        scores = jnp.where(allowed[None, None], scores, -jnp.inf)
        row_max = jnp.max(scores, axis=-1, keepdims=True)
        log_total = row_max + jnp.log(jnp.sum(jnp.exp(scores - row_max), axis=-1, keepdims=True))
        softmax_weight = jnp.exp(scores - log_total).astype(jnp.bfloat16)
        softmax_weight = lax.optimization_barrier(softmax_weight).astype(jnp.float32)
        attended = jnp.einsum("kgqs,skd->qkgd", softmax_weight, value_piece).astype(jnp.bfloat16)
        attended_wide = lax.optimization_barrier(attended).astype(jnp.float32)
        row_dot = jnp.einsum("qkgd,qkgd->kgq", gradient_piece, attended_wide)
        prob_grad = jnp.einsum("qkgd,skd->kgqs", gradient_piece, value_piece)
        score_gradient = (softmax_weight * (prob_grad - row_dot[..., None]) * score_scale).astype(jnp.bfloat16)
        score_gradient = lax.optimization_barrier(score_gradient).astype(jnp.float32)
        query_gradient = jnp.einsum("kgqs,skd->qkgd", score_gradient, key_piece).astype(jnp.bfloat16)
        key_portion = jnp.einsum("anbx,bano->xao", score_gradient, query_piece).reshape(LISTED_BLOCKS, BLOCK_TOKENS, KEY_VALUE_HEADS, HEAD_SIZE)
        value_portion = jnp.einsum("anbx,bano->xao", softmax_weight, gradient_piece).reshape(LISTED_BLOCKS, BLOCK_TOKENS, KEY_VALUE_HEADS, HEAD_SIZE)
        key_running = key_running.at[listed_entries].add(key_portion)
        value_running = value_running.at[listed_entries].add(value_portion)
        return (key_running, value_running), (attended, query_gradient)

    blank_running = jnp.zeros((MASK_BLOCKS, BLOCK_TOKENS, KEY_VALUE_HEADS, HEAD_SIZE), jnp.float32)
    (key_running, value_running), (attended, query_gradient) = lax.scan(step_block, (blank_running, blank_running), jnp.arange(MASK_BLOCKS, dtype=jnp.int32))
    return (attended.reshape(PACKED_TOKENS, QUERY_HEADS, HEAD_SIZE), query_gradient.reshape(PACKED_TOKENS, QUERY_HEADS, HEAD_SIZE), key_running.reshape(PACKED_TOKENS, KEY_VALUE_HEADS, HEAD_SIZE).astype(jnp.bfloat16), value_running.reshape(PACKED_TOKENS, KEY_VALUE_HEADS, HEAD_SIZE).astype(jnp.bfloat16))
```

```python
import functools

import jax
import jax.numpy as jnp
from jax import lax
from jax.experimental import pallas as pl
from jax.experimental.pallas import tpu as pltpu
from jax.sharding import Mesh, PartitionSpec as P

BLOCK = 128
WIDTH = 128
LISTED = 8
ENTRIES = 16
Z, X, CORE, HEAD = 8, 4, 2, 8
CTX = Z * X * CORE
GROUP = 8
QUARTER = 32
MOST = 14
LOG2E = 1.4426950408889634
MIB = 1 << 20

SMEM = pl.BlockSpec(memory_space=pltpu.SMEM)
VMEM = pl.BlockSpec(memory_space=pltpu.VMEM)


def owner_x(block):
    return lax.rem(lax.shift_right_logical(block, 2), X)


def owner_core(block):
    return lax.rem(lax.shift_right_logical(block, 1), CORE)


def slab_row(block):
    return lax.shift_right_logical(block, 4) * 2 + lax.rem(block, 2)


def gather_kernel(place, ent, slot, first, own_ref, oth_ref, s1, s2, s3):
    z, x, core = place[0], place[1], place[2]
    for k, out in ((1, s1), (2, s2), (3, s3)):
        base = (z * (X * CORE) + lax.rem(x + k, X) * CORE + core) * ENTRIES

        @pl.loop(0, ENTRIES)
        def _(e):
            block = ent[base + e]
            row = slab_row(block)
            sl = slot[base + e]
            mine = (first[base + e] == e) & (owner_x(block) == x)
            same_core = owner_core(block) == core

            @pl.when(mine & same_core)
            def _():
                out[sl] = own_ref[row]

            @pl.when(mine & jnp.logical_not(same_core))
            def _():
                out[sl] = oth_ref[row]


def scatter_kernel(place, ent, slot, first, g0, g1, g2, g3, own_out, oth_out, acc):
    z, x, core = place[0], place[1], place[2]
    acc[...] = jnp.zeros_like(acc)
    for k, buf in ((0, g0), (1, g1), (2, g2), (3, g3)):
        base = (z * (X * CORE) + lax.rem(x + k, X) * CORE + core) * ENTRIES

        @pl.loop(0, ENTRIES)
        def _(e):
            block = ent[base + e]
            mine = (first[base + e] == e) & (owner_x(block) == x)

            @pl.when(mine)
            def _():
                away = jnp.where(owner_core(block) == core, 0, ENTRIES)
                row = slab_row(block) + away
                acc[row] += buf[slot[base + e]].astype(jnp.float32)

    own_out[...] = acc[:ENTRIES].astype(jnp.bfloat16)
    oth_out[...] = acc[ENTRIES:].astype(jnp.bfloat16)


def attend_kernel(
    place, ent, kind, slot, first,
    qd, own_ref, oth_ref, r1, r2, r3, sess,
    out, g0, g1, g2, g3,
    kc, vc, kt, vt, mask, s_scr, p_scr, d_scr, dk, dv,
):
    z, x, core = place[0], place[1], place[2]
    me = z * (X * CORE) + x * CORE + core
    base = me * ENTRIES
    scale = WIDTH**-0.5
    rows = 2 * BLOCK
    contract_last = (((1,), (1,)), ((), ()))

    @pl.loop(0, 2)
    def _(b):
        index = me * 2 + b
        sess_q = sess[pl.ds(index, 1), :]
        key_iota = lax.broadcasted_iota(jnp.int32, (BLOCK, BLOCK), 0)
        query_iota = lax.broadcasted_iota(jnp.int32, (BLOCK, BLOCK), 1)

        @pl.loop(0, LISTED)
        def _(l):
            e = base + b * LISTED + l
            block = ent[e]
            row = slab_row(block)
            sl = slot[e]
            away = lax.rem(x - owner_x(block) + X, X)
            same_core = owner_core(block) == core
            at = pl.ds(pl.multiple_of(l * BLOCK, BLOCK), BLOCK)

            def take(tile):
                kc[at, :] = tile[:BLOCK]
                vc[at, :] = tile[BLOCK:]

            @pl.when((away == 0) & same_core)
            def _():
                take(own_ref[row])

            @pl.when((away == 0) & jnp.logical_not(same_core))
            def _():
                take(oth_ref[row])

            for k, buf in ((1, r1), (2, r2), (3, r3)):

                @pl.when(away == k)
                def _():
                    take(buf[sl])

            t = kind[e]
            sess_k = jnp.broadcast_to(sess[pl.ds(block, 1), :], (BLOCK, BLOCK)).T
            needs = jnp.where((t == 0) | (t == 2), 1.0, 0.0)
            shift = jnp.where(t == 0, (block - index) * BLOCK, jnp.where(t == 3, 0, -(1 << 20)))
            seen = ((sess_k - sess_q) * needs == 0.0) & (key_iota + shift <= query_iota)
            mask[at, :] = jnp.where(seen, jnp.inf, -jnp.inf)

        for l in range(LISTED):
            at = slice(l * BLOCK, (l + 1) * BLOCK)
            kt[:, at] = kc[at, :].astype(jnp.float32).T.astype(jnp.bfloat16)
            vt[:, at] = vc[at, :].astype(jnp.float32).T.astype(jnp.bfloat16)

        for l in range(LISTED):
            dk[b * LISTED + l] = jnp.zeros((BLOCK, WIDTH), jnp.float32)
            dv[b * LISTED + l] = jnp.zeros((BLOCK, WIDTH), jnp.float32)

        @pl.loop(0, GROUP // 2)
        def _(pair):
            quarters = pl.ds(b * 4, 4)

            def both(what):
                return jnp.concatenate(
                    [
                        qd[quarters, what, 2 * pair + i].reshape(BLOCK, WIDTH)
                        for i in range(2)
                    ],
                    axis=0,
                )

            q = both(0)
            do = both(1)
            top = jnp.full((8, rows), -jnp.inf, jnp.float32)
            for l in range(LISTED):
                at = slice(l * BLOCK, (l + 1) * BLOCK)
                s = lax.dot_general(
                    kc[at, :], q, contract_last, preferred_element_type=jnp.float32
                )
                m = mask[at, :]
                s = jnp.minimum(s, jnp.concatenate([m, m], axis=1))
                s_scr[at, :] = s
                top = jnp.maximum(top, jnp.max(s.reshape(BLOCK // 8, 8, rows), axis=0))
            top = jnp.max(top, axis=0, keepdims=True)
            total = jnp.zeros((8, rows), jnp.float32)
            for l in range(LISTED):
                at = slice(l * BLOCK, (l + 1) * BLOCK)
                w = jnp.exp2((s_scr[at, :] - top) * (scale * LOG2E))
                s_scr[at, :] = w
                total = total + jnp.sum(w.reshape(BLOCK // 8, 8, rows), axis=0)
            inverse = 1.0 / jnp.sum(total, axis=0, keepdims=True)
            for l in range(LISTED):
                at = slice(l * BLOCK, (l + 1) * BLOCK)
                p_scr[at, :] = (s_scr[at, :] * inverse).astype(jnp.bfloat16)
            o_t = jnp.dot(vt[...], p_scr[...], preferred_element_type=jnp.float32)
            do_t = do.astype(jnp.float32).T
            o_round = o_t.astype(jnp.bfloat16).astype(jnp.float32)
            row_dot = jnp.sum(o_round * do_t, axis=0, keepdims=True)
            scaled = inverse * scale
            for l in range(LISTED):
                at = slice(l * BLOCK, (l + 1) * BLOCK)
                dp = lax.dot_general(
                    vc[at, :], do, contract_last, preferred_element_type=jnp.float32
                )
                ds = ((s_scr[at, :] * scaled) * (dp - row_dot)).astype(jnp.bfloat16)
                d_scr[at, :] = ds
                dk[b * LISTED + l] += jnp.dot(ds, q, preferred_element_type=jnp.float32)
                dv[b * LISTED + l] += jnp.dot(
                    p_scr[at, :], do, preferred_element_type=jnp.float32
                )
            dq_t = jnp.dot(kt[...], d_scr[...], preferred_element_type=jnp.float32)
            o = o_t.T.astype(jnp.bfloat16)
            dq = dq_t.T.astype(jnp.bfloat16)
            for i in range(2):
                at = slice(i * BLOCK, (i + 1) * BLOCK)
                out[quarters, 0, 2 * pair + i] = o[at].reshape(4, QUARTER, WIDTH)
                out[quarters, 1, 2 * pair + i] = dq[at].reshape(4, QUARTER, WIDTH)

    @pl.loop(LISTED, ENTRIES)
    def _(e):
        f = first[base + e]

        @pl.when(f != e)
        def _():
            dk[f] += dk[e]
            dv[f] += dv[e]

    @pl.loop(0, ENTRIES)
    def _(e):
        away = lax.rem(x - owner_x(ent[base + e]) + X, X)
        sl = slot[base + e]
        keep = first[base + e] == e
        for k, buf in ((0, g0), (1, g1), (2, g2), (3, g3)):

            @pl.when(keep & (away == k))
            def _():
                buf[sl, :BLOCK, :] = dk[e].astype(jnp.bfloat16)
                buf[sl, BLOCK:, :] = dv[e].astype(jnp.bfloat16)


def blocks(count):
    return jax.ShapeDtypeStruct((count, 2 * BLOCK, WIDTH), jnp.bfloat16)


def shift(array, axis, by):
    size = lax.axis_size(axis)
    return lax.ppermute(array, axis, [(i, (i + by) % size) for i in range(size)])


def params(mib):
    return pltpu.CompilerParams(vmem_limit_bytes=mib * MIB)


def exchange(array, axis):
    return lax.all_to_all(array, axis, split_axis=0, concat_axis=0, tiled=True)


def per_device(slots, queries, keys, values, output_gradient, kv_list, kv_type, session_id):
    place = jnp.stack(
        [lax.axis_index("z"), lax.axis_index("x"), lax.axis_index("core")]
    ).astype(jnp.int32)

    ent = kv_list.reshape(CTX, ENTRIES)
    order = jnp.arange(ENTRIES, dtype=jnp.int32)
    equal = ent[:, :, None] == ent[:, None, :]
    first = jnp.min(jnp.where(equal, order[None, None, :], ENTRIES), axis=2)
    fresh = first == order[None, :]
    column = owner_x(ent)
    before = (
        fresh[:, None, :]
        & (column[:, :, None] == column[:, None, :])
        & (order[None, None, :] < first[:, :, None])
    )
    slot = jnp.sum(before.astype(jnp.int32), axis=2)
    ent, first, slot = ent.reshape(-1), first.reshape(-1), slot.reshape(-1)
    kind = kv_type.reshape(-1)
    sess = session_id.astype(jnp.float32).reshape(-1, BLOCK)

    kv = jnp.stack([keys, values]).transpose(2, 0, 1, 3)
    kv = exchange(kv, "head")
    kv = kv.reshape(2, 4, 2, QUARTER, WIDTH).transpose(0, 2, 1, 3, 4)
    kv = kv.reshape(1, 2, 2 * BLOCK, WIDTH)
    own = exchange(jnp.broadcast_to(kv, (Z, 2, 2 * BLOCK, WIDTH)), "z")
    own = own.reshape(ENTRIES, 2 * BLOCK, WIDTH)
    other = shift(own, "core", 1)

    sends = pl.pallas_call(
        gather_kernel,
        out_shape=[blocks(slots)] * 3,
        in_specs=[SMEM] * 4 + [VMEM] * 2,
        out_specs=[VMEM] * 3,
        compiler_params=params(16),
    )(place, ent, slot, first, own, other)
    fetched = [shift(sends[k - 1], "x", k) for k in (1, 2, 3)]

    qd = jnp.stack([queries, output_gradient]).reshape(2, QUARTER, HEAD, GROUP, WIDTH)
    qd = qd.transpose(2, 0, 3, 1, 4)
    qd, own = lax.optimization_barrier((qd, own))
    qd = exchange(qd, "head")

    out, g0, g1, g2, g3 = pl.pallas_call(
        attend_kernel,
        out_shape=[jax.ShapeDtypeStruct((HEAD, 2, GROUP, QUARTER, WIDTH), jnp.bfloat16), blocks(ENTRIES)]
        + [blocks(slots)] * 3,
        in_specs=[SMEM] * 5 + [VMEM] * 7,
        out_specs=[VMEM] * 5,
        scratch_shapes=[
            pltpu.VMEM((LISTED * BLOCK, WIDTH), jnp.bfloat16),
            pltpu.VMEM((LISTED * BLOCK, WIDTH), jnp.bfloat16),
            pltpu.VMEM((WIDTH, LISTED * BLOCK), jnp.bfloat16),
            pltpu.VMEM((WIDTH, LISTED * BLOCK), jnp.bfloat16),
            pltpu.VMEM((LISTED * BLOCK, BLOCK), jnp.float32),
            pltpu.VMEM((LISTED * BLOCK, 2 * BLOCK), jnp.float32),
            pltpu.VMEM((LISTED * BLOCK, 2 * BLOCK), jnp.bfloat16),
            pltpu.VMEM((LISTED * BLOCK, 2 * BLOCK), jnp.bfloat16),
            pltpu.VMEM((ENTRIES, BLOCK, WIDTH), jnp.float32),
            pltpu.VMEM((ENTRIES, BLOCK, WIDTH), jnp.float32),
        ],
        compiler_params=params(40),
        cost_estimate=pl.CostEstimate(
            flops=5 * 2 * 2048 * 1024 * 128, bytes_accessed=8 * MIB, transcendentals=2048 * 1024
        ),
    )(place, ent, kind, slot, first, qd, own, other, *fetched, sess)

    returned = [shift(g, "x", -k) for k, g in ((1, g1), (2, g2), (3, g3))]
    out = exchange(out, "head")
    own_sum, other_sum = pl.pallas_call(
        scatter_kernel,
        out_shape=[blocks(ENTRIES)] * 2,
        in_specs=[SMEM] * 4 + [VMEM] * 4,
        out_specs=[VMEM] * 2,
        scratch_shapes=[pltpu.VMEM((2 * ENTRIES, 2 * BLOCK, WIDTH), jnp.float32)],
        compiler_params=params(24),
    )(place, ent, slot, first, g0, *returned)
    from_core = shift(other_sum, "core", 1)
    column_sum = (own_sum.astype(jnp.float32) + from_core.astype(jnp.float32)).astype(jnp.bfloat16)
    parts = exchange(column_sum.reshape(Z, 2, 2, BLOCK, WIDTH), "z")
    total = jnp.sum(parts.astype(jnp.float32), axis=0).astype(jnp.bfloat16)
    total = total.reshape(2, 2, 4, QUARTER, WIDTH).transpose(0, 2, 1, 3, 4)
    total = exchange(total.reshape(HEAD, 2, QUARTER, WIDTH), "head")
    total = total.transpose(1, 2, 0, 3)

    out = out.transpose(1, 3, 0, 2, 4).reshape(2, QUARTER, HEAD * GROUP, WIDTH)
    return out[0], out[1], total[0], total[1]


def solution(mesh):
    fine = Mesh(mesh.devices.reshape(Z, X, CORE, HEAD), ("z", "x", "core", "head"))
    split = P(("z", "x", "core", "head"), None, None)
    return jax.shard_map(
        functools.partial(per_device, MOST),
        mesh=fine,
        in_specs=(split,) * 4 + (P(),) * 3,
        out_specs=(split,) * 4,
        check_vma=False,
    )
```

```python
import functools

import jax
import jax.numpy as jnp
from jax import lax
from jax.experimental import pallas as pl
from jax.experimental.pallas import tpu as pltpu
from jax.sharding import Mesh, PartitionSpec as P

BLOCK = 128
WIDTH = 128
LISTED = 8
ENTRIES = 16
Z, X, CORE, HEAD = 8, 4, 2, 8
CTX = Z * X * CORE
GROUP = 8
QUARTER = 32
MOST = 14
FEW = 9
LOG2E = 1.4426950408889634
MIB = 1 << 20

SMEM = pl.BlockSpec(memory_space=pltpu.SMEM)
VMEM = pl.BlockSpec(memory_space=pltpu.VMEM)


def owner_x(block):
    return lax.rem(lax.shift_right_logical(block, 2), X)


def owner_core(block):
    return lax.rem(lax.shift_right_logical(block, 1), CORE)


def slab_row(block):
    return lax.shift_right_logical(block, 4) * 2 + lax.rem(block, 2)


def gather_kernel(place, ent, slot, first, own_ref, oth_ref, s1, s2, s3):
    z, x, core = place[0], place[1], place[2]
    for k, out in ((1, s1), (2, s2), (3, s3)):
        base = (z * (X * CORE) + lax.rem(x + k, X) * CORE + core) * ENTRIES

        @pl.loop(0, ENTRIES)
        def _(e):
            block = ent[base + e]
            row = slab_row(block)
            sl = slot[base + e]
            mine = (first[base + e] == e) & (owner_x(block) == x)
            same_core = owner_core(block) == core

            @pl.when(mine & same_core)
            def _():
                out[sl] = own_ref[row]

            @pl.when(mine & jnp.logical_not(same_core))
            def _():
                out[sl] = oth_ref[row]


def scatter_kernel(place, ent, slot, first, g0, g1, g2, g3, own_out, oth_out, acc):
    z, x, core = place[0], place[1], place[2]
    acc[...] = jnp.zeros_like(acc)
    for k, buf in ((0, g0), (1, g1), (2, g2), (3, g3)):
        base = (z * (X * CORE) + lax.rem(x + k, X) * CORE + core) * ENTRIES

        @pl.loop(0, ENTRIES)
        def _(e):
            block = ent[base + e]
            mine = (first[base + e] == e) & (owner_x(block) == x)

            @pl.when(mine)
            def _():
                away = jnp.where(owner_core(block) == core, 0, ENTRIES)
                row = slab_row(block) + away
                acc[row] += buf[slot[base + e]].astype(jnp.float32)

    own_out[...] = acc[:ENTRIES].astype(jnp.bfloat16)
    oth_out[...] = acc[ENTRIES:].astype(jnp.bfloat16)


def attend_kernel(
    place, ent, kind, slot, first,
    qd, own_ref, oth_ref, r1, r2, r3, sess,
    out, g0, g1, g2, g3,
    kc, vc, kt, vt, mask, s_scr, p_scr, d_scr, dk, dv,
):
    z, x, core = place[0], place[1], place[2]
    me = z * (X * CORE) + x * CORE + core
    base = me * ENTRIES
    scale = WIDTH**-0.5
    rows = 2 * BLOCK
    contract_last = (((1,), (1,)), ((), ()))

    @pl.loop(0, 2)
    def _(b):
        index = me * 2 + b
        sess_q = sess[pl.ds(index, 1), :]
        key_iota = lax.broadcasted_iota(jnp.int32, (BLOCK, BLOCK), 0)
        query_iota = lax.broadcasted_iota(jnp.int32, (BLOCK, BLOCK), 1)

        @pl.loop(0, LISTED)
        def _(l):
            e = base + b * LISTED + l
            block = ent[e]
            row = slab_row(block)
            sl = slot[e]
            away = lax.rem(x - owner_x(block) + X, X)
            same_core = owner_core(block) == core
            at = pl.ds(pl.multiple_of(l * BLOCK, BLOCK), BLOCK)

            def take(tile):
                tile = tile.reshape(4, 2, QUARTER, WIDTH)
                kc[at, :] = tile[:, 0].reshape(BLOCK, WIDTH)
                vc[at, :] = tile[:, 1].reshape(BLOCK, WIDTH)

            @pl.when((away == 0) & same_core)
            def _():
                take(own_ref[row])

            @pl.when((away == 0) & jnp.logical_not(same_core))
            def _():
                take(oth_ref[row])

            for k, buf in ((1, r1), (2, r2), (3, r3)):

                @pl.when(away == k)
                def _():
                    take(buf[sl])

            t = kind[e]
            sess_k = jnp.broadcast_to(sess[pl.ds(block, 1), :], (BLOCK, BLOCK)).T
            needs = jnp.where((t == 0) | (t == 2), 1.0, 0.0)
            shift = jnp.where(t == 0, (block - index) * BLOCK, jnp.where(t == 3, 0, -(1 << 20)))
            seen = ((sess_k - sess_q) * needs == 0.0) & (key_iota + shift <= query_iota)
            mask[at, :] = jnp.where(seen, jnp.inf, -jnp.inf)

        for l in range(LISTED):
            at = slice(l * BLOCK, (l + 1) * BLOCK)
            kt[:, at] = kc[at, :].astype(jnp.float32).T.astype(jnp.bfloat16)
            vt[:, at] = vc[at, :].astype(jnp.float32).T.astype(jnp.bfloat16)

        for l in range(LISTED):
            dk[b * LISTED + l] = jnp.zeros((BLOCK, WIDTH), jnp.float32)
            dv[b * LISTED + l] = jnp.zeros((BLOCK, WIDTH), jnp.float32)

        @pl.loop(0, GROUP // 2)
        def _(pair):
            quarters = pl.ds(b * 4, 4)

            def both(what):
                return jnp.concatenate(
                    [
                        qd[quarters, what, 2 * pair + i].reshape(BLOCK, WIDTH)
                        for i in range(2)
                    ],
                    axis=0,
                )

            q = both(0)
            do = both(1)
            top = jnp.full((8, rows), -jnp.inf, jnp.float32)
            for l in range(LISTED):
                at = slice(l * BLOCK, (l + 1) * BLOCK)
                s = lax.dot_general(
                    kc[at, :], q, contract_last, preferred_element_type=jnp.float32
                )
                m = mask[at, :]
                s = jnp.minimum(s, jnp.concatenate([m, m], axis=1))
                s_scr[at, :] = s
                top = jnp.maximum(top, jnp.max(s.reshape(BLOCK // 8, 8, rows), axis=0))
            top = jnp.max(top, axis=0, keepdims=True)
            total = jnp.zeros((8, rows), jnp.float32)
            for l in range(LISTED):
                at = slice(l * BLOCK, (l + 1) * BLOCK)
                w = jnp.exp2((s_scr[at, :] - top) * (scale * LOG2E))
                s_scr[at, :] = w
                total = total + jnp.sum(w.reshape(BLOCK // 8, 8, rows), axis=0)
            inverse = 1.0 / jnp.sum(total, axis=0, keepdims=True)
            for l in range(LISTED):
                at = slice(l * BLOCK, (l + 1) * BLOCK)
                p_scr[at, :] = (s_scr[at, :] * inverse).astype(jnp.bfloat16)
            o_t = jnp.dot(vt[...], p_scr[...], preferred_element_type=jnp.float32)
            do_t = do.astype(jnp.float32).T
            o_round = o_t.astype(jnp.bfloat16).astype(jnp.float32)
            row_dot = jnp.sum(o_round * do_t, axis=0, keepdims=True)
            scaled = inverse * scale
            for l in range(LISTED):
                at = slice(l * BLOCK, (l + 1) * BLOCK)
                dp = lax.dot_general(
                    vc[at, :], do, contract_last, preferred_element_type=jnp.float32
                )
                ds = ((s_scr[at, :] * scaled) * (dp - row_dot)).astype(jnp.bfloat16)
                d_scr[at, :] = ds
                dk[b * LISTED + l] += jnp.dot(ds, q, preferred_element_type=jnp.float32)
                dv[b * LISTED + l] += jnp.dot(
                    p_scr[at, :], do, preferred_element_type=jnp.float32
                )
            dq_t = jnp.dot(kt[...], d_scr[...], preferred_element_type=jnp.float32)
            o = o_t.T.astype(jnp.bfloat16)
            dq = dq_t.T.astype(jnp.bfloat16)
            for i in range(2):
                at = slice(i * BLOCK, (i + 1) * BLOCK)
                out[quarters, 0, 2 * pair + i] = o[at].reshape(4, QUARTER, WIDTH)
                out[quarters, 1, 2 * pair + i] = dq[at].reshape(4, QUARTER, WIDTH)

    @pl.loop(LISTED, ENTRIES)
    def _(e):
        f = first[base + e]

        @pl.when(f != e)
        def _():
            dk[f] += dk[e]
            dv[f] += dv[e]

    @pl.loop(0, ENTRIES)
    def _(e):
        away = lax.rem(x - owner_x(ent[base + e]) + X, X)
        sl = slot[base + e]
        keep = first[base + e] == e
        for k, buf in ((0, g0), (1, g1), (2, g2), (3, g3)):

            @pl.when(keep & (away == k))
            def _():
                parts = [dk[e].reshape(4, 1, QUARTER, WIDTH), dv[e].reshape(4, 1, QUARTER, WIDTH)]
                tile = jnp.concatenate(parts, axis=1).astype(jnp.bfloat16)
                buf[sl] = tile.reshape(2 * BLOCK, WIDTH)


def blocks(count):
    return jax.ShapeDtypeStruct((count, 2 * BLOCK, WIDTH), jnp.bfloat16)


def shift(array, axis, by):
    size = lax.axis_size(axis)
    return lax.ppermute(array, axis, [(i, (i + by) % size) for i in range(size)])


def params(mib):
    return pltpu.CompilerParams(vmem_limit_bytes=mib * MIB)


def exchange(array, axis):
    return lax.all_to_all(array, axis, split_axis=0, concat_axis=0, tiled=True)


def between(slots, place, tables, own, queries, output_gradient, sess):
    ent, kind, slot, first = tables
    other = shift(own, "core", 1)
    sends = pl.pallas_call(
        gather_kernel,
        out_shape=[blocks(slots)] * 3,
        in_specs=[SMEM] * 4 + [VMEM] * 2,
        out_specs=[VMEM] * 3,
        compiler_params=params(16),
    )(place, ent, slot, first, own, other)
    fetched = [shift(sends[k - 1], "x", k) for k in (1, 2, 3)]

    qd = jnp.stack([queries, output_gradient]).reshape(2, QUARTER, HEAD, GROUP, WIDTH)
    qd = exchange(qd.transpose(2, 0, 3, 1, 4), "head")

    out, g0, g1, g2, g3 = pl.pallas_call(
        attend_kernel,
        out_shape=[jax.ShapeDtypeStruct((HEAD, 2, GROUP, QUARTER, WIDTH), jnp.bfloat16), blocks(ENTRIES)]
        + [blocks(slots)] * 3,
        in_specs=[SMEM] * 5 + [VMEM] * 7,
        out_specs=[VMEM] * 5,
        scratch_shapes=[
            pltpu.VMEM((LISTED * BLOCK, WIDTH), jnp.bfloat16),
            pltpu.VMEM((LISTED * BLOCK, WIDTH), jnp.bfloat16),
            pltpu.VMEM((WIDTH, LISTED * BLOCK), jnp.bfloat16),
            pltpu.VMEM((WIDTH, LISTED * BLOCK), jnp.bfloat16),
            pltpu.VMEM((LISTED * BLOCK, BLOCK), jnp.float32),
            pltpu.VMEM((LISTED * BLOCK, 2 * BLOCK), jnp.float32),
            pltpu.VMEM((LISTED * BLOCK, 2 * BLOCK), jnp.bfloat16),
            pltpu.VMEM((LISTED * BLOCK, 2 * BLOCK), jnp.bfloat16),
            pltpu.VMEM((ENTRIES, BLOCK, WIDTH), jnp.float32),
            pltpu.VMEM((ENTRIES, BLOCK, WIDTH), jnp.float32),
        ],
        compiler_params=params(40),
        cost_estimate=pl.CostEstimate(
            flops=5 * 2 * 2048 * 1024 * 128, bytes_accessed=8 * MIB, transcendentals=2048 * 1024
        ),
    )(place, ent, kind, slot, first, qd, own, other, *fetched, sess)

    returned = [shift(g, "x", -k) for k, g in ((1, g1), (2, g2), (3, g3))]
    out = exchange(out, "head")
    *returned, out = lax.optimization_barrier((*returned, out))
    own_sum, other_sum = pl.pallas_call(
        scatter_kernel,
        out_shape=[blocks(ENTRIES)] * 2,
        in_specs=[SMEM] * 4 + [VMEM] * 4,
        out_specs=[VMEM] * 2,
        scratch_shapes=[pltpu.VMEM((2 * ENTRIES, 2 * BLOCK, WIDTH), jnp.float32)],
        compiler_params=params(24),
    )(place, ent, slot, first, g0, *returned)
    return out, own_sum, other_sum


def per_device(queries, keys, values, output_gradient, kv_list, kv_type, session_id):
    where = [lax.axis_index(axis) for axis in ("z", "x", "core")]
    place = jnp.stack(where).astype(jnp.int32)

    ent = kv_list.reshape(CTX, ENTRIES)
    order = jnp.arange(ENTRIES, dtype=jnp.int32)
    equal = ent[:, :, None] == ent[:, None, :]
    first = jnp.min(jnp.where(equal, order[None, None, :], ENTRIES), axis=2)
    fresh = first == order[None, :]
    column = owner_x(ent)
    before = (
        fresh[:, None, :]
        & (column[:, :, None] == column[:, None, :])
        & (order[None, None, :] < first[:, :, None])
    )
    slot = jnp.sum(before.astype(jnp.int32), axis=2)
    home = lax.rem(jnp.arange(CTX, dtype=jnp.int32) // CORE, X)
    most = jnp.max(jnp.where(column == home[:, None], 0, slot + 1))
    tables = (ent.reshape(-1), kv_type.reshape(-1), slot.reshape(-1), first.reshape(-1))
    sess = session_id.astype(jnp.float32).reshape(-1, BLOCK)

    kv = jnp.stack([keys, values]).transpose(2, 0, 1, 3)
    kv = jnp.broadcast_to(kv, (Z, HEAD, 2, QUARTER, WIDTH))
    own = exchange(kv.reshape(Z * HEAD, 2, QUARTER, WIDTH), ("z", "head"))
    own = own.reshape(ENTRIES, 2 * BLOCK, WIDTH)

    out, own_sum, other_sum = lax.cond(
        most <= FEW,
        functools.partial(between, FEW),
        functools.partial(between, MOST),
        place, tables, own, queries, output_gradient, sess,
    )

    from_core = shift(other_sum, "core", 1)
    column_sum = (own_sum.astype(jnp.float32) + from_core.astype(jnp.float32)).astype(jnp.bfloat16)
    parts = exchange(column_sum.reshape(Z * HEAD, 2, QUARTER, WIDTH), ("z", "head"))
    parts = parts.reshape(Z, HEAD, 2, QUARTER, WIDTH)
    total = jnp.sum(parts.astype(jnp.float32), axis=0).astype(jnp.bfloat16)
    total = total.transpose(1, 2, 0, 3)

    out = out.transpose(1, 3, 0, 2, 4).reshape(2, QUARTER, HEAD * GROUP, WIDTH)
    return out[0], out[1], total[0], total[1]


def solution(mesh):
    fine = Mesh(mesh.devices.reshape(Z, X, CORE, HEAD), ("z", "x", "core", "head"))
    split = P(("z", "x", "core", "head"), None, None)
    return jax.shard_map(
        per_device,
        mesh=fine,
        in_specs=(split,) * 4 + (P(),) * 3,
        out_specs=(split,) * 4,
        check_vma=False,
    )
```

```python
import functools

import jax
import jax.numpy as jnp
from jax import lax
from jax.experimental import pallas as pl
from jax.experimental.pallas import tpu as pltpu
from jax.sharding import Mesh, PartitionSpec as P

BLOCK = 128
WIDTH = 128
LISTED = 8
ENTRIES = 16
Z, X, CORE, HEAD = 8, 4, 2, 8
CTX = Z * X * CORE
GROUP = 8
QUARTER = 32
SLOTS = (7, 8, 9, 14)
LOG2E = 1.4426950408889634
MIB = 1 << 20

SMEM = pl.BlockSpec(memory_space=pltpu.SMEM)
VMEM = pl.BlockSpec(memory_space=pltpu.VMEM)


def owner_x(block):
    return lax.rem(lax.shift_right_logical(block, 2), X)


def owner_core(block):
    return lax.rem(lax.shift_right_logical(block, 1), CORE)


def slab_row(block):
    return lax.shift_right_logical(block, 4) * 2 + lax.rem(block, 2)


def gather_kernel(place, ent, slot, first, own_ref, oth_ref, s1, s2, s3):
    z, x, core = place[0], place[1], place[2]
    for k, out in ((1, s1), (2, s2), (3, s3)):
        base = (z * (X * CORE) + lax.rem(x + k, X) * CORE + core) * ENTRIES

        @pl.loop(0, ENTRIES)
        def _(e):
            block = ent[base + e]
            row = slab_row(block)
            sl = slot[base + e]
            mine = (first[base + e] == e) & (owner_x(block) == x)
            same_core = owner_core(block) == core

            @pl.when(mine & same_core)
            def _():
                out[sl] = own_ref[row]

            @pl.when(mine & jnp.logical_not(same_core))
            def _():
                out[sl] = oth_ref[row]


def scatter_kernel(place, ent, slot, first, g0, g1, g2, g3, own_out, oth_out, acc):
    z, x, core = place[0], place[1], place[2]
    acc[...] = jnp.zeros_like(acc)
    for k, buf in ((0, g0), (1, g1), (2, g2), (3, g3)):
        base = (z * (X * CORE) + lax.rem(x + k, X) * CORE + core) * ENTRIES

        @pl.loop(0, ENTRIES)
        def _(e):
            block = ent[base + e]
            mine = (first[base + e] == e) & (owner_x(block) == x)

            @pl.when(mine)
            def _():
                away = jnp.where(owner_core(block) == core, 0, ENTRIES)
                row = slab_row(block) + away
                acc[row] += buf[slot[base + e]].astype(jnp.float32)

    own_out[...] = acc[:ENTRIES].astype(jnp.bfloat16)
    oth_out[...] = acc[ENTRIES:].astype(jnp.bfloat16)


def mask_kernel(place, ent, kind, sess, mask):
    me = (place[0] * X + place[1]) * CORE + place[2]
    key_iota = lax.broadcasted_iota(jnp.int32, (BLOCK, BLOCK), 0)
    query_iota = lax.broadcasted_iota(jnp.int32, (BLOCK, BLOCK), 1)

    @pl.loop(0, ENTRIES)
    def _(e):
        index = me * 2 + e // LISTED
        block, t = ent[me * ENTRIES + e], kind[me * ENTRIES + e]
        sess_q = sess[pl.ds(index, 1), :]
        sess_k = jnp.broadcast_to(sess[pl.ds(block, 1), :], (BLOCK, BLOCK)).T
        needs = jnp.where((t == 0) | (t == 2), 1.0, 0.0)
        shift = jnp.where(t == 0, (block - index) * BLOCK, jnp.where(t == 3, 0, -(1 << 20)))
        seen = ((sess_k - sess_q) * needs == 0.0) & (key_iota + shift <= query_iota)
        mask[e] = jnp.where(seen, jnp.inf, -jnp.inf)


def attend_kernel(
    place, ent, slot, first,
    qd, own_ref, oth_ref, r1, r2, r3, mask,
    out, g0, g1, g2, g3,
    kc, vc, kt, vt, qs, dos, s_scr, p_scr, d_scr, dk, dv,
):
    z, x, core = place[0], place[1], place[2]
    me = z * (X * CORE) + x * CORE + core
    base = me * ENTRIES
    scale = WIDTH**-0.5
    rows = 2 * BLOCK
    contract_last = (((1,), (1,)), ((), ()))

    @pl.loop(0, 2)
    def _(b):
        @pl.loop(0, LISTED)
        def _(l):
            e = base + b * LISTED + l
            block = ent[e]
            row = slab_row(block)
            sl = slot[e]
            away = lax.rem(x - owner_x(block) + X, X)
            same_core = owner_core(block) == core
            at = pl.ds(pl.multiple_of(l * BLOCK, BLOCK), BLOCK)

            def take(tile):
                tile = tile.reshape(4, 2, QUARTER, WIDTH)
                kc[at, :] = tile[:, 0].reshape(BLOCK, WIDTH)
                vc[at, :] = tile[:, 1].reshape(BLOCK, WIDTH)

            @pl.when((away == 0) & same_core)
            def _():
                take(own_ref[row])

            @pl.when((away == 0) & jnp.logical_not(same_core))
            def _():
                take(oth_ref[row])

            for k, buf in ((1, r1), (2, r2), (3, r3)):

                @pl.when(away == k)
                def _():
                    take(buf[sl])

        for l in range(LISTED):
            at = slice(l * BLOCK, (l + 1) * BLOCK)
            kt[:, at] = kc[at, :].astype(jnp.float32).T.astype(jnp.bfloat16)
            vt[:, at] = vc[at, :].astype(jnp.float32).T.astype(jnp.bfloat16)

        quarters = pl.ds(b * 4, 4)
        for g in range(GROUP):
            at = slice(g * BLOCK, (g + 1) * BLOCK)
            qs[at, :] = qd[quarters, 0, g].reshape(BLOCK, WIDTH)
            dos[at, :] = qd[quarters, 1, g].reshape(BLOCK, WIDTH)

        def score(pair):
            q = qs[pair * rows : (pair + 1) * rows, :]
            top = jnp.full((8, rows), -jnp.inf, jnp.float32)
            for l in range(LISTED):
                at = slice(l * BLOCK, (l + 1) * BLOCK)
                s = lax.dot_general(
                    kc[at, :], q, contract_last, preferred_element_type=jnp.float32
                )
                m = mask[b * LISTED + l]
                s = jnp.minimum(s, jnp.concatenate([m, m], axis=1))
                s_scr[pair % 2, at, :] = s
                top = jnp.maximum(top, jnp.max(s.reshape(BLOCK // 8, 8, rows), axis=0))
            return jnp.max(top, axis=0, keepdims=True)

        top = score(0)
        for pair in range(GROUP // 2):
            cols = slice(pair * rows, (pair + 1) * rows)
            now = pair % 2
            total = jnp.zeros((8, rows), jnp.float32)
            for l in range(LISTED):
                at = slice(l * BLOCK, (l + 1) * BLOCK)
                w = jnp.exp2((s_scr[now, at, :] - top) * (scale * LOG2E))
                s_scr[now, at, :] = w
                total = total + jnp.sum(w.reshape(BLOCK // 8, 8, rows), axis=0)
            inverse = 1.0 / jnp.sum(total, axis=0, keepdims=True)
            if pair < GROUP // 2 - 1:
                top = score(pair + 1)
            for l in range(LISTED):
                at = slice(l * BLOCK, (l + 1) * BLOCK)
                p_scr[at, cols] = (s_scr[now, at, :] * inverse).astype(jnp.bfloat16)
            o_t = jnp.dot(vt[...], p_scr[:, cols], preferred_element_type=jnp.float32)
            do = dos[cols, :]
            do_t = do.astype(jnp.float32).T
            o_round = o_t.astype(jnp.bfloat16).astype(jnp.float32)
            row_dot = jnp.sum(o_round * do_t, axis=0, keepdims=True)
            scaled = inverse * scale
            for l in range(LISTED):
                at = slice(l * BLOCK, (l + 1) * BLOCK)
                dp = lax.dot_general(
                    vc[at, :], do, contract_last, preferred_element_type=jnp.float32
                )
                ds = ((s_scr[now, at, :] * scaled) * (dp - row_dot)).astype(jnp.bfloat16)
                d_scr[at, cols] = ds
            dq_t = jnp.dot(kt[...], d_scr[:, cols], preferred_element_type=jnp.float32)
            o = o_t.T.astype(jnp.bfloat16)
            dq = dq_t.T.astype(jnp.bfloat16)
            for i in range(2):
                at = slice(i * BLOCK, (i + 1) * BLOCK)
                out[quarters, 0, 2 * pair + i] = o[at].reshape(4, QUARTER, WIDTH)
                out[quarters, 1, 2 * pair + i] = dq[at].reshape(4, QUARTER, WIDTH)

        here = pl.ds(b * LISTED, LISTED)
        dk[here] = jnp.dot(d_scr[...], qs[...], preferred_element_type=jnp.float32).reshape(LISTED, BLOCK, WIDTH)
        dv[here] = jnp.dot(p_scr[...], dos[...], preferred_element_type=jnp.float32).reshape(LISTED, BLOCK, WIDTH)

    @pl.loop(LISTED, ENTRIES)
    def _(e):
        f = first[base + e]

        @pl.when(f != e)
        def _():
            dk[f] += dk[e]
            dv[f] += dv[e]

    @pl.loop(0, ENTRIES)
    def _(e):
        away = lax.rem(x - owner_x(ent[base + e]) + X, X)
        sl = slot[base + e]
        keep = first[base + e] == e
        for k, buf in ((0, g0), (1, g1), (2, g2), (3, g3)):

            @pl.when(keep & (away == k))
            def _():
                parts = [dk[e].reshape(4, 1, QUARTER, WIDTH), dv[e].reshape(4, 1, QUARTER, WIDTH)]
                tile = jnp.concatenate(parts, axis=1).astype(jnp.bfloat16)
                buf[sl] = tile.reshape(2 * BLOCK, WIDTH)


def blocks(count):
    return jax.ShapeDtypeStruct((count, 2 * BLOCK, WIDTH), jnp.bfloat16)


def shift(array, axis, by):
    size = lax.axis_size(axis)
    return lax.ppermute(array, axis, [(i, (i + by) % size) for i in range(size)])


def params(mib):
    return pltpu.CompilerParams(vmem_limit_bytes=mib * MIB)


def exchange(array, axis):
    return lax.all_to_all(array, axis, split_axis=0, concat_axis=0, tiled=True)


def masks(*operands):
    return pl.pallas_call(
        mask_kernel,
        out_shape=jax.ShapeDtypeStruct((ENTRIES, BLOCK, BLOCK), jnp.float32),
        in_specs=[SMEM] * 3 + [VMEM],
        out_specs=VMEM,
        compiler_params=params(4),
        cost_estimate=pl.CostEstimate(flops=ENTRIES * BLOCK * BLOCK * 8, bytes_accessed=MIB, transcendentals=0),
    )(*operands)


def attend(slots, *operands):
    return pl.pallas_call(
        attend_kernel,
        out_shape=[jax.ShapeDtypeStruct((HEAD, 2, GROUP, QUARTER, WIDTH), jnp.bfloat16), blocks(ENTRIES)]
        + [blocks(slots)] * 3,
        in_specs=[SMEM] * 4 + [VMEM] * 7,
        out_specs=[VMEM] * 5,
        scratch_shapes=[
            pltpu.VMEM((LISTED * BLOCK, WIDTH), jnp.bfloat16),
            pltpu.VMEM((LISTED * BLOCK, WIDTH), jnp.bfloat16),
            pltpu.VMEM((WIDTH, LISTED * BLOCK), jnp.bfloat16),
            pltpu.VMEM((WIDTH, LISTED * BLOCK), jnp.bfloat16),
            pltpu.VMEM((GROUP * BLOCK, WIDTH), jnp.bfloat16),
            pltpu.VMEM((GROUP * BLOCK, WIDTH), jnp.bfloat16),
            pltpu.VMEM((2, LISTED * BLOCK, 2 * BLOCK), jnp.float32),
            pltpu.VMEM((LISTED * BLOCK, GROUP * BLOCK), jnp.bfloat16),
            pltpu.VMEM((LISTED * BLOCK, GROUP * BLOCK), jnp.bfloat16),
            pltpu.VMEM((ENTRIES, BLOCK, WIDTH), jnp.float32),
            pltpu.VMEM((ENTRIES, BLOCK, WIDTH), jnp.float32),
        ],
        compiler_params=params(24),
        cost_estimate=pl.CostEstimate(
            flops=5 * 2 * 2048 * 1024 * 128, bytes_accessed=8 * MIB, transcendentals=2048 * 1024
        ),
    )(*operands)


def between(slots, place, tables, own, queries, output_gradient, sess):
    ent, kind, slot, first = tables
    other = shift(own, "core", 1)
    sends = pl.pallas_call(
        gather_kernel,
        out_shape=[blocks(slots)] * 3,
        in_specs=[SMEM] * 4 + [VMEM] * 2,
        out_specs=[VMEM] * 3,
        compiler_params=params(8),
    )(place, ent, slot, first, own, other)
    now, *sends = lax.optimization_barrier((place, *sends))
    fetched = [shift(sends[k - 1], "x", k) for k in (1, 2, 3)]
    mask = masks(now, ent, kind, sess)

    qd = jnp.stack([queries, output_gradient]).reshape(2, QUARTER, HEAD, GROUP, WIDTH)
    qd = exchange(qd.transpose(2, 0, 3, 1, 4), "head")

    out, g0, g1, g2, g3 = attend(
        slots, place, ent, slot, first, qd, own, other, *fetched, mask
    )

    returned = [shift(g, "x", -k) for k, g in ((1, g1), (2, g2), (3, g3))]
    out = exchange(out, "head")
    *returned, out = lax.optimization_barrier((*returned, out))
    own_sum, other_sum = pl.pallas_call(
        scatter_kernel,
        out_shape=[blocks(ENTRIES)] * 2,
        in_specs=[SMEM] * 4 + [VMEM] * 4,
        out_specs=[VMEM] * 2,
        scratch_shapes=[pltpu.VMEM((2 * ENTRIES, 2 * BLOCK, WIDTH), jnp.float32)],
        compiler_params=params(14),
    )(place, ent, slot, first, g0, *returned)
    return out, own_sum, other_sum


def per_device(queries, keys, values, output_gradient, kv_list, kv_type, session_id):
    where = [lax.axis_index(axis) for axis in ("z", "x", "core")]
    place = jnp.stack(where).astype(jnp.int32)

    ent = kv_list.reshape(CTX, ENTRIES)
    order = jnp.arange(ENTRIES, dtype=jnp.int32)
    equal = ent[:, :, None] == ent[:, None, :]
    first = jnp.min(jnp.where(equal, order[None, None, :], ENTRIES), axis=2)
    fresh = first == order[None, :]
    column = owner_x(ent)
    before = (
        fresh[:, None, :]
        & (column[:, :, None] == column[:, None, :])
        & (order[None, None, :] < first[:, :, None])
    )
    slot = jnp.sum(before.astype(jnp.int32), axis=2)
    home = lax.rem(jnp.arange(CTX, dtype=jnp.int32) // CORE, X)
    most = jnp.max(jnp.where(column == home[:, None], 0, slot + 1))
    tables = (ent.reshape(-1), kv_type.reshape(-1), slot.reshape(-1), first.reshape(-1))
    sess = session_id.astype(jnp.float32).reshape(-1, BLOCK)

    kv = jnp.stack([keys, values]).transpose(2, 0, 1, 3)
    kv = jnp.broadcast_to(kv, (Z, HEAD, 2, QUARTER, WIDTH))
    own = exchange(kv.reshape(Z * HEAD, 2, QUARTER, WIDTH), ("z", "head"))
    own = own.reshape(ENTRIES, 2 * BLOCK, WIDTH)

    out, own_sum, other_sum = lax.switch(
        sum((most > few).astype(jnp.int32) for few in SLOTS[:-1]),
        [functools.partial(between, slots) for slots in SLOTS],
        place, tables, own, queries, output_gradient, sess,
    )

    from_core = shift(other_sum, "core", 1)
    column_sum = (own_sum.astype(jnp.float32) + from_core.astype(jnp.float32)).astype(jnp.bfloat16)
    parts = exchange(column_sum.reshape(Z * HEAD, 2, QUARTER, WIDTH), ("z", "head"))
    parts = parts.reshape(Z, HEAD, 2, QUARTER, WIDTH)
    total = jnp.sum(parts.astype(jnp.float32), axis=0).astype(jnp.bfloat16)
    total = total.transpose(1, 2, 0, 3)

    out = out.transpose(1, 3, 0, 2, 4).reshape(2, QUARTER, HEAD * GROUP, WIDTH)
    return out[0], out[1], total[0], total[1]


def solution(mesh):
    fine = Mesh(mesh.devices.reshape(Z, X, CORE, HEAD), ("z", "x", "core", "head"))
    split = P(("z", "x", "core", "head"), None, None)
    return jax.shard_map(
        per_device,
        mesh=fine,
        in_specs=(split,) * 4 + (P(),) * 3,
        out_specs=(split,) * 4,
        check_vma=False,
    )
```

```python
import functools

import jax
import jax.numpy as jnp
from jax import lax
from jax.experimental import pallas as pl
from jax.experimental.pallas import tpu as pltpu
from jax.sharding import Mesh, PartitionSpec as P

BLOCK = 128
WIDTH = 128
LISTED = 8
ENTRIES = 16
Z, X, CORE, HEAD = 8, 4, 2, 8
CTX = Z * X * CORE
GROUP = 8
QUARTER = 32
SLOTS = (7, 8, 9, 14)
LOG2E = 1.4426950408889634
MIB = 1 << 20

SMEM = pl.BlockSpec(memory_space=pltpu.SMEM)
VMEM = pl.BlockSpec(memory_space=pltpu.VMEM)
HBM = pl.BlockSpec(memory_space=pltpu.HBM)
DMA = pltpu.SemaphoreType.DMA


def fields(code):
    bits, parts = (4, 1, 2, 4, 1), []
    for bit in bits:
        parts.append(code & ((1 << bit) - 1))
        code = lax.shift_right_logical(code, bit)
    return (*parts, code)


def coded(kv_list):
    ent = kv_list.reshape(CTX, ENTRIES)
    order = jnp.arange(ENTRIES, dtype=jnp.int32)
    equal = ent[:, :, None] == ent[:, None, :]
    first = jnp.min(jnp.where(equal, order[None, None, :], ENTRIES), axis=2)
    fresh = first == order[None, :]
    column = lax.rem(ent // 4, X)
    before = (
        fresh[:, None, :]
        & (column[:, :, None] == column[:, None, :])
        & (order[None, None, :] < first[:, :, None])
    )
    slot = jnp.sum(before.astype(jnp.int32), axis=2)
    home = lax.rem(jnp.arange(CTX, dtype=jnp.int32) // CORE, X)
    most = jnp.max(jnp.where(column == home[:, None], 0, slot + 1))
    row = ent // 16 * 2 + lax.rem(ent, 2)
    core = lax.rem(ent // 2, CORE)
    code = slot + 16 * (fresh.astype(jnp.int32) + 2 * first)
    code = row + 16 * (core + CORE * (column + X * code))
    return code.reshape(-1), most


def neighbour_entries(place, code, k, what):
    z, x, core = place[0], place[1], place[2]
    base = ((z * X + ((x + k) & (X - 1))) * CORE + core) * ENTRIES

    @pl.loop(0, ENTRIES)
    def _(e):
        row, owner_core, owner_x, sl, fresh, _ = fields(code[base + e])

        @pl.when((fresh == 1) & (owner_x == x))
        def _():
            what(e, row, owner_core == core, sl)


def gather_kernel(place, code, own, oth, s1, s2, s3, sem):
    def all_copies(act):
        for k, out in ((1, s1), (2, s2), (3, s3)):

            def one(e, row, same_core, sl, k=k, out=out):
                for source, chosen in ((own, same_core), (oth, jnp.logical_not(same_core))):

                    @pl.when(chosen)
                    def _(source=source):
                        done = sem.at[(k - 1) * ENTRIES + e]
                        act(pltpu.make_async_copy(source.at[row], out.at[sl], done))

            neighbour_entries(place, code, k, one)

    all_copies(lambda copy: copy.start())
    all_copies(lambda copy: copy.wait())


def scatter_kernel(place, code, g0, g1, g2, g3, own_out, oth_out, stage, acc, sem):
    buffers = ((0, g0), (1, g1), (2, g2), (3, g3))

    def copy(k, buf, e, sl):
        place_of = k * ENTRIES + e
        return pltpu.make_async_copy(buf.at[sl], stage.at[place_of], sem.at[place_of])

    for k, buf in buffers:

        def start(e, row, same_core, sl, k=k, buf=buf):
            copy(k, buf, e, sl).start()

        neighbour_entries(place, code, k, start)

    acc[...] = jnp.zeros_like(acc)
    for k, buf in buffers:

        def add(e, row, same_core, sl, k=k, buf=buf):
            copy(k, buf, e, sl).wait()
            to = row + jnp.where(same_core, 0, ENTRIES)
            acc[to] += stage[k * ENTRIES + e].astype(jnp.float32)

        neighbour_entries(place, code, k, add)

    own_out[...] = acc[:ENTRIES].astype(jnp.bfloat16)
    oth_out[...] = acc[ENTRIES:].astype(jnp.bfloat16)


def mask_kernel(place, ent, kind, sess, mask):
    me = (place[0] * X + place[1]) * CORE + place[2]
    key_iota = lax.broadcasted_iota(jnp.int32, (BLOCK, BLOCK), 0)
    query_iota = lax.broadcasted_iota(jnp.int32, (BLOCK, BLOCK), 1)

    @pl.loop(0, ENTRIES)
    def _(e):
        index = me * 2 + e // LISTED
        block, t = ent[me * ENTRIES + e], kind[me * ENTRIES + e]
        sess_q = sess[pl.ds(index, 1), :]
        sess_k = jnp.broadcast_to(sess[pl.ds(block, 1), :], (BLOCK, BLOCK)).T
        needs = jnp.where((t == 0) | (t == 2), 1.0, 0.0)
        shift = jnp.where(t == 0, (block - index) * BLOCK, jnp.where(t == 3, 0, -(1 << 20)))
        seen = ((sess_k - sess_q) * needs == 0.0) & (key_iota + shift <= query_iota)
        mask[e] = jnp.where(seen, jnp.inf, -jnp.inf)


def attend_kernel(
    place, code, qd_in, own, oth, r1, r2, r3, mask_in,
    out_to, g0, g1, g2, g3,
    qd, tiles, mask, out, kc, vc, kt, vt, qs, dos, s_scr, p_scr, d_scr, dk, dv,
    tile_sem, part_sem, out_sem, back_sem,
):
    z, x, core = place[0], place[1], place[2]
    base = ((z * X + x) * CORE + core) * ENTRIES
    scale = WIDTH**-0.5
    rows = 2 * BLOCK
    contract_last = (((1,), (1,)), ((), ()))

    def query_copy(b):
        half = pl.ds(b * 4, 4)
        return pltpu.make_async_copy(qd_in.at[half], qd.at[half], part_sem.at[0, b])

    def mask_copy(b):
        half = pl.ds(b * LISTED, LISTED)
        return pltpu.make_async_copy(mask_in.at[half], mask.at[half], part_sem.at[1, b])

    def out_copy(b):
        half = pl.ds(b * 4, 4)
        return pltpu.make_async_copy(out.at[half], out_to.at[half], out_sem.at[b])

    @pl.loop(0, 2)
    def _(b):
        query_copy(b).start()
        mask_copy(b).start()

        @pl.loop(0, LISTED)
        def _(l):
            e = b * LISTED + l
            row, owner_core, owner_x, sl, _, _ = fields(code[base + e])
            away = (x - owner_x) & (X - 1)
            here = (away == 0) & (owner_core == core)
            beside = (away == 0) & (owner_core != core)
            sources = ((own, row, here), (oth, row, beside), (r1, sl, away == 1))
            sources += ((r2, sl, away == 2), (r3, sl, away == 3))
            for source, at, chosen in sources:

                @pl.when(chosen)
                def _(source=source, at=at):
                    pltpu.make_async_copy(source.at[at], tiles.at[e], tile_sem.at[e]).start()

    @pl.loop(0, 2)
    def _(b):
        query_copy(b).wait()
        mask_copy(b).wait()

        @pl.loop(0, LISTED)
        def _(l):
            e = b * LISTED + l
            pltpu.make_async_copy(own.at[0], tiles.at[e], tile_sem.at[e]).wait()

        for l in range(LISTED):
            at = slice(l * BLOCK, (l + 1) * BLOCK)
            tile = tiles[b * LISTED + l].reshape(4, 2, QUARTER, WIDTH)
            kc[at, :] = tile[:, 0].reshape(BLOCK, WIDTH)
            vc[at, :] = tile[:, 1].reshape(BLOCK, WIDTH)

        for l in range(LISTED):
            at = slice(l * BLOCK, (l + 1) * BLOCK)
            kt[:, at] = kc[at, :].astype(jnp.float32).T.astype(jnp.bfloat16)
            vt[:, at] = vc[at, :].astype(jnp.float32).T.astype(jnp.bfloat16)

        quarters = pl.ds(b * 4, 4)
        for g in range(GROUP):
            at = slice(g * BLOCK, (g + 1) * BLOCK)
            qs[at, :] = qd[quarters, 0, g].reshape(BLOCK, WIDTH)
            dos[at, :] = qd[quarters, 1, g].reshape(BLOCK, WIDTH)

        def score(pair):
            q = qs[pair * rows : (pair + 1) * rows, :]
            top = jnp.full((8, rows), -jnp.inf, jnp.float32)
            for l in range(LISTED):
                at = slice(l * BLOCK, (l + 1) * BLOCK)
                s = lax.dot_general(
                    kc[at, :], q, contract_last, preferred_element_type=jnp.float32
                )
                m = mask[b * LISTED + l]
                s = jnp.minimum(s, jnp.concatenate([m, m], axis=1))
                s_scr[pair % 2, at, :] = s
                top = jnp.maximum(top, jnp.max(s.reshape(BLOCK // 8, 8, rows), axis=0))
            return jnp.max(top, axis=0, keepdims=True)

        top = score(0)
        for pair in range(GROUP // 2):
            cols = slice(pair * rows, (pair + 1) * rows)
            now = pair % 2
            total = jnp.zeros((8, rows), jnp.float32)
            for l in range(LISTED):
                at = slice(l * BLOCK, (l + 1) * BLOCK)
                w = jnp.exp2((s_scr[now, at, :] - top) * (scale * LOG2E))
                s_scr[now, at, :] = w
                total = total + jnp.sum(w.reshape(BLOCK // 8, 8, rows), axis=0)
            inverse = 1.0 / jnp.sum(total, axis=0, keepdims=True)
            if pair < GROUP // 2 - 1:
                top = score(pair + 1)
            for l in range(LISTED):
                at = slice(l * BLOCK, (l + 1) * BLOCK)
                p_scr[at, cols] = (s_scr[now, at, :] * inverse).astype(jnp.bfloat16)
            o_t = jnp.dot(vt[...], p_scr[:, cols], preferred_element_type=jnp.float32)
            do = dos[cols, :]
            do_t = do.astype(jnp.float32).T
            o_round = o_t.astype(jnp.bfloat16).astype(jnp.float32)
            row_dot = jnp.sum(o_round * do_t, axis=0, keepdims=True)
            scaled = inverse * scale
            for l in range(LISTED):
                at = slice(l * BLOCK, (l + 1) * BLOCK)
                dp = lax.dot_general(
                    vc[at, :], do, contract_last, preferred_element_type=jnp.float32
                )
                ds = ((s_scr[now, at, :] * scaled) * (dp - row_dot)).astype(jnp.bfloat16)
                d_scr[at, cols] = ds
            dq_t = jnp.dot(kt[...], d_scr[:, cols], preferred_element_type=jnp.float32)
            o = o_t.T.astype(jnp.bfloat16)
            dq = dq_t.T.astype(jnp.bfloat16)
            for i in range(2):
                at = slice(i * BLOCK, (i + 1) * BLOCK)
                out[quarters, 0, 2 * pair + i] = o[at].reshape(4, QUARTER, WIDTH)
                out[quarters, 1, 2 * pair + i] = dq[at].reshape(4, QUARTER, WIDTH)

        here = pl.ds(b * LISTED, LISTED)
        dk[here] = jnp.dot(d_scr[...], qs[...], preferred_element_type=jnp.float32).reshape(LISTED, BLOCK, WIDTH)
        dv[here] = jnp.dot(p_scr[...], dos[...], preferred_element_type=jnp.float32).reshape(LISTED, BLOCK, WIDTH)

        out_copy(b).start()

    @pl.loop(LISTED, ENTRIES)
    def _(e):
        *_, fresh, f = fields(code[base + e])

        @pl.when(fresh == 0)
        def _():
            dk[f] += dk[e]
            dv[f] += dv[e]

    def back_copies(e, act):
        _, _, owner_x, sl, fresh, _ = fields(code[base + e])
        away = (x - owner_x) & (X - 1)
        for k, buf in ((0, g0), (1, g1), (2, g2), (3, g3)):

            @pl.when((fresh == 1) & (away == k))
            def _(buf=buf):
                act(pltpu.make_async_copy(tiles.at[e], buf.at[sl], back_sem.at[e]))

    @pl.loop(0, ENTRIES)
    def _(e):
        parts = [dk[e].reshape(4, 1, QUARTER, WIDTH), dv[e].reshape(4, 1, QUARTER, WIDTH)]
        tile = jnp.concatenate(parts, axis=1).astype(jnp.bfloat16)
        tiles[e] = tile.reshape(2 * BLOCK, WIDTH)
        back_copies(e, lambda copy: copy.start())

    @pl.loop(0, ENTRIES)
    def _(e):
        back_copies(e, lambda copy: copy.wait())

    @pl.loop(0, 2)
    def _(b):
        out_copy(b).wait()


def blocks(count):
    return jax.ShapeDtypeStruct((count, 2 * BLOCK, WIDTH), jnp.bfloat16)


def shift(array, axis, by):
    size = lax.axis_size(axis)
    return lax.ppermute(array, axis, [(i, (i + by) % size) for i in range(size)])


def params(mib):
    return pltpu.CompilerParams(vmem_limit_bytes=mib * MIB)


def exchange(array, axis):
    return lax.all_to_all(array, axis, split_axis=0, concat_axis=0, tiled=True)


def masks(*operands):
    return pl.pallas_call(
        mask_kernel,
        out_shape=jax.ShapeDtypeStruct((ENTRIES, BLOCK, BLOCK), jnp.float32),
        in_specs=[SMEM] * 3 + [VMEM],
        out_specs=VMEM,
        compiler_params=params(4),
        cost_estimate=pl.CostEstimate(flops=ENTRIES * BLOCK * BLOCK * 8, bytes_accessed=MIB, transcendentals=0),
    )(*operands)


def attend(slots, *operands):
    outs = jax.ShapeDtypeStruct((HEAD, 2, GROUP, QUARTER, WIDTH), jnp.bfloat16)
    return pl.pallas_call(
        attend_kernel,
        out_shape=[outs, blocks(ENTRIES)] + [blocks(slots)] * 3,
        in_specs=[SMEM] * 2 + [HBM] * 7,
        out_specs=[HBM] * 5,
        scratch_shapes=[
            pltpu.VMEM((HEAD, 2, GROUP, QUARTER, WIDTH), jnp.bfloat16),
            pltpu.VMEM((ENTRIES, 2 * BLOCK, WIDTH), jnp.bfloat16),
            pltpu.VMEM((ENTRIES, BLOCK, BLOCK), jnp.float32),
            pltpu.VMEM((HEAD, 2, GROUP, QUARTER, WIDTH), jnp.bfloat16),
            pltpu.VMEM((LISTED * BLOCK, WIDTH), jnp.bfloat16),
            pltpu.VMEM((LISTED * BLOCK, WIDTH), jnp.bfloat16),
            pltpu.VMEM((WIDTH, LISTED * BLOCK), jnp.bfloat16),
            pltpu.VMEM((WIDTH, LISTED * BLOCK), jnp.bfloat16),
            pltpu.VMEM((GROUP * BLOCK, WIDTH), jnp.bfloat16),
            pltpu.VMEM((GROUP * BLOCK, WIDTH), jnp.bfloat16),
            pltpu.VMEM((2, LISTED * BLOCK, 2 * BLOCK), jnp.float32),
            pltpu.VMEM((LISTED * BLOCK, GROUP * BLOCK), jnp.bfloat16),
            pltpu.VMEM((LISTED * BLOCK, GROUP * BLOCK), jnp.bfloat16),
            pltpu.VMEM((ENTRIES, BLOCK, WIDTH), jnp.float32),
            pltpu.VMEM((ENTRIES, BLOCK, WIDTH), jnp.float32),
            DMA((ENTRIES,)),
            DMA((2, 2)),
            DMA((2,)),
            DMA((ENTRIES,)),
        ],
        compiler_params=params(24),
        cost_estimate=pl.CostEstimate(
            flops=5 * 2 * 2048 * 1024 * 128, bytes_accessed=8 * MIB, transcendentals=2048 * 1024
        ),
    )(*operands)


def between(slots, place, tables, own, queries, output_gradient, sess):
    code, ent, kind = tables
    other = shift(own, "core", 1)
    sends = pl.pallas_call(
        gather_kernel,
        out_shape=[blocks(slots)] * 3,
        in_specs=[SMEM] * 2 + [HBM] * 2,
        out_specs=[HBM] * 3,
        scratch_shapes=[DMA((3 * ENTRIES,))],
        compiler_params=params(4),
    )(place, code, own, other)
    now, *sends = lax.optimization_barrier((place, *sends))
    fetched = [shift(sends[k - 1], "x", k) for k in (1, 2, 3)]
    mask = masks(now, ent, kind, sess)

    qd = jnp.stack([queries, output_gradient]).reshape(2, QUARTER, HEAD, GROUP, WIDTH)
    qd = exchange(qd.transpose(2, 0, 3, 1, 4), "head")

    out, g0, g1, g2, g3 = attend(
        slots, place, code, qd, own, other, *fetched, mask
    )

    returned = [shift(g, "x", -k) for k, g in ((1, g1), (2, g2), (3, g3))]
    out = exchange(out, "head")
    *returned, out = lax.optimization_barrier((*returned, out))
    own_sum, other_sum = pl.pallas_call(
        scatter_kernel,
        out_shape=[blocks(ENTRIES)] * 2,
        in_specs=[SMEM] * 2 + [HBM] * 4,
        out_specs=[VMEM] * 2,
        scratch_shapes=[
            pltpu.VMEM((4 * ENTRIES, 2 * BLOCK, WIDTH), jnp.bfloat16),
            pltpu.VMEM((2 * ENTRIES, 2 * BLOCK, WIDTH), jnp.float32),
            DMA((4 * ENTRIES,)),
        ],
        compiler_params=params(14),
    )(place, code, g0, *returned)
    return out, own_sum, other_sum


def per_device(queries, keys, values, output_gradient, kv_list, kv_type, session_id):
    where = [lax.axis_index(axis) for axis in ("z", "x", "core")]
    place = jnp.stack(where).astype(jnp.int32)

    code, most = coded(kv_list)
    tables = (code, kv_list.reshape(-1), kv_type.reshape(-1))
    sess = session_id.astype(jnp.float32).reshape(-1, BLOCK)

    kv = jnp.stack([keys, values]).transpose(2, 0, 1, 3)
    kv = jnp.broadcast_to(kv, (Z, HEAD, 2, QUARTER, WIDTH))
    own = exchange(kv.reshape(Z * HEAD, 2, QUARTER, WIDTH), ("z", "head"))
    own = own.reshape(ENTRIES, 2 * BLOCK, WIDTH)

    out, own_sum, other_sum = lax.switch(
        sum((most > few).astype(jnp.int32) for few in SLOTS[:-1]),
        [functools.partial(between, slots) for slots in SLOTS],
        place, tables, own, queries, output_gradient, sess,
    )

    from_core = shift(other_sum, "core", 1)
    column_sum = (own_sum.astype(jnp.float32) + from_core.astype(jnp.float32)).astype(jnp.bfloat16)
    parts = exchange(column_sum.reshape(Z * HEAD, 2, QUARTER, WIDTH), ("z", "head"))
    parts = parts.reshape(Z, HEAD, 2, QUARTER, WIDTH)
    total = jnp.sum(parts.astype(jnp.float32), axis=0).astype(jnp.bfloat16)
    total = total.transpose(1, 2, 0, 3)

    out = out.transpose(1, 3, 0, 2, 4).reshape(2, QUARTER, HEAD * GROUP, WIDTH)
    return out[0], out[1], total[0], total[1]


def solution(mesh):
    fine = Mesh(mesh.devices.reshape(Z, X, CORE, HEAD), ("z", "x", "core", "head"))
    split = P(("z", "x", "core", "head"), None, None)
    return jax.shard_map(
        per_device,
        mesh=fine,
        in_specs=(split,) * 4 + (P(),) * 3,
        out_specs=(split,) * 4,
        check_vma=False,
    )
```

```python
import functools

import jax
import jax.numpy as jnp
from jax import lax
from jax.experimental import pallas as pl
from jax.experimental.pallas import tpu as pltpu
from jax.sharding import Mesh, PartitionSpec as P

BLOCK = 128
WIDTH = 128
LISTED = 8
ENTRIES = 16
Z, X, CORE, HEAD = 8, 4, 2, 8
CTX = Z * X * CORE
GROUP = 8
QUARTER = 32
SLOTS = (7, 8, 9, 14)
LOG2E = 1.4426950408889634
MIB = 1 << 20

SMEM = pl.BlockSpec(memory_space=pltpu.SMEM)
VMEM = pl.BlockSpec(memory_space=pltpu.VMEM)
HBM = pl.BlockSpec(memory_space=pltpu.HBM)
DMA = pltpu.SemaphoreType.DMA


def fields(code):
    bits, parts = (4, 1, 2, 4, 1), []
    for bit in bits:
        parts.append(code & ((1 << bit) - 1))
        code = lax.shift_right_logical(code, bit)
    return (*parts, code)


def coded(kv_list):
    ent = kv_list.reshape(CTX, ENTRIES)
    order = jnp.arange(ENTRIES, dtype=jnp.int32)
    equal = ent[:, :, None] == ent[:, None, :]
    first = jnp.min(jnp.where(equal, order[None, None, :], ENTRIES), axis=2)
    fresh = first == order[None, :]
    column = lax.rem(ent // 4, X)
    before = (
        fresh[:, None, :]
        & (column[:, :, None] == column[:, None, :])
        & (order[None, None, :] < first[:, :, None])
    )
    slot = jnp.sum(before.astype(jnp.int32), axis=2)
    home = lax.rem(jnp.arange(CTX, dtype=jnp.int32) // CORE, X)
    most = jnp.max(jnp.where(column == home[:, None], 0, slot + 1))
    row = ent // 16 * 2 + lax.rem(ent, 2)
    core = lax.rem(ent // 2, CORE)
    code = slot + 16 * (fresh.astype(jnp.int32) + 2 * first)
    code = row + 16 * (core + CORE * (column + X * code))
    return code.reshape(-1), most


def neighbour_entries(place, code, k, what):
    z, x, core = place[0], place[1], place[2]
    base = ((z * X + ((x + k) & (X - 1))) * CORE + core) * ENTRIES

    @pl.loop(0, ENTRIES)
    def _(e):
        row, owner_core, owner_x, sl, fresh, _ = fields(code[base + e])

        @pl.when((fresh == 1) & (owner_x == x))
        def _():
            what(e, row, owner_core == core, sl)


def gather_kernel(place, code, own, oth, s1, s2, s3, sem):
    def all_copies(act):
        for k, out in ((1, s1), (2, s2), (3, s3)):

            def one(e, row, same_core, sl, k=k, out=out):
                for source, chosen in ((own, same_core), (oth, jnp.logical_not(same_core))):

                    @pl.when(chosen)
                    def _(source=source):
                        done = sem.at[(k - 1) * ENTRIES + e]
                        act(pltpu.make_async_copy(source.at[row], out.at[sl], done))

            neighbour_entries(place, code, k, one)

    all_copies(lambda copy: copy.start())
    all_copies(lambda copy: copy.wait())


def scatter_kernel(place, code, g0, g1, g2, g3, own_out, oth_out, acc):
    acc[...] = jnp.zeros_like(acc)
    for k, buf in ((0, g0), (1, g1), (2, g2), (3, g3)):

        def add(e, row, same_core, sl, buf=buf):
            to = row + jnp.where(same_core, 0, ENTRIES)
            acc[to] += buf[sl].astype(jnp.float32)

        neighbour_entries(place, code, k, add)

    own_out[...] = acc[:ENTRIES].astype(jnp.bfloat16)
    oth_out[...] = acc[ENTRIES:].astype(jnp.bfloat16)


def mask_kernel(place, ent, kind, sess, mask):
    me = (place[0] * X + place[1]) * CORE + place[2]
    key_iota = lax.broadcasted_iota(jnp.int32, (BLOCK, BLOCK), 0)
    query_iota = lax.broadcasted_iota(jnp.int32, (BLOCK, BLOCK), 1)

    @pl.loop(0, ENTRIES)
    def _(e):
        index = me * 2 + e // LISTED
        block, t = ent[me * ENTRIES + e], kind[me * ENTRIES + e]
        sess_q = sess[pl.ds(index, 1), :]
        sess_k = jnp.broadcast_to(sess[pl.ds(block, 1), :], (BLOCK, BLOCK)).T
        needs = jnp.where((t == 0) | (t == 2), 1.0, 0.0)
        shift = jnp.where(t == 0, (block - index) * BLOCK, jnp.where(t == 3, 0, -(1 << 20)))
        seen = ((sess_k - sess_q) * needs == 0.0) & (key_iota + shift <= query_iota)
        mask[e] = jnp.where(seen, jnp.inf, -jnp.inf)


def attend_kernel(
    place, code, qd_in, own, oth, r1, r2, r3, mask_in,
    out, g0, g1, g2, g3,
    qd, tiles, mask, kc, vc, kt, vt, qs, dos, s_scr, p_scr, d_scr, dk, dv,
    tile_sem, part_sem,
):
    z, x, core = place[0], place[1], place[2]
    base = ((z * X + x) * CORE + core) * ENTRIES
    scale = WIDTH**-0.5
    rows = 2 * BLOCK
    contract_last = (((1,), (1,)), ((), ()))

    def query_copy(b):
        half = pl.ds(b * 4, 4)
        return pltpu.make_async_copy(qd_in.at[half], qd.at[half], part_sem.at[0, b])

    def mask_copy(b):
        half = pl.ds(b * LISTED, LISTED)
        return pltpu.make_async_copy(mask_in.at[half], mask.at[half], part_sem.at[1, b])

    @pl.loop(0, 2)
    def _(b):
        query_copy(b).start()
        mask_copy(b).start()

        @pl.loop(0, LISTED)
        def _(l):
            e = b * LISTED + l
            row, owner_core, owner_x, sl, _, _ = fields(code[base + e])
            away = (x - owner_x) & (X - 1)
            here = (away == 0) & (owner_core == core)
            beside = (away == 0) & (owner_core != core)
            sources = ((own, row, here), (oth, row, beside), (r1, sl, away == 1))
            sources += ((r2, sl, away == 2), (r3, sl, away == 3))
            for source, at, chosen in sources:

                @pl.when(chosen)
                def _(source=source, at=at):
                    pltpu.make_async_copy(source.at[at], tiles.at[e], tile_sem.at[e]).start()

    @pl.loop(0, 2)
    def _(b):
        query_copy(b).wait()
        mask_copy(b).wait()

        @pl.loop(0, LISTED)
        def _(l):
            e = b * LISTED + l
            pltpu.make_async_copy(own.at[0], tiles.at[e], tile_sem.at[e]).wait()

        for l in range(LISTED):
            at = slice(l * BLOCK, (l + 1) * BLOCK)
            tile = tiles[b * LISTED + l].reshape(4, 2, QUARTER, WIDTH)
            kc[at, :] = tile[:, 0].reshape(BLOCK, WIDTH)
            vc[at, :] = tile[:, 1].reshape(BLOCK, WIDTH)

        for l in range(LISTED):
            at = slice(l * BLOCK, (l + 1) * BLOCK)
            kt[:, at] = kc[at, :].astype(jnp.float32).T.astype(jnp.bfloat16)
            vt[:, at] = vc[at, :].astype(jnp.float32).T.astype(jnp.bfloat16)

        quarters = pl.ds(b * 4, 4)
        for g in range(GROUP):
            at = slice(g * BLOCK, (g + 1) * BLOCK)
            qs[at, :] = qd[quarters, 0, g].reshape(BLOCK, WIDTH)
            dos[at, :] = qd[quarters, 1, g].reshape(BLOCK, WIDTH)

        def score(pair):
            q = qs[pair * rows : (pair + 1) * rows, :]
            top = jnp.full((8, rows), -jnp.inf, jnp.float32)
            for l in range(LISTED):
                at = slice(l * BLOCK, (l + 1) * BLOCK)
                s = lax.dot_general(
                    kc[at, :], q, contract_last, preferred_element_type=jnp.float32
                )
                m = mask[b * LISTED + l]
                s = jnp.minimum(s, jnp.concatenate([m, m], axis=1))
                s_scr[pair % 2, at, :] = s
                top = jnp.maximum(top, jnp.max(s.reshape(BLOCK // 8, 8, rows), axis=0))
            return jnp.max(top, axis=0, keepdims=True)

        top = score(0)
        for pair in range(GROUP // 2):
            cols = slice(pair * rows, (pair + 1) * rows)
            now = pair % 2
            total = jnp.zeros((8, rows), jnp.float32)
            for l in range(LISTED):
                at = slice(l * BLOCK, (l + 1) * BLOCK)
                w = jnp.exp2((s_scr[now, at, :] - top) * (scale * LOG2E))
                s_scr[now, at, :] = w
                total = total + jnp.sum(w.reshape(BLOCK // 8, 8, rows), axis=0)
            inverse = 1.0 / jnp.sum(total, axis=0, keepdims=True)
            if pair < GROUP // 2 - 1:
                top = score(pair + 1)
            for l in range(LISTED):
                at = slice(l * BLOCK, (l + 1) * BLOCK)
                p_scr[at, cols] = (s_scr[now, at, :] * inverse).astype(jnp.bfloat16)
            o_t = jnp.dot(vt[...], p_scr[:, cols], preferred_element_type=jnp.float32)
            do = dos[cols, :]
            do_t = do.astype(jnp.float32).T
            o_round = o_t.astype(jnp.bfloat16).astype(jnp.float32)
            row_dot = jnp.sum(o_round * do_t, axis=0, keepdims=True)
            scaled = inverse * scale
            for l in range(LISTED):
                at = slice(l * BLOCK, (l + 1) * BLOCK)
                dp = lax.dot_general(
                    vc[at, :], do, contract_last, preferred_element_type=jnp.float32
                )
                ds = ((s_scr[now, at, :] * scaled) * (dp - row_dot)).astype(jnp.bfloat16)
                d_scr[at, cols] = ds
            dq_t = jnp.dot(kt[...], d_scr[:, cols], preferred_element_type=jnp.float32)
            o = o_t.T.astype(jnp.bfloat16)
            dq = dq_t.T.astype(jnp.bfloat16)
            for i in range(2):
                at = slice(i * BLOCK, (i + 1) * BLOCK)
                out[quarters, 0, 2 * pair + i] = o[at].reshape(4, QUARTER, WIDTH)
                out[quarters, 1, 2 * pair + i] = dq[at].reshape(4, QUARTER, WIDTH)

        here = pl.ds(b * LISTED, LISTED)
        dk[here] = jnp.dot(d_scr[...], qs[...], preferred_element_type=jnp.float32).reshape(LISTED, BLOCK, WIDTH)
        dv[here] = jnp.dot(p_scr[...], dos[...], preferred_element_type=jnp.float32).reshape(LISTED, BLOCK, WIDTH)


    @pl.loop(LISTED, ENTRIES)
    def _(e):
        *_, fresh, f = fields(code[base + e])

        @pl.when(fresh == 0)
        def _():
            dk[f] += dk[e]
            dv[f] += dv[e]

    @pl.loop(0, ENTRIES)
    def _(e):
        _, _, owner_x, sl, fresh, _ = fields(code[base + e])
        away = (x - owner_x) & (X - 1)
        for k, buf in ((0, g0), (1, g1), (2, g2), (3, g3)):

            @pl.when((fresh == 1) & (away == k))
            def _(buf=buf):
                parts = [dk[e].reshape(4, 1, QUARTER, WIDTH), dv[e].reshape(4, 1, QUARTER, WIDTH)]
                tile = jnp.concatenate(parts, axis=1).astype(jnp.bfloat16)
                buf[sl] = tile.reshape(2 * BLOCK, WIDTH)


def blocks(count):
    return jax.ShapeDtypeStruct((count, 2 * BLOCK, WIDTH), jnp.bfloat16)


def shift(array, axis, by):
    size = lax.axis_size(axis)
    return lax.ppermute(array, axis, [(i, (i + by) % size) for i in range(size)])


def params(mib):
    return pltpu.CompilerParams(vmem_limit_bytes=mib * MIB)


def exchange(array, axis):
    return lax.all_to_all(array, axis, split_axis=0, concat_axis=0, tiled=True)


def masks(*operands):
    return pl.pallas_call(
        mask_kernel,
        out_shape=jax.ShapeDtypeStruct((ENTRIES, BLOCK, BLOCK), jnp.float32),
        in_specs=[SMEM] * 3 + [VMEM],
        out_specs=VMEM,
        compiler_params=params(4),
        cost_estimate=pl.CostEstimate(flops=ENTRIES * BLOCK * BLOCK * 8, bytes_accessed=MIB, transcendentals=0),
    )(*operands)


def attend(slots, *operands):
    outs = jax.ShapeDtypeStruct((HEAD, 2, GROUP, QUARTER, WIDTH), jnp.bfloat16)
    return pl.pallas_call(
        attend_kernel,
        out_shape=[outs, blocks(ENTRIES)] + [blocks(slots)] * 3,
        in_specs=[SMEM] * 2 + [HBM] * 7,
        out_specs=[VMEM] * 5,
        scratch_shapes=[
            pltpu.VMEM((HEAD, 2, GROUP, QUARTER, WIDTH), jnp.bfloat16),
            pltpu.VMEM((ENTRIES, 2 * BLOCK, WIDTH), jnp.bfloat16),
            pltpu.VMEM((ENTRIES, BLOCK, BLOCK), jnp.float32),
            pltpu.VMEM((LISTED * BLOCK, WIDTH), jnp.bfloat16),
            pltpu.VMEM((LISTED * BLOCK, WIDTH), jnp.bfloat16),
            pltpu.VMEM((WIDTH, LISTED * BLOCK), jnp.bfloat16),
            pltpu.VMEM((WIDTH, LISTED * BLOCK), jnp.bfloat16),
            pltpu.VMEM((GROUP * BLOCK, WIDTH), jnp.bfloat16),
            pltpu.VMEM((GROUP * BLOCK, WIDTH), jnp.bfloat16),
            pltpu.VMEM((2, LISTED * BLOCK, 2 * BLOCK), jnp.float32),
            pltpu.VMEM((LISTED * BLOCK, GROUP * BLOCK), jnp.bfloat16),
            pltpu.VMEM((LISTED * BLOCK, GROUP * BLOCK), jnp.bfloat16),
            pltpu.VMEM((ENTRIES, BLOCK, WIDTH), jnp.float32),
            pltpu.VMEM((ENTRIES, BLOCK, WIDTH), jnp.float32),
            DMA((ENTRIES,)),
            DMA((2, 2)),
        ],
        compiler_params=params(24),
        cost_estimate=pl.CostEstimate(
            flops=5 * 2 * 2048 * 1024 * 128, bytes_accessed=8 * MIB, transcendentals=2048 * 1024
        ),
    )(*operands)


def between(slots, place, tables, own, queries, output_gradient, sess):
    code, ent, kind = tables
    other = shift(own, "core", 1)
    sends = pl.pallas_call(
        gather_kernel,
        out_shape=[blocks(slots)] * 3,
        in_specs=[SMEM] * 2 + [HBM] * 2,
        out_specs=[HBM] * 3,
        scratch_shapes=[DMA((3 * ENTRIES,))],
        compiler_params=params(4),
    )(place, code, own, other)
    now, *sends = lax.optimization_barrier((place, *sends))
    fetched = [shift(sends[k - 1], "x", k) for k in (1, 2, 3)]
    mask = masks(now, ent, kind, sess)

    qd = jnp.stack([queries, output_gradient]).reshape(2, QUARTER, HEAD, GROUP, WIDTH)
    qd = exchange(qd.transpose(2, 0, 3, 1, 4), "head")

    out, g0, g1, g2, g3 = attend(
        slots, place, code, qd, own, other, *fetched, mask
    )

    returned = [shift(g, "x", -k) for k, g in ((1, g1), (2, g2), (3, g3))]
    out = exchange(out, "head")
    *returned, out = lax.optimization_barrier((*returned, out))
    own_sum, other_sum = pl.pallas_call(
        scatter_kernel,
        out_shape=[blocks(ENTRIES)] * 2,
        in_specs=[SMEM] * 2 + [VMEM] * 4,
        out_specs=[VMEM] * 2,
        scratch_shapes=[pltpu.VMEM((2 * ENTRIES, 2 * BLOCK, WIDTH), jnp.float32)],
        compiler_params=params(14),
    )(place, code, g0, *returned)
    from_core = shift(other_sum, "core", 1)
    column_sum = (own_sum.astype(jnp.float32) + from_core.astype(jnp.float32)).astype(jnp.bfloat16)
    parts = exchange(column_sum.reshape(Z * HEAD, 2, QUARTER, WIDTH), ("z", "head"))
    parts = parts.reshape(Z, HEAD, 2, QUARTER, WIDTH)
    total = jnp.sum(parts.astype(jnp.float32), axis=0).astype(jnp.bfloat16)
    total = total.transpose(1, 2, 0, 3)

    out = out.transpose(1, 3, 0, 2, 4).reshape(2, QUARTER, HEAD * GROUP, WIDTH)
    return out[0], out[1], total[0], total[1]


def per_device(queries, keys, values, output_gradient, kv_list, kv_type, session_id):
    where = [lax.axis_index(axis) for axis in ("z", "x", "core")]
    place = jnp.stack(where).astype(jnp.int32)

    code, most = coded(kv_list)
    tables = (code, kv_list.reshape(-1), kv_type.reshape(-1))
    sess = session_id.astype(jnp.float32).reshape(-1, BLOCK)

    kv = jnp.stack([keys, values]).transpose(2, 0, 1, 3)
    kv = jnp.broadcast_to(kv, (Z, HEAD, 2, QUARTER, WIDTH))
    own = exchange(kv.reshape(Z * HEAD, 2, QUARTER, WIDTH), ("z", "head"))
    own = own.reshape(ENTRIES, 2 * BLOCK, WIDTH)

    return lax.switch(
        sum((most > few).astype(jnp.int32) for few in SLOTS[:-1]),
        [functools.partial(between, slots) for slots in SLOTS],
        place, tables, own, queries, output_gradient, sess,
    )


def solution(mesh):
    fine = Mesh(mesh.devices.reshape(Z, X, CORE, HEAD), ("z", "x", "core", "head"))
    split = P(("z", "x", "core", "head"), None, None)
    return jax.shard_map(
        per_device,
        mesh=fine,
        in_specs=(split,) * 4 + (P(),) * 3,
        out_specs=(split,) * 4,
        check_vma=False,
    )
```

```python
import functools

import jax
import jax.numpy as jnp
from jax import lax
from jax.experimental import pallas as pl
from jax.experimental.pallas import tpu as pltpu
from jax.sharding import Mesh, PartitionSpec as P

BLOCK = 128
WIDTH = 128
LISTED = 8
ENTRIES = 16
Z, X, CORE, HEAD = 8, 4, 2, 8
CTX = Z * X * CORE
GROUP = 8
QUARTER = 32
SLOTS = (7, 8, 9, 14)
LOG2E = 1.4426950408889634
MIB = 1 << 20

SMEM = pl.BlockSpec(memory_space=pltpu.SMEM)
VMEM = pl.BlockSpec(memory_space=pltpu.VMEM)
HBM = pl.BlockSpec(memory_space=pltpu.HBM)
DMA = pltpu.SemaphoreType.DMA


def fields(code):
    bits, parts = (4, 1, 2, 4, 1), []
    for bit in bits:
        parts.append(code & ((1 << bit) - 1))
        code = lax.shift_right_logical(code, bit)
    return (*parts, code)


def coded(kv_list):
    ent = kv_list.reshape(CTX, ENTRIES)
    order = jnp.arange(ENTRIES, dtype=jnp.int32)
    equal = ent[:, :, None] == ent[:, None, :]
    first = jnp.min(jnp.where(equal, order[None, None, :], ENTRIES), axis=2)
    fresh = first == order[None, :]
    column = lax.rem(ent // 4, X)
    before = (
        fresh[:, None, :]
        & (column[:, :, None] == column[:, None, :])
        & (order[None, None, :] < first[:, :, None])
    )
    slot = jnp.sum(before.astype(jnp.int32), axis=2)
    home = lax.rem(jnp.arange(CTX, dtype=jnp.int32) // CORE, X)
    most = jnp.max(jnp.where(column == home[:, None], 0, slot + 1))
    row = ent // 16 * 2 + lax.rem(ent, 2)
    core = lax.rem(ent // 2, CORE)
    code = slot + 16 * (fresh.astype(jnp.int32) + 2 * first)
    code = row + 16 * (core + CORE * (column + X * code))
    return code.reshape(-1), most


def neighbour_entries(place, code, k, what):
    z, x, core = place[0], place[1], place[2]
    base = ((z * X + ((x + k) & (X - 1))) * CORE + core) * ENTRIES

    @pl.loop(0, ENTRIES)
    def _(e):
        row, owner_core, owner_x, sl, fresh, _ = fields(code[base + e])

        @pl.when((fresh == 1) & (owner_x == x))
        def _():
            what(e, row, owner_core == core, sl)


def gather_kernel(place, code, own, oth, s1, s2, s3, sem):
    for k, out in ((1, s1), (2, s2), (3, s3)):

        def start(e, row, same_core, sl, k=k, out=out):
            for source, chosen in ((own, same_core), (oth, jnp.logical_not(same_core))):

                @pl.when(chosen)
                def _(source=source):
                    copy = pltpu.make_async_copy(source.at[row], out.at[sl], sem.at[k, sl])
                    copy.start()

        neighbour_entries(place, code, k, start)

    for k, out in ((1, s1), (2, s2), (3, s3)):
        z, x, core = place[0], place[1], place[2]
        base = ((z * X + ((x + k) & (X - 1))) * CORE + core) * ENTRIES

        def count(e, found, base=base):
            _, _, owner_x, _, fresh, _ = fields(code[base + e])
            return found + jnp.where((fresh == 1) & (owner_x == x), 1, 0)

        @pl.loop(0, lax.fori_loop(0, ENTRIES, count, 0))
        def _(sl, k=k, out=out):
            pltpu.make_async_copy(own.at[0], out.at[sl], sem.at[k, sl]).wait()


def scatter_kernel(place, code, g0, g1, g2, g3, own_out, oth_out, acc):
    acc[...] = jnp.zeros_like(acc)
    for k, buf in ((0, g0), (1, g1), (2, g2), (3, g3)):

        def add(e, row, same_core, sl, buf=buf):
            to = row + jnp.where(same_core, 0, ENTRIES)
            acc[to] += buf[sl].astype(jnp.float32)

        neighbour_entries(place, code, k, add)

    own_out[...] = acc[:ENTRIES].astype(jnp.bfloat16)
    oth_out[...] = acc[ENTRIES:].astype(jnp.bfloat16)


def mask_kernel(place, ent, kind, sess, mask):
    me = (place[0] * X + place[1]) * CORE + place[2]
    key_iota = lax.broadcasted_iota(jnp.int32, (BLOCK, BLOCK), 0)
    query_iota = lax.broadcasted_iota(jnp.int32, (BLOCK, BLOCK), 1)

    @pl.loop(0, ENTRIES)
    def _(e):
        index = me * 2 + e // LISTED
        block, t = ent[me * ENTRIES + e], kind[me * ENTRIES + e]
        sess_q = sess[pl.ds(index, 1), :]
        sess_k = jnp.broadcast_to(sess[pl.ds(block, 1), :], (BLOCK, BLOCK)).T
        needs = jnp.where((t == 0) | (t == 2), 1.0, 0.0)
        shift = jnp.where(t == 0, (block - index) * BLOCK, jnp.where(t == 3, 0, -(1 << 20)))
        seen = ((sess_k - sess_q) * needs == 0.0) & (key_iota + shift <= query_iota)
        mask[e] = jnp.where(seen, jnp.inf, -jnp.inf)


def attend_kernel(
    place, code, qd_in, own, oth, r1, r2, r3, mask_in,
    out_to, g0, g1, g2, g3,
    qd, tiles, mask, out, kc, vc, kt, vt, qs, dos, s_scr, p_scr, d_scr, dk, dv,
    tile_sem, part_sem, out_sem, back_sem,
):
    z, x, core = place[0], place[1], place[2]
    base = ((z * X + x) * CORE + core) * ENTRIES
    scale = WIDTH**-0.5
    rows = 2 * BLOCK
    contract_last = (((1,), (1,)), ((), ()))

    def query_copy(b):
        half = pl.ds(b * 4, 4)
        return pltpu.make_async_copy(qd_in.at[half], qd.at[half], part_sem.at[0, b])

    def mask_copy(b):
        half = pl.ds(b * LISTED, LISTED)
        return pltpu.make_async_copy(mask_in.at[half], mask.at[half], part_sem.at[1, b])

    def out_copy(b):
        half = pl.ds(b * 4, 4)
        return pltpu.make_async_copy(out.at[half], out_to.at[half], out_sem.at[b])

    @pl.loop(0, 2)
    def _(b):
        query_copy(b).start()
        mask_copy(b).start()

        @pl.loop(0, LISTED)
        def _(l):
            e = b * LISTED + l
            row, owner_core, owner_x, sl, _, _ = fields(code[base + e])
            away = (x - owner_x) & (X - 1)
            here = (away == 0) & (owner_core == core)
            beside = (away == 0) & (owner_core != core)
            sources = ((own, row, here), (oth, row, beside), (r1, sl, away == 1))
            sources += ((r2, sl, away == 2), (r3, sl, away == 3))
            for source, at, chosen in sources:

                @pl.when(chosen)
                def _(source=source, at=at):
                    pltpu.make_async_copy(source.at[at], tiles.at[e], tile_sem.at[e]).start()

    @pl.loop(0, 2)
    def _(b):
        query_copy(b).wait()
        mask_copy(b).wait()

        @pl.loop(0, LISTED)
        def _(l):
            e = b * LISTED + l
            pltpu.make_async_copy(own.at[0], tiles.at[e], tile_sem.at[e]).wait()

        for l in range(LISTED):
            at = slice(l * BLOCK, (l + 1) * BLOCK)
            tile = tiles[b * LISTED + l].reshape(4, 2, QUARTER, WIDTH)
            kc[at, :] = tile[:, 0].reshape(BLOCK, WIDTH)
            vc[at, :] = tile[:, 1].reshape(BLOCK, WIDTH)

        for l in range(LISTED):
            at = slice(l * BLOCK, (l + 1) * BLOCK)
            kt[:, at] = kc[at, :].astype(jnp.float32).T.astype(jnp.bfloat16)
            vt[:, at] = vc[at, :].astype(jnp.float32).T.astype(jnp.bfloat16)

        quarters = pl.ds(b * 4, 4)
        for g in range(GROUP):
            at = slice(g * BLOCK, (g + 1) * BLOCK)
            qs[at, :] = qd[quarters, 0, g].reshape(BLOCK, WIDTH)
            dos[at, :] = qd[quarters, 1, g].reshape(BLOCK, WIDTH)

        def score(pair):
            q = qs[pair * rows : (pair + 1) * rows, :]
            top = jnp.full((8, rows), -jnp.inf, jnp.float32)
            for l in range(LISTED):
                at = slice(l * BLOCK, (l + 1) * BLOCK)
                s = lax.dot_general(
                    kc[at, :], q, contract_last, preferred_element_type=jnp.float32
                )
                m = mask[b * LISTED + l]
                s = jnp.minimum(s, jnp.concatenate([m, m], axis=1))
                s_scr[pair % 2, at, :] = s
                top = jnp.maximum(top, jnp.max(s.reshape(BLOCK // 8, 8, rows), axis=0))
            return jnp.max(top, axis=0, keepdims=True)

        top = score(0)
        for pair in range(GROUP // 2):
            cols = slice(pair * rows, (pair + 1) * rows)
            now = pair % 2
            total = jnp.zeros((8, rows), jnp.float32)
            for l in range(LISTED):
                at = slice(l * BLOCK, (l + 1) * BLOCK)
                w = jnp.exp2((s_scr[now, at, :] - top) * (scale * LOG2E))
                s_scr[now, at, :] = w
                total = total + jnp.sum(w.reshape(BLOCK // 8, 8, rows), axis=0)
            inverse = 1.0 / jnp.sum(total, axis=0, keepdims=True)
            if pair < GROUP // 2 - 1:
                top = score(pair + 1)
            for l in range(LISTED):
                at = slice(l * BLOCK, (l + 1) * BLOCK)
                p_scr[at, cols] = (s_scr[now, at, :] * inverse).astype(jnp.bfloat16)
            o_t = jnp.dot(vt[...], p_scr[:, cols], preferred_element_type=jnp.float32)
            do = dos[cols, :]
            do_t = do.astype(jnp.float32).T
            o_round = o_t.astype(jnp.bfloat16).astype(jnp.float32)
            row_dot = jnp.sum(o_round * do_t, axis=0, keepdims=True)
            scaled = inverse * scale
            for l in range(LISTED):
                at = slice(l * BLOCK, (l + 1) * BLOCK)
                dp = lax.dot_general(
                    vc[at, :], do, contract_last, preferred_element_type=jnp.float32
                )
                ds = ((s_scr[now, at, :] * scaled) * (dp - row_dot)).astype(jnp.bfloat16)
                d_scr[at, cols] = ds
            dq_t = jnp.dot(kt[...], d_scr[:, cols], preferred_element_type=jnp.float32)
            o = o_t.T.astype(jnp.bfloat16)
            dq = dq_t.T.astype(jnp.bfloat16)
            for i in range(2):
                at = slice(i * BLOCK, (i + 1) * BLOCK)
                out[quarters, 0, 2 * pair + i] = o[at].reshape(4, QUARTER, WIDTH)
                out[quarters, 1, 2 * pair + i] = dq[at].reshape(4, QUARTER, WIDTH)

        here = pl.ds(b * LISTED, LISTED)
        dk[here] = jnp.dot(d_scr[...], qs[...], preferred_element_type=jnp.float32).reshape(LISTED, BLOCK, WIDTH)
        dv[here] = jnp.dot(p_scr[...], dos[...], preferred_element_type=jnp.float32).reshape(LISTED, BLOCK, WIDTH)

        out_copy(b).start()

    @pl.loop(LISTED, ENTRIES)
    def _(e):
        *_, fresh, f = fields(code[base + e])

        @pl.when(fresh == 0)
        def _():
            dk[f] += dk[e]
            dv[f] += dv[e]

    def back_copies(e, act):
        _, _, owner_x, sl, fresh, _ = fields(code[base + e])
        away = (x - owner_x) & (X - 1)
        for k, buf in ((0, g0), (1, g1), (2, g2), (3, g3)):

            @pl.when((fresh == 1) & (away == k))
            def _(buf=buf):
                act(pltpu.make_async_copy(tiles.at[e], buf.at[sl], back_sem.at[e]))

    @pl.loop(0, ENTRIES)
    def _(e):
        parts = [dk[e].reshape(4, 1, QUARTER, WIDTH), dv[e].reshape(4, 1, QUARTER, WIDTH)]
        tile = jnp.concatenate(parts, axis=1).astype(jnp.bfloat16)
        tiles[e] = tile.reshape(2 * BLOCK, WIDTH)
        back_copies(e, lambda copy: copy.start())

    @pl.loop(0, ENTRIES)
    def _(e):
        back_copies(e, lambda copy: copy.wait())

    @pl.loop(0, 2)
    def _(b):
        out_copy(b).wait()


def blocks(count):
    return jax.ShapeDtypeStruct((count, 2 * BLOCK, WIDTH), jnp.bfloat16)


def shift(array, axis, by):
    size = lax.axis_size(axis)
    return lax.ppermute(array, axis, [(i, (i + by) % size) for i in range(size)])


def params(mib):
    return pltpu.CompilerParams(vmem_limit_bytes=mib * MIB)


def exchange(array, axis):
    return lax.all_to_all(array, axis, split_axis=0, concat_axis=0, tiled=True)


def masks(*operands):
    return pl.pallas_call(
        mask_kernel,
        out_shape=jax.ShapeDtypeStruct((ENTRIES, BLOCK, BLOCK), jnp.float32),
        in_specs=[SMEM] * 3 + [VMEM],
        out_specs=VMEM,
        compiler_params=params(4),
        cost_estimate=pl.CostEstimate(flops=ENTRIES * BLOCK * BLOCK * 8, bytes_accessed=MIB, transcendentals=0),
    )(*operands)


def attend(slots, *operands):
    outs = jax.ShapeDtypeStruct((HEAD, 2, GROUP, QUARTER, WIDTH), jnp.bfloat16)
    return pl.pallas_call(
        attend_kernel,
        out_shape=[outs, blocks(ENTRIES)] + [blocks(slots)] * 3,
        in_specs=[SMEM] * 2 + [HBM] * 7,
        out_specs=[HBM] * 5,
        scratch_shapes=[
            pltpu.VMEM((HEAD, 2, GROUP, QUARTER, WIDTH), jnp.bfloat16),
            pltpu.VMEM((ENTRIES, 2 * BLOCK, WIDTH), jnp.bfloat16),
            pltpu.VMEM((ENTRIES, BLOCK, BLOCK), jnp.float32),
            pltpu.VMEM((HEAD, 2, GROUP, QUARTER, WIDTH), jnp.bfloat16),
            pltpu.VMEM((LISTED * BLOCK, WIDTH), jnp.bfloat16),
            pltpu.VMEM((LISTED * BLOCK, WIDTH), jnp.bfloat16),
            pltpu.VMEM((WIDTH, LISTED * BLOCK), jnp.bfloat16),
            pltpu.VMEM((WIDTH, LISTED * BLOCK), jnp.bfloat16),
            pltpu.VMEM((GROUP * BLOCK, WIDTH), jnp.bfloat16),
            pltpu.VMEM((GROUP * BLOCK, WIDTH), jnp.bfloat16),
            pltpu.VMEM((2, LISTED * BLOCK, 2 * BLOCK), jnp.float32),
            pltpu.VMEM((LISTED * BLOCK, GROUP * BLOCK), jnp.bfloat16),
            pltpu.VMEM((LISTED * BLOCK, GROUP * BLOCK), jnp.bfloat16),
            pltpu.VMEM((ENTRIES, BLOCK, WIDTH), jnp.float32),
            pltpu.VMEM((ENTRIES, BLOCK, WIDTH), jnp.float32),
            DMA((ENTRIES,)),
            DMA((2, 2)),
            DMA((2,)),
            DMA((ENTRIES,)),
        ],
        compiler_params=params(60),
        cost_estimate=pl.CostEstimate(
            flops=5 * 2 * 2048 * 1024 * 128, bytes_accessed=8 * MIB, transcendentals=2048 * 1024
        ),
    )(*operands)


def between(slots, place, tables, own, queries, output_gradient, sess):
    code, ent, kind = tables
    other = shift(own, "core", 1)
    sends = pl.pallas_call(
        gather_kernel,
        out_shape=[blocks(slots)] * 3,
        in_specs=[SMEM] * 2 + [HBM] * 2,
        out_specs=[HBM] * 3,
        scratch_shapes=[DMA((X, ENTRIES))],
        compiler_params=params(4),
    )(place, code, own, other)
    now, *sends = lax.optimization_barrier((place, *sends))
    fetched = [shift(sends[k - 1], "x", k) for k in (1, 2, 3)]
    mask = masks(now, ent, kind, sess)

    qd = jnp.stack([queries, output_gradient]).reshape(2, QUARTER, HEAD, GROUP, WIDTH)
    qd = exchange(qd.transpose(2, 0, 3, 1, 4), "head")

    out, g0, g1, g2, g3 = attend(
        slots, place, code, qd, own, other, *fetched, mask
    )

    returned = [shift(g, "x", -k) for k, g in ((1, g1), (2, g2), (3, g3))]
    out = exchange(out, "head")
    *returned, out = lax.optimization_barrier((*returned, out))
    own_sum, other_sum = pl.pallas_call(
        scatter_kernel,
        out_shape=[blocks(ENTRIES)] * 2,
        in_specs=[SMEM] * 2 + [VMEM] * 4,
        out_specs=[VMEM] * 2,
        scratch_shapes=[pltpu.VMEM((2 * ENTRIES, 2 * BLOCK, WIDTH), jnp.float32)],
        compiler_params=params(14),
    )(place, code, g0, *returned)
    from_core = shift(other_sum, "core", 1)
    column_sum = (own_sum.astype(jnp.float32) + from_core.astype(jnp.float32)).astype(jnp.bfloat16)
    return out, column_sum


def per_device(queries, keys, values, output_gradient, kv_list, kv_type, session_id):
    where = [lax.axis_index(axis) for axis in ("z", "x", "core")]
    place = jnp.stack(where).astype(jnp.int32)

    code, most = coded(kv_list)
    tables = (code, kv_list.reshape(-1), kv_type.reshape(-1))
    sess = session_id.astype(jnp.float32).reshape(-1, BLOCK)

    kv = jnp.stack([keys, values]).transpose(2, 0, 1, 3)
    kv = jnp.broadcast_to(kv, (Z, HEAD, 2, QUARTER, WIDTH))
    own = exchange(kv.reshape(Z * HEAD, 2, QUARTER, WIDTH), ("z", "head"))
    own = own.reshape(ENTRIES, 2 * BLOCK, WIDTH)

    out, column_sum = lax.switch(
        sum((most > few).astype(jnp.int32) for few in SLOTS[:-1]),
        [functools.partial(between, slots) for slots in SLOTS],
        place, tables, own, queries, output_gradient, sess,
    )

    parts = exchange(column_sum.reshape(Z * HEAD, 2, QUARTER, WIDTH), ("z", "head"))
    parts = parts.reshape(Z, HEAD, 2, QUARTER, WIDTH)
    total = jnp.sum(parts.astype(jnp.float32), axis=0).astype(jnp.bfloat16)
    total = total.transpose(1, 2, 0, 3)

    out = out.transpose(1, 3, 0, 2, 4).reshape(2, QUARTER, HEAD * GROUP, WIDTH)
    return out[0], out[1], total[0], total[1]


def solution(mesh):
    fine = Mesh(mesh.devices.reshape(Z, X, CORE, HEAD), ("z", "x", "core", "head"))
    split = P(("z", "x", "core", "head"), None, None)
    return jax.shard_map(
        per_device,
        mesh=fine,
        in_specs=(split,) * 4 + (P(),) * 3,
        out_specs=(split,) * 4,
        check_vma=False,
    )
```

```python
import functools

import jax
import jax.numpy as jnp
from jax import lax
from jax.experimental import pallas as pl
from jax.experimental.pallas import tpu as pltpu
from jax.sharding import Mesh, PartitionSpec as P

BLOCK = 128
WIDTH = 128
LISTED = 8
ENTRIES = 16
Z, X, CORE, HEAD = 8, 4, 2, 8
CTX = Z * X * CORE
GROUP = 8
QUARTER = 32
SLOTS = (7, 8, 9, 14)
LOG2E = 1.4426950408889634
MIB = 1 << 20

SMEM = pl.BlockSpec(memory_space=pltpu.SMEM)
VMEM = pl.BlockSpec(memory_space=pltpu.VMEM)
HBM = pl.BlockSpec(memory_space=pltpu.HBM)
DMA = pltpu.SemaphoreType.DMA


def fields(code):
    bits, parts = (4, 1, 2, 4, 1), []
    for bit in bits:
        parts.append(code & ((1 << bit) - 1))
        code = lax.shift_right_logical(code, bit)
    return (*parts, code)


def coded(kv_list):
    ent = kv_list.reshape(CTX, ENTRIES)
    order = jnp.arange(ENTRIES, dtype=jnp.int32)
    equal = ent[:, :, None] == ent[:, None, :]
    first = jnp.min(jnp.where(equal, order[None, None, :], ENTRIES), axis=2)
    fresh = first == order[None, :]
    column = lax.rem(ent // 4, X)
    before = (
        fresh[:, None, :]
        & (column[:, :, None] == column[:, None, :])
        & (order[None, None, :] < first[:, :, None])
    )
    slot = jnp.sum(before.astype(jnp.int32), axis=2)
    home = lax.rem(jnp.arange(CTX, dtype=jnp.int32) // CORE, X)
    most = jnp.max(jnp.where(column == home[:, None], 0, slot + 1))
    row = ent // 16 * 2 + lax.rem(ent, 2)
    core = lax.rem(ent // 2, CORE)
    code = slot + 16 * (fresh.astype(jnp.int32) + 2 * first)
    code = row + 16 * (core + CORE * (column + X * code))
    return code.reshape(-1), most


def neighbour_entries(place, code, k, what):
    z, x, core = place[0], place[1], place[2]
    base = ((z * X + ((x + k) & (X - 1))) * CORE + core) * ENTRIES

    @pl.loop(0, ENTRIES)
    def _(e):
        row, owner_core, owner_x, sl, fresh, _ = fields(code[base + e])

        @pl.when((fresh == 1) & (owner_x == x))
        def _():
            what(e, row, owner_core == core, sl)


def gather_kernel(place, code, own, oth, s1, s2, s3, sem):
    for k, out in ((1, s1), (2, s2), (3, s3)):

        def start(e, row, same_core, sl, k=k, out=out):
            for source, chosen in ((own, same_core), (oth, jnp.logical_not(same_core))):

                @pl.when(chosen)
                def _(source=source):
                    copy = pltpu.make_async_copy(source.at[row], out.at[sl], sem.at[k, sl])
                    copy.start()

        neighbour_entries(place, code, k, start)

    for k, out in ((1, s1), (2, s2), (3, s3)):
        z, x, core = place[0], place[1], place[2]
        base = ((z * X + ((x + k) & (X - 1))) * CORE + core) * ENTRIES

        def count(e, found, base=base):
            _, _, owner_x, _, fresh, _ = fields(code[base + e])
            return found + jnp.where((fresh == 1) & (owner_x == x), 1, 0)

        @pl.loop(0, lax.fori_loop(0, ENTRIES, count, 0))
        def _(sl, k=k, out=out):
            pltpu.make_async_copy(own.at[0], out.at[sl], sem.at[k, sl]).wait()


def scatter_kernel(place, code, g0, g1, g2, g3, own_out, oth_out, acc):
    acc[...] = jnp.zeros_like(acc)
    for k, buf in ((0, g0), (1, g1), (2, g2), (3, g3)):

        def add(e, row, same_core, sl, buf=buf):
            to = row + jnp.where(same_core, 0, ENTRIES)
            acc[to] += buf[sl].astype(jnp.float32)

        neighbour_entries(place, code, k, add)

    own_out[...] = acc[:ENTRIES].astype(jnp.bfloat16)
    oth_out[...] = acc[ENTRIES:].astype(jnp.bfloat16)


def mask_kernel(place, ent, kind, sess, mask):
    me = (place[0] * X + place[1]) * CORE + place[2]
    key_iota = lax.broadcasted_iota(jnp.int32, (BLOCK, BLOCK), 0)
    query_iota = lax.broadcasted_iota(jnp.int32, (BLOCK, BLOCK), 1)

    @pl.loop(0, ENTRIES)
    def _(e):
        index = me * 2 + e // LISTED
        block, t = ent[e % LISTED, index], kind[e % LISTED, index]
        sess_q = sess[pl.ds(index, 1), :]
        sess_k = jnp.broadcast_to(sess[pl.ds(block, 1), :], (BLOCK, BLOCK)).T
        needs = jnp.where((t == 0) | (t == 2), 1.0, 0.0)
        shift = jnp.where(t == 0, (block - index) * BLOCK, jnp.where(t == 3, 0, -(1 << 20)))
        seen = ((sess_k - sess_q) * needs == 0.0) & (key_iota + shift <= query_iota)
        mask[e] = jnp.where(seen, jnp.inf, -jnp.inf)


def attend_kernel(
    place, code, qd_in, own, oth, r1, r2, r3, mask_in,
    out_to, g0, g1, g2, g3,
    qd, tiles, mask, out, kc, vc, kt, vt, qs, dos, s_scr, p_scr, d_scr, dk, dv,
    tile_sem, part_sem, out_sem, back_sem,
):
    z, x, core = place[0], place[1], place[2]
    base = ((z * X + x) * CORE + core) * ENTRIES
    scale = WIDTH**-0.5
    rows = 2 * BLOCK
    contract_last = (((1,), (1,)), ((), ()))

    def query_copy(b):
        half = pl.ds(b * 4, 4)
        return pltpu.make_async_copy(qd_in.at[half], qd.at[half], part_sem.at[0, b])

    def mask_copy(b):
        half = pl.ds(b * LISTED, LISTED)
        return pltpu.make_async_copy(mask_in.at[half], mask.at[half], part_sem.at[1, b])

    def out_copy(b):
        half = pl.ds(b * 4, 4)
        return pltpu.make_async_copy(out.at[half], out_to.at[half], out_sem.at[b])

    @pl.loop(0, 2)
    def _(b):
        query_copy(b).start()
        mask_copy(b).start()

        @pl.loop(0, LISTED)
        def _(l):
            e = b * LISTED + l
            row, owner_core, owner_x, sl, _, _ = fields(code[base + e])
            away = (x - owner_x) & (X - 1)
            here = (away == 0) & (owner_core == core)
            beside = (away == 0) & (owner_core != core)
            sources = ((own, row, here), (oth, row, beside), (r1, sl, away == 1))
            sources += ((r2, sl, away == 2), (r3, sl, away == 3))
            for source, at, chosen in sources:

                @pl.when(chosen)
                def _(source=source, at=at):
                    pltpu.make_async_copy(source.at[at], tiles.at[e], tile_sem.at[e]).start()

    @pl.loop(0, 2)
    def _(b):
        query_copy(b).wait()
        mask_copy(b).wait()

        @pl.loop(0, LISTED)
        def _(l):
            e = b * LISTED + l
            pltpu.make_async_copy(own.at[0], tiles.at[e], tile_sem.at[e]).wait()

        for l in range(LISTED):
            at = slice(l * BLOCK, (l + 1) * BLOCK)
            tile = tiles[b * LISTED + l].reshape(4, 2, QUARTER, WIDTH)
            kc[at, :] = tile[:, 0].reshape(BLOCK, WIDTH)
            vc[at, :] = tile[:, 1].reshape(BLOCK, WIDTH)

        for l in range(LISTED):
            at = slice(l * BLOCK, (l + 1) * BLOCK)
            kt[:, at] = kc[at, :].astype(jnp.float32).T.astype(jnp.bfloat16)
            vt[:, at] = vc[at, :].astype(jnp.float32).T.astype(jnp.bfloat16)

        quarters = pl.ds(b * 4, 4)
        for g in range(GROUP):
            at = slice(g * BLOCK, (g + 1) * BLOCK)
            qs[at, :] = qd[quarters, 0, g].reshape(BLOCK, WIDTH)
            dos[at, :] = qd[quarters, 1, g].reshape(BLOCK, WIDTH)

        def score(pair):
            q = qs[pair * rows : (pair + 1) * rows, :]
            top = jnp.full((8, rows), -jnp.inf, jnp.float32)
            for l in range(LISTED):
                at = slice(l * BLOCK, (l + 1) * BLOCK)
                s = lax.dot_general(
                    kc[at, :], q, contract_last, preferred_element_type=jnp.float32
                )
                m = mask[b * LISTED + l]
                s = jnp.minimum(s, jnp.concatenate([m, m], axis=1))
                s_scr[pair % 2, at, :] = s
                top = jnp.maximum(top, jnp.max(s.reshape(BLOCK // 8, 8, rows), axis=0))
            return jnp.max(top, axis=0, keepdims=True)

        top = score(0)
        for pair in range(GROUP // 2):
            cols = slice(pair * rows, (pair + 1) * rows)
            now = pair % 2
            total = jnp.zeros((8, rows), jnp.float32)
            for l in range(LISTED):
                at = slice(l * BLOCK, (l + 1) * BLOCK)
                w = jnp.exp2((s_scr[now, at, :] - top) * (scale * LOG2E))
                s_scr[now, at, :] = w
                total = total + jnp.sum(w.reshape(BLOCK // 8, 8, rows), axis=0)
            inverse = 1.0 / jnp.sum(total, axis=0, keepdims=True)
            if pair < GROUP // 2 - 1:
                top = score(pair + 1)
            for l in range(LISTED):
                at = slice(l * BLOCK, (l + 1) * BLOCK)
                p_scr[at, cols] = (s_scr[now, at, :] * inverse).astype(jnp.bfloat16)
            o_t = jnp.dot(vt[...], p_scr[:, cols], preferred_element_type=jnp.float32)
            do = dos[cols, :]
            do_t = do.astype(jnp.float32).T
            o_round = o_t.astype(jnp.bfloat16).astype(jnp.float32)
            row_dot = jnp.sum(o_round * do_t, axis=0, keepdims=True)
            scaled = inverse * scale
            for l in range(LISTED):
                at = slice(l * BLOCK, (l + 1) * BLOCK)
                dp = lax.dot_general(
                    vc[at, :], do, contract_last, preferred_element_type=jnp.float32
                )
                ds = ((s_scr[now, at, :] * scaled) * (dp - row_dot)).astype(jnp.bfloat16)
                d_scr[at, cols] = ds
            dq_t = jnp.dot(kt[...], d_scr[:, cols], preferred_element_type=jnp.float32)
            o = o_t.T.astype(jnp.bfloat16)
            dq = dq_t.T.astype(jnp.bfloat16)
            for i in range(2):
                at = slice(i * BLOCK, (i + 1) * BLOCK)
                out[quarters, 0, 2 * pair + i] = o[at].reshape(4, QUARTER, WIDTH)
                out[quarters, 1, 2 * pair + i] = dq[at].reshape(4, QUARTER, WIDTH)

        here = pl.ds(b * LISTED, LISTED)
        dk[here] = jnp.dot(d_scr[...], qs[...], preferred_element_type=jnp.float32).reshape(LISTED, BLOCK, WIDTH)
        dv[here] = jnp.dot(p_scr[...], dos[...], preferred_element_type=jnp.float32).reshape(LISTED, BLOCK, WIDTH)

        out_copy(b).start()

    @pl.loop(LISTED, ENTRIES)
    def _(e):
        *_, fresh, f = fields(code[base + e])

        @pl.when(fresh == 0)
        def _():
            dk[f] += dk[e]
            dv[f] += dv[e]

    def back_copies(e, act):
        _, _, owner_x, sl, fresh, _ = fields(code[base + e])
        away = (x - owner_x) & (X - 1)
        for k, buf in ((0, g0), (1, g1), (2, g2), (3, g3)):

            @pl.when((fresh == 1) & (away == k))
            def _(buf=buf):
                act(pltpu.make_async_copy(tiles.at[e], buf.at[sl], back_sem.at[e]))

    @pl.loop(0, ENTRIES)
    def _(e):
        parts = [dk[e].reshape(4, 1, QUARTER, WIDTH), dv[e].reshape(4, 1, QUARTER, WIDTH)]
        tile = jnp.concatenate(parts, axis=1).astype(jnp.bfloat16)
        tiles[e] = tile.reshape(2 * BLOCK, WIDTH)
        back_copies(e, lambda copy: copy.start())

    @pl.loop(0, ENTRIES)
    def _(e):
        back_copies(e, lambda copy: copy.wait())

    @pl.loop(0, 2)
    def _(b):
        out_copy(b).wait()


def blocks(count):
    return jax.ShapeDtypeStruct((count, 2 * BLOCK, WIDTH), jnp.bfloat16)


def shift(array, axis, by):
    size = lax.axis_size(axis)
    return lax.ppermute(array, axis, [(i, (i + by) % size) for i in range(size)])


def params(mib):
    return pltpu.CompilerParams(vmem_limit_bytes=mib * MIB)


def exchange(array, axis):
    return lax.all_to_all(array, axis, split_axis=0, concat_axis=0, tiled=True)


def gather(slots, *operands):
    return pl.pallas_call(
        gather_kernel,
        out_shape=[blocks(slots)] * 3,
        in_specs=[SMEM] * 2 + [HBM] * 2,
        out_specs=[HBM] * 3,
        scratch_shapes=[DMA((X, ENTRIES))],
        compiler_params=params(4),
    )(*operands)


def scatter(*operands):
    return pl.pallas_call(
        scatter_kernel,
        out_shape=[blocks(ENTRIES)] * 2,
        in_specs=[SMEM] * 2 + [VMEM] * 4,
        out_specs=[VMEM] * 2,
        scratch_shapes=[pltpu.VMEM((2 * ENTRIES, 2 * BLOCK, WIDTH), jnp.float32)],
        compiler_params=params(14),
    )(*operands)


def add_kernel(left, right, total):
    total[...] = (left[...].astype(jnp.float32) + right[...].astype(jnp.float32)).astype(jnp.bfloat16)


def add(*operands):
    return pl.pallas_call(
        add_kernel,
        out_shape=blocks(ENTRIES),
        in_specs=[VMEM] * 2,
        out_specs=VMEM,
        compiler_params=params(8),
    )(*operands)


def masks(*operands):
    return pl.pallas_call(
        mask_kernel,
        out_shape=jax.ShapeDtypeStruct((ENTRIES, BLOCK, BLOCK), jnp.float32),
        in_specs=[SMEM] * 3 + [VMEM],
        out_specs=VMEM,
        compiler_params=params(4),
        cost_estimate=pl.CostEstimate(flops=ENTRIES * BLOCK * BLOCK * 8, bytes_accessed=MIB, transcendentals=0),
    )(*operands)


def attend(slots, *operands):
    outs = jax.ShapeDtypeStruct((HEAD, 2, GROUP, QUARTER, WIDTH), jnp.bfloat16)
    return pl.pallas_call(
        attend_kernel,
        out_shape=[outs, blocks(ENTRIES)] + [blocks(slots)] * 3,
        in_specs=[SMEM] * 2 + [HBM] * 7,
        out_specs=[HBM] * 5,
        scratch_shapes=[
            pltpu.VMEM((HEAD, 2, GROUP, QUARTER, WIDTH), jnp.bfloat16),
            pltpu.VMEM((ENTRIES, 2 * BLOCK, WIDTH), jnp.bfloat16),
            pltpu.VMEM((ENTRIES, BLOCK, BLOCK), jnp.float32),
            pltpu.VMEM((HEAD, 2, GROUP, QUARTER, WIDTH), jnp.bfloat16),
            pltpu.VMEM((LISTED * BLOCK, WIDTH), jnp.bfloat16),
            pltpu.VMEM((LISTED * BLOCK, WIDTH), jnp.bfloat16),
            pltpu.VMEM((WIDTH, LISTED * BLOCK), jnp.bfloat16),
            pltpu.VMEM((WIDTH, LISTED * BLOCK), jnp.bfloat16),
            pltpu.VMEM((GROUP * BLOCK, WIDTH), jnp.bfloat16),
            pltpu.VMEM((GROUP * BLOCK, WIDTH), jnp.bfloat16),
            pltpu.VMEM((2, LISTED * BLOCK, 2 * BLOCK), jnp.float32),
            pltpu.VMEM((LISTED * BLOCK, GROUP * BLOCK), jnp.bfloat16),
            pltpu.VMEM((LISTED * BLOCK, GROUP * BLOCK), jnp.bfloat16),
            pltpu.VMEM((ENTRIES, BLOCK, WIDTH), jnp.float32),
            pltpu.VMEM((ENTRIES, BLOCK, WIDTH), jnp.float32),
            DMA((ENTRIES,)),
            DMA((2, 2)),
            DMA((2,)),
            DMA((ENTRIES,)),
        ],
        compiler_params=params(60),
        cost_estimate=pl.CostEstimate(
            flops=5 * 2 * 2048 * 1024 * 128, bytes_accessed=8 * MIB, transcendentals=2048 * 1024
        ),
    )(*operands)


def between(slots, place, tables, own, queries, output_gradient, sess):
    code, ent, kind = tables
    other = shift(own, "core", 1)
    sends = gather(slots, place, code, own, other)
    now, *sends = lax.optimization_barrier((place, *sends))
    fetched = [shift(sends[k - 1], "x", k) for k in (1, 2, 3)]
    mask = masks(now, ent, kind, sess)

    qd = jnp.stack([queries, output_gradient]).reshape(2, QUARTER, HEAD, GROUP, WIDTH)
    qd = exchange(qd.transpose(2, 0, 3, 1, 4), "head")

    out, g0, g1, g2, g3 = attend(
        slots, place, code, qd, own, other, *fetched, mask
    )

    returned = [shift(g, "x", -k) for k, g in ((1, g1), (2, g2), (3, g3))]
    out = exchange(out, "head")
    *returned, out = lax.optimization_barrier((*returned, out))
    own_sum, other_sum = scatter(place, code, g0, *returned)
    from_core = shift(other_sum, "core", 1)
    column_sum = add(own_sum, from_core)
    return out, column_sum


def per_device(queries, keys, values, output_gradient, kv_list, kv_type, session_id):
    where = [lax.axis_index(axis) for axis in ("z", "x", "core")]
    place = jnp.stack(where).astype(jnp.int32)

    code, most = coded(kv_list)
    sess = session_id.astype(jnp.float32).reshape(-1, BLOCK)

    kv = jnp.stack([keys, values]).transpose(2, 0, 1, 3)
    kv = jnp.broadcast_to(kv, (Z, HEAD, 2, QUARTER, WIDTH))
    own = exchange(kv.reshape(Z * HEAD, 2, QUARTER, WIDTH), ("z", "head"))
    own = own.reshape(ENTRIES, 2 * BLOCK, WIDTH)

    own, code, most, sess = lax.optimization_barrier((own, code, most, sess))
    tables = (code, kv_list.T, kv_type.T)
    out, column_sum = lax.switch(
        sum((most > few).astype(jnp.int32) for few in SLOTS[:-1]),
        [functools.partial(between, slots) for slots in SLOTS],
        place, tables, own, queries, output_gradient, sess,
    )

    parts = exchange(column_sum.reshape(Z * HEAD, 2, QUARTER, WIDTH), ("z", "head"))
    parts = parts.reshape(Z, HEAD, 2, QUARTER, WIDTH)
    total = jnp.sum(parts.astype(jnp.float32), axis=0).astype(jnp.bfloat16)
    total = total.transpose(1, 2, 0, 3)

    out = out.transpose(1, 3, 0, 2, 4).reshape(2, QUARTER, HEAD * GROUP, WIDTH)
    return out[0], out[1], total[0], total[1]


def solution(mesh):
    fine = Mesh(mesh.devices.reshape(Z, X, CORE, HEAD), ("z", "x", "core", "head"))
    split = P(("z", "x", "core", "head"), None, None)
    return jax.shard_map(
        per_device,
        mesh=fine,
        in_specs=(split,) * 4 + (P(),) * 3,
        out_specs=(split,) * 4,
        check_vma=False,
    )
```

```python
import functools

import jax
import jax.numpy as jnp
from jax import lax
from jax.experimental import pallas as pl
from jax.experimental.pallas import tpu as pltpu
from jax.sharding import Mesh, PartitionSpec as P

BLOCK = 128
WIDTH = 128
LISTED = 8
ENTRIES = 16
Z, X, CORE, HEAD = 8, 4, 2, 8
CTX = Z * X * CORE
GROUP = 8
QUARTER = 32
SLOTS = (7, 8, 9, 14)
LOG2E = 1.4426950408889634
MIB = 1 << 20

SMEM = pl.BlockSpec(memory_space=pltpu.SMEM)
VMEM = pl.BlockSpec(memory_space=pltpu.VMEM)
HBM = pl.BlockSpec(memory_space=pltpu.HBM)
DMA = pltpu.SemaphoreType.DMA


def fields(code):
    bits, parts = (4, 1, 2, 4, 1), []
    for bit in bits:
        parts.append(code & ((1 << bit) - 1))
        code = lax.shift_right_logical(code, bit)
    return (*parts, code)


def coded(kv_list):
    ent = kv_list.reshape(CTX, ENTRIES)
    order = jnp.arange(ENTRIES, dtype=jnp.int32)
    equal = ent[:, :, None] == ent[:, None, :]
    first = jnp.min(jnp.where(equal, order[None, None, :], ENTRIES), axis=2)
    fresh = first == order[None, :]
    column = lax.rem(ent // 4, X)
    before = (
        fresh[:, None, :]
        & (column[:, :, None] == column[:, None, :])
        & (order[None, None, :] < first[:, :, None])
    )
    slot = jnp.sum(before.astype(jnp.int32), axis=2)
    home = lax.rem(jnp.arange(CTX, dtype=jnp.int32) // CORE, X)
    most = jnp.max(jnp.where(column == home[:, None], 0, slot + 1))
    row = ent // 16 * 2 + lax.rem(ent, 2)
    core = lax.rem(ent // 2, CORE)
    code = slot + 16 * (fresh.astype(jnp.int32) + 2 * first)
    code = row + 16 * (core + CORE * (column + X * code))
    return code.reshape(-1), most


def neighbour_entries(place, code, k, what):
    z, x, core = place[0], place[1], place[2]
    base = ((z * X + ((x + k) & (X - 1))) * CORE + core) * ENTRIES

    @pl.loop(0, ENTRIES)
    def _(e):
        row, owner_core, owner_x, sl, fresh, _ = fields(code[base + e])

        @pl.when((fresh == 1) & (owner_x == x))
        def _():
            what(e, row, owner_core == core, sl)


def gather_kernel(place, code, own, oth, s1, s2, s3, sem):
    for k, out in ((1, s1), (2, s2), (3, s3)):

        def start(e, row, same_core, sl, k=k, out=out):
            for source, chosen in ((own, same_core), (oth, jnp.logical_not(same_core))):

                @pl.when(chosen)
                def _(source=source):
                    copy = pltpu.make_async_copy(source.at[row], out.at[sl], sem.at[k, sl])
                    copy.start()

        neighbour_entries(place, code, k, start)

    for k, out in ((1, s1), (2, s2), (3, s3)):
        z, x, core = place[0], place[1], place[2]
        base = ((z * X + ((x + k) & (X - 1))) * CORE + core) * ENTRIES

        def count(e, found, base=base):
            _, _, owner_x, _, fresh, _ = fields(code[base + e])
            return found + jnp.where((fresh == 1) & (owner_x == x), 1, 0)

        @pl.loop(0, lax.fori_loop(0, ENTRIES, count, 0))
        def _(sl, k=k, out=out):
            pltpu.make_async_copy(own.at[0], out.at[sl], sem.at[k, sl]).wait()


def scatter_kernel(place, code, g0, g1, g2, g3, own_out, oth_out, acc):
    acc[...] = jnp.zeros_like(acc)
    for k, buf in ((0, g0), (1, g1), (2, g2), (3, g3)):

        def add(e, row, same_core, sl, buf=buf):
            to = row + jnp.where(same_core, 0, ENTRIES)
            acc[to] += buf[sl].astype(jnp.float32)

        neighbour_entries(place, code, k, add)

    own_out[...] = acc[:ENTRIES].astype(jnp.bfloat16)
    oth_out[...] = acc[ENTRIES:].astype(jnp.bfloat16)


def mask_kernel(place, ent, kind, sess, mask):
    me = (place[0] * X + place[1]) * CORE + place[2]
    key_iota = lax.broadcasted_iota(jnp.int32, (BLOCK, BLOCK), 0)
    query_iota = lax.broadcasted_iota(jnp.int32, (BLOCK, BLOCK), 1)

    @pl.loop(0, ENTRIES)
    def _(e):
        index = me * 2 + e // LISTED
        block, t = ent[e % LISTED, index], kind[e % LISTED, index]
        sess_q = sess[pl.ds(index, 1), :]
        sess_k = jnp.broadcast_to(sess[pl.ds(block, 1), :], (BLOCK, BLOCK)).T
        needs = jnp.where((t == 0) | (t == 2), 1.0, 0.0)
        shift = jnp.where(t == 0, (block - index) * BLOCK, jnp.where(t == 3, 0, -(1 << 20)))
        seen = ((sess_k - sess_q) * needs == 0.0) & (key_iota + shift <= query_iota)
        mask[e] = jnp.where(seen, jnp.inf, -jnp.inf)


def attend_kernel(
    place, code, qd_in, own, oth, r1, r2, r3, mask_in,
    out_to, g0, g1, g2, g3,
    qd, tiles, mask, out, kc, vc, kt, vt, qs, dos, s_scr, p_scr, d_scr, dk, dv,
    tile_sem, part_sem, out_sem, back_sem,
):
    z, x, core = place[0], place[1], place[2]
    base = ((z * X + x) * CORE + core) * ENTRIES
    scale = WIDTH**-0.5
    rows = 2 * BLOCK
    contract_last = (((1,), (1,)), ((), ()))

    def query_copy(b):
        half = pl.ds(b * 4, 4)
        return pltpu.make_async_copy(qd_in.at[half], qd.at[half], part_sem.at[0, b])

    def mask_copy(b):
        half = pl.ds(b * LISTED, LISTED)
        return pltpu.make_async_copy(mask_in.at[half], mask.at[half], part_sem.at[1, b])

    def out_copy(b):
        half = pl.ds(b * 4, 4)
        return pltpu.make_async_copy(out.at[half], out_to.at[half], out_sem.at[b])

    @pl.loop(0, 2)
    def _(b):
        query_copy(b).start()
        mask_copy(b).start()

        @pl.loop(0, LISTED)
        def _(l):
            e = b * LISTED + l
            row, owner_core, owner_x, sl, _, _ = fields(code[base + e])
            away = (x - owner_x) & (X - 1)
            here = (away == 0) & (owner_core == core)
            beside = (away == 0) & (owner_core != core)
            sources = ((own, row, here), (oth, row, beside), (r1, sl, away == 1))
            sources += ((r2, sl, away == 2), (r3, sl, away == 3))
            for source, at, chosen in sources:

                @pl.when(chosen)
                def _(source=source, at=at):
                    pltpu.make_async_copy(source.at[at], tiles.at[e], tile_sem.at[e]).start()

    @pl.loop(0, 2)
    def _(b):
        query_copy(b).wait()
        mask_copy(b).wait()

        @pl.loop(0, LISTED)
        def _(l):
            e = b * LISTED + l
            pltpu.make_async_copy(own.at[0], tiles.at[e], tile_sem.at[e]).wait()

        for l in range(LISTED):
            at = slice(l * BLOCK, (l + 1) * BLOCK)
            tile = tiles[b * LISTED + l].reshape(4, 2, QUARTER, WIDTH)
            kc[at, :] = tile[:, 0].reshape(BLOCK, WIDTH)
            vc[at, :] = tile[:, 1].reshape(BLOCK, WIDTH)

        for l in range(LISTED):
            at = slice(l * BLOCK, (l + 1) * BLOCK)
            kt[:, at] = kc[at, :].astype(jnp.float32).T.astype(jnp.bfloat16)
            vt[:, at] = vc[at, :].astype(jnp.float32).T.astype(jnp.bfloat16)

        quarters = pl.ds(b * 4, 4)
        for g in range(GROUP):
            at = slice(g * BLOCK, (g + 1) * BLOCK)
            qs[at, :] = qd[quarters, 0, g].reshape(BLOCK, WIDTH)
            dos[at, :] = qd[quarters, 1, g].reshape(BLOCK, WIDTH)

        def score(pair):
            q = qs[pair * rows : (pair + 1) * rows, :]
            top = jnp.full((8, rows), -jnp.inf, jnp.float32)
            for l in range(LISTED):
                at = slice(l * BLOCK, (l + 1) * BLOCK)
                s = lax.dot_general(
                    kc[at, :], q, contract_last, preferred_element_type=jnp.float32
                )
                m = mask[b * LISTED + l]
                s = jnp.minimum(s, jnp.concatenate([m, m], axis=1))
                s_scr[pair % 2, at, :] = s
                top = jnp.maximum(top, jnp.max(s.reshape(BLOCK // 8, 8, rows), axis=0))
            return jnp.max(top, axis=0, keepdims=True)

        top = score(0)
        for pair in range(GROUP // 2):
            cols = slice(pair * rows, (pair + 1) * rows)
            now = pair % 2
            total = jnp.zeros((8, rows), jnp.float32)
            for l in range(LISTED):
                at = slice(l * BLOCK, (l + 1) * BLOCK)
                w = jnp.exp2((s_scr[now, at, :] - top) * (scale * LOG2E))
                s_scr[now, at, :] = w
                total = total + jnp.sum(w.reshape(BLOCK // 8, 8, rows), axis=0)
            inverse = 1.0 / jnp.sum(total, axis=0, keepdims=True)
            if pair < GROUP // 2 - 1:
                top = score(pair + 1)
            for l in range(LISTED):
                at = slice(l * BLOCK, (l + 1) * BLOCK)
                p_scr[at, cols] = (s_scr[now, at, :] * inverse).astype(jnp.bfloat16)
            o_t = jnp.dot(vt[...], p_scr[:, cols], preferred_element_type=jnp.float32)
            do = dos[cols, :]
            do_t = do.astype(jnp.float32).T
            o_round = o_t.astype(jnp.bfloat16).astype(jnp.float32)
            row_dot = jnp.sum(o_round * do_t, axis=0, keepdims=True)
            scaled = inverse * scale
            for l in range(LISTED):
                at = slice(l * BLOCK, (l + 1) * BLOCK)
                dp = lax.dot_general(
                    vc[at, :], do, contract_last, preferred_element_type=jnp.float32
                )
                ds = ((s_scr[now, at, :] * scaled) * (dp - row_dot)).astype(jnp.bfloat16)
                d_scr[at, cols] = ds
            dq_t = jnp.dot(kt[...], d_scr[:, cols], preferred_element_type=jnp.float32)
            o = o_t.T.astype(jnp.bfloat16)
            dq = dq_t.T.astype(jnp.bfloat16)
            for i in range(2):
                at = slice(i * BLOCK, (i + 1) * BLOCK)
                out[quarters, 0, 2 * pair + i] = o[at].reshape(4, QUARTER, WIDTH)
                out[quarters, 1, 2 * pair + i] = dq[at].reshape(4, QUARTER, WIDTH)

        here = pl.ds(b * LISTED, LISTED)
        dk[here] = jnp.dot(d_scr[...], qs[...], preferred_element_type=jnp.float32).reshape(LISTED, BLOCK, WIDTH)
        dv[here] = jnp.dot(p_scr[...], dos[...], preferred_element_type=jnp.float32).reshape(LISTED, BLOCK, WIDTH)

        out_copy(b).start()

    @pl.loop(LISTED, ENTRIES)
    def _(e):
        *_, fresh, f = fields(code[base + e])

        @pl.when(fresh == 0)
        def _():
            dk[f] += dk[e]
            dv[f] += dv[e]

    def back_copies(e, act):
        _, _, owner_x, sl, fresh, _ = fields(code[base + e])
        away = (x - owner_x) & (X - 1)
        for k, buf in ((0, g0), (1, g1), (2, g2), (3, g3)):

            @pl.when((fresh == 1) & (away == k))
            def _(buf=buf):
                act(pltpu.make_async_copy(tiles.at[e], buf.at[sl], back_sem.at[e]))

    @pl.loop(0, ENTRIES)
    def _(e):
        parts = [dk[e].reshape(4, 1, QUARTER, WIDTH), dv[e].reshape(4, 1, QUARTER, WIDTH)]
        tile = jnp.concatenate(parts, axis=1).astype(jnp.bfloat16)
        tiles[e] = tile.reshape(2 * BLOCK, WIDTH)
        back_copies(e, lambda copy: copy.start())

    @pl.loop(0, ENTRIES)
    def _(e):
        back_copies(e, lambda copy: copy.wait())

    @pl.loop(0, 2)
    def _(b):
        out_copy(b).wait()


def blocks(count):
    return jax.ShapeDtypeStruct((count, 2 * BLOCK, WIDTH), jnp.bfloat16)


def shift(array, axis, by):
    size = lax.axis_size(axis)
    return lax.ppermute(array, axis, [(i, (i + by) % size) for i in range(size)])


def params(mib):
    return pltpu.CompilerParams(vmem_limit_bytes=mib * MIB)


def exchange(array, axis):
    return lax.all_to_all(array, axis, split_axis=0, concat_axis=0, tiled=True)


def gather(slots, *operands):
    return pl.pallas_call(
        gather_kernel,
        out_shape=[blocks(slots)] * 3,
        in_specs=[SMEM] * 2 + [HBM] * 2,
        out_specs=[HBM] * 3,
        scratch_shapes=[DMA((X, ENTRIES))],
        compiler_params=params(4),
    )(*operands)


def scatter(*operands):
    return pl.pallas_call(
        scatter_kernel,
        out_shape=[blocks(ENTRIES)] * 2,
        in_specs=[SMEM] * 2 + [VMEM] * 4,
        out_specs=[VMEM] * 2,
        scratch_shapes=[pltpu.VMEM((2 * ENTRIES, 2 * BLOCK, WIDTH), jnp.float32)],
        compiler_params=params(14),
    )(*operands)


def add_kernel(left, right, total):
    total[...] = (left[...].astype(jnp.float32) + right[...].astype(jnp.float32)).astype(jnp.bfloat16)


def add(*operands):
    return pl.pallas_call(
        add_kernel,
        out_shape=blocks(ENTRIES),
        in_specs=[VMEM] * 2,
        out_specs=VMEM,
        compiler_params=params(8),
    )(*operands)


def masks(*operands):
    return pl.pallas_call(
        mask_kernel,
        out_shape=jax.ShapeDtypeStruct((ENTRIES, BLOCK, BLOCK), jnp.float32),
        in_specs=[SMEM] * 3 + [VMEM],
        out_specs=VMEM,
        compiler_params=params(4),
        cost_estimate=pl.CostEstimate(flops=ENTRIES * BLOCK * BLOCK * 8, bytes_accessed=MIB, transcendentals=0),
    )(*operands)


def attend(slots, *operands):
    outs = jax.ShapeDtypeStruct((HEAD, 2, GROUP, QUARTER, WIDTH), jnp.bfloat16)
    return pl.pallas_call(
        attend_kernel,
        out_shape=[outs, blocks(ENTRIES)] + [blocks(slots)] * 3,
        in_specs=[SMEM] * 2 + [HBM] * 7,
        out_specs=[HBM] * 5,
        scratch_shapes=[
            pltpu.VMEM((HEAD, 2, GROUP, QUARTER, WIDTH), jnp.bfloat16),
            pltpu.VMEM((ENTRIES, 2 * BLOCK, WIDTH), jnp.bfloat16),
            pltpu.VMEM((ENTRIES, BLOCK, BLOCK), jnp.float32),
            pltpu.VMEM((HEAD, 2, GROUP, QUARTER, WIDTH), jnp.bfloat16),
            pltpu.VMEM((LISTED * BLOCK, WIDTH), jnp.bfloat16),
            pltpu.VMEM((LISTED * BLOCK, WIDTH), jnp.bfloat16),
            pltpu.VMEM((WIDTH, LISTED * BLOCK), jnp.bfloat16),
            pltpu.VMEM((WIDTH, LISTED * BLOCK), jnp.bfloat16),
            pltpu.VMEM((GROUP * BLOCK, WIDTH), jnp.bfloat16),
            pltpu.VMEM((GROUP * BLOCK, WIDTH), jnp.bfloat16),
            pltpu.VMEM((2, LISTED * BLOCK, 2 * BLOCK), jnp.float32),
            pltpu.VMEM((LISTED * BLOCK, GROUP * BLOCK), jnp.bfloat16),
            pltpu.VMEM((LISTED * BLOCK, GROUP * BLOCK), jnp.bfloat16),
            pltpu.VMEM((ENTRIES, BLOCK, WIDTH), jnp.float32),
            pltpu.VMEM((ENTRIES, BLOCK, WIDTH), jnp.float32),
            DMA((ENTRIES,)),
            DMA((2, 2)),
            DMA((2,)),
            DMA((ENTRIES,)),
        ],
        compiler_params=params(60),
        cost_estimate=pl.CostEstimate(
            flops=5 * 2 * 2048 * 1024 * 128, bytes_accessed=8 * MIB, transcendentals=2048 * 1024
        ),
    )(*operands)


def between(slots, place, code, own, other, qd, mask):
    sends = gather(slots, place, code, own, other)
    fetched = [shift(sends[k - 1], "x", k) for k in (1, 2, 3)]
    out, g0, g1, g2, g3 = attend(
        slots, place, code, qd, own, other, *fetched, mask
    )

    returned = [shift(g, "x", -k) for k, g in ((1, g1), (2, g2), (3, g3))]
    out = exchange(out, "head")
    *returned, out = lax.optimization_barrier((*returned, out))
    own_sum, other_sum = scatter(place, code, g0, *returned)
    from_core = shift(other_sum, "core", 1)
    column_sum = add(own_sum, from_core)
    return out, column_sum


def per_device(queries, keys, values, output_gradient, kv_list, kv_type, session_id):
    where = [lax.axis_index(axis) for axis in ("z", "x", "core")]
    place = jnp.stack(where).astype(jnp.int32)

    code, most = coded(kv_list)
    sess = session_id.astype(jnp.float32).reshape(-1, BLOCK)

    code, most = lax.optimization_barrier((code, most))

    kv = exchange(jnp.stack([keys, values]).transpose(2, 0, 1, 3), "head")
    kv = kv.reshape(2, 2 * BLOCK, WIDTH)
    kv, queries, output_gradient, sess = lax.optimization_barrier(
        (kv, queries, output_gradient, sess)
    )
    own = lax.all_gather(kv, "z", axis=0, tiled=True)

    qd = jnp.stack([queries, output_gradient]).reshape(2, QUARTER, HEAD, GROUP, WIDTH)
    qd = exchange(qd.transpose(2, 0, 3, 1, 4), "head")
    mask = masks(place, kv_list.T, kv_type.T, sess)
    own, qd, mask = lax.optimization_barrier((own, qd, mask))
    other = shift(own, "core", 1)

    out, column_sum = lax.switch(
        sum((most > few).astype(jnp.int32) for few in SLOTS[:-1]),
        [functools.partial(between, slots) for slots in SLOTS],
        place, code, own, other, qd, mask,
    )

    parts = exchange(column_sum.reshape(Z * HEAD, 2, QUARTER, WIDTH), ("z", "head"))
    parts = parts.reshape(Z, HEAD, 2, QUARTER, WIDTH)
    total = jnp.sum(parts.astype(jnp.float32), axis=0).astype(jnp.bfloat16)
    total = total.transpose(1, 2, 0, 3)

    out = out.transpose(1, 3, 0, 2, 4).reshape(2, QUARTER, HEAD * GROUP, WIDTH)
    return out[0], out[1], total[0], total[1]


def solution(mesh):
    fine = Mesh(mesh.devices.reshape(Z, X, CORE, HEAD), ("z", "x", "core", "head"))
    split = P(("z", "x", "core", "head"), None, None)
    return jax.shard_map(
        per_device,
        mesh=fine,
        in_specs=(split,) * 4 + (P(),) * 3,
        out_specs=(split,) * 4,
        check_vma=False,
    )
```

```python
import functools

import jax
import jax.numpy as jnp
from jax import lax
from jax.experimental import pallas as pl
from jax.experimental.pallas import tpu as pltpu
from jax.sharding import Mesh, PartitionSpec as P

BLOCK = 128
WIDTH = 128
LISTED = 8
ENTRIES = 16
Z, X, CORE, HEAD = 8, 4, 2, 8
CTX = Z * X * CORE
GROUP = 8
QUARTER = 32
SLOTS = (7, 8, 9, 14)
LOG2E = 1.4426950408889634
MIB = 1 << 20

SMEM = pl.BlockSpec(memory_space=pltpu.SMEM)
VMEM = pl.BlockSpec(memory_space=pltpu.VMEM)
HBM = pl.BlockSpec(memory_space=pltpu.HBM)
DMA = pltpu.SemaphoreType.DMA


def fields(code):
    bits, parts = (4, 1, 2, 4, 1), []
    for bit in bits:
        parts.append(code & ((1 << bit) - 1))
        code = lax.shift_right_logical(code, bit)
    return (*parts, code)


def coded(kv_list):
    ent = kv_list.reshape(CTX, ENTRIES)
    order = jnp.arange(ENTRIES, dtype=jnp.int32)
    equal = ent[:, :, None] == ent[:, None, :]
    first = jnp.min(jnp.where(equal, order[None, None, :], ENTRIES), axis=2)
    fresh = first == order[None, :]
    column = lax.rem(ent // 4, X)
    before = (
        fresh[:, None, :]
        & (column[:, :, None] == column[:, None, :])
        & (order[None, None, :] < first[:, :, None])
    )
    slot = jnp.sum(before.astype(jnp.int32), axis=2)
    home = lax.rem(jnp.arange(CTX, dtype=jnp.int32) // CORE, X)
    most = jnp.max(jnp.where(column == home[:, None], 0, slot + 1))
    row = ent // 16 * 2 + lax.rem(ent, 2)
    core = lax.rem(ent // 2, CORE)
    code = slot + 16 * (fresh.astype(jnp.int32) + 2 * first)
    code = row + 16 * (core + CORE * (column + X * code))
    return code.reshape(-1), most


def neighbour_entries(place, code, k, what):
    z, x, core = place[0], place[1], place[2]
    base = ((z * X + ((x + k) & (X - 1))) * CORE + core) * ENTRIES

    @pl.loop(0, ENTRIES)
    def _(e):
        row, owner_core, owner_x, sl, fresh, _ = fields(code[base + e])

        @pl.when((fresh == 1) & (owner_x == x))
        def _():
            what(e, row, owner_core == core, sl)


def gather_kernel(place, code, own, oth, s1, s2, s3, sem):
    def all_copies(act):
        for k, out in ((1, s1), (2, s2), (3, s3)):

            def one(e, row, same_core, sl, k=k, out=out):
                for source, chosen in ((own, same_core), (oth, jnp.logical_not(same_core))):

                    @pl.when(chosen)
                    def _(source=source):
                        done = sem.at[(k - 1) * ENTRIES + e]
                        act(pltpu.make_async_copy(source.at[row], out.at[sl], done))

            neighbour_entries(place, code, k, one)

    all_copies(lambda copy: copy.start())
    all_copies(lambda copy: copy.wait())


def scatter_kernel(place, code, g0, g1, g2, g3, own_out, oth_out, acc):
    acc[...] = jnp.zeros_like(acc)
    for k, buf in ((0, g0), (1, g1), (2, g2), (3, g3)):

        def add(e, row, same_core, sl, buf=buf):
            to = row + jnp.where(same_core, 0, ENTRIES)
            acc[to] += buf[sl].astype(jnp.float32)

        neighbour_entries(place, code, k, add)

    own_out[...] = acc[:ENTRIES].astype(jnp.bfloat16)
    oth_out[...] = acc[ENTRIES:].astype(jnp.bfloat16)


def mask_kernel(place, ent, kind, sess, mask):
    me = (place[0] * X + place[1]) * CORE + place[2]
    key_iota = lax.broadcasted_iota(jnp.int32, (BLOCK, BLOCK), 0)
    query_iota = lax.broadcasted_iota(jnp.int32, (BLOCK, BLOCK), 1)

    @pl.loop(0, ENTRIES)
    def _(e):
        index = me * 2 + e // LISTED
        block, t = ent[e % LISTED, index], kind[e % LISTED, index]
        sess_q = sess[pl.ds(index, 1), :]
        sess_k = jnp.broadcast_to(sess[pl.ds(block, 1), :], (BLOCK, BLOCK)).T
        needs = jnp.where((t == 0) | (t == 2), 1.0, 0.0)
        shift = jnp.where(t == 0, (block - index) * BLOCK, jnp.where(t == 3, 0, -(1 << 20)))
        seen = ((sess_k - sess_q) * needs == 0.0) & (key_iota + shift <= query_iota)
        mask[e] = jnp.where(seen, jnp.inf, -jnp.inf)


def attend_kernel(
    place, code, qd_in, own, oth, r1, r2, r3, mask_in,
    out_to, g0, g1, g2, g3,
    qd, tiles, mask, out, kc, vc, kt, vt, qs, dos, s_scr, p_scr, d_scr, dk, dv,
    tile_sem, part_sem, out_sem, back_sem,
):
    z, x, core = place[0], place[1], place[2]
    base = ((z * X + x) * CORE + core) * ENTRIES
    scale = WIDTH**-0.5
    rows = 2 * BLOCK
    contract_last = (((1,), (1,)), ((), ()))

    def query_copy(b):
        half = pl.ds(b * 4, 4)
        return pltpu.make_async_copy(qd_in.at[half], qd.at[half], part_sem.at[0, b])

    def mask_copy(b):
        half = pl.ds(b * LISTED, LISTED)
        return pltpu.make_async_copy(mask_in.at[half], mask.at[half], part_sem.at[1, b])

    def out_copy(b):
        half = pl.ds(b * 4, 4)
        return pltpu.make_async_copy(out.at[half], out_to.at[half], out_sem.at[b])

    @pl.loop(0, 2)
    def _(b):
        query_copy(b).start()
        mask_copy(b).start()

        @pl.loop(0, LISTED)
        def _(l):
            e = b * LISTED + l
            row, owner_core, owner_x, sl, _, _ = fields(code[base + e])
            away = (x - owner_x) & (X - 1)
            here = (away == 0) & (owner_core == core)
            beside = (away == 0) & (owner_core != core)
            sources = ((own, row, here), (oth, row, beside), (r1, sl, away == 1))
            sources += ((r2, sl, away == 2), (r3, sl, away == 3))
            for source, at, chosen in sources:

                @pl.when(chosen)
                def _(source=source, at=at):
                    pltpu.make_async_copy(source.at[at], tiles.at[e], tile_sem.at[e]).start()

    @pl.loop(0, 2)
    def _(b):
        query_copy(b).wait()
        mask_copy(b).wait()

        @pl.loop(0, LISTED)
        def _(l):
            e = b * LISTED + l
            pltpu.make_async_copy(own.at[0], tiles.at[e], tile_sem.at[e]).wait()

        for l in range(LISTED):
            at = slice(l * BLOCK, (l + 1) * BLOCK)
            tile = tiles[b * LISTED + l].reshape(4, 2, QUARTER, WIDTH)
            kc[at, :] = tile[:, 0].reshape(BLOCK, WIDTH)
            vc[at, :] = tile[:, 1].reshape(BLOCK, WIDTH)

        for l in range(LISTED):
            at = slice(l * BLOCK, (l + 1) * BLOCK)
            kt[:, at] = kc[at, :].astype(jnp.float32).T.astype(jnp.bfloat16)
            vt[:, at] = vc[at, :].astype(jnp.float32).T.astype(jnp.bfloat16)

        quarters = pl.ds(b * 4, 4)
        for g in range(GROUP):
            at = slice(g * BLOCK, (g + 1) * BLOCK)
            qs[at, :] = qd[quarters, 0, g].reshape(BLOCK, WIDTH)
            dos[at, :] = qd[quarters, 1, g].reshape(BLOCK, WIDTH)

        def score(pair):
            q = qs[pair * rows : (pair + 1) * rows, :]
            top = jnp.full((8, rows), -jnp.inf, jnp.float32)
            for l in range(LISTED):
                at = slice(l * BLOCK, (l + 1) * BLOCK)
                s = lax.dot_general(
                    kc[at, :], q, contract_last, preferred_element_type=jnp.float32
                )
                m = mask[b * LISTED + l]
                s = jnp.minimum(s, jnp.concatenate([m, m], axis=1))
                s_scr[pair % 2, at, :] = s
                top = jnp.maximum(top, jnp.max(s.reshape(BLOCK // 8, 8, rows), axis=0))
            return jnp.max(top, axis=0, keepdims=True)

        top = score(0)
        for pair in range(GROUP // 2):
            cols = slice(pair * rows, (pair + 1) * rows)
            now = pair % 2
            total = jnp.zeros((8, rows), jnp.float32)
            for l in range(LISTED):
                at = slice(l * BLOCK, (l + 1) * BLOCK)
                w = jnp.exp2((s_scr[now, at, :] - top) * (scale * LOG2E))
                s_scr[now, at, :] = w
                total = total + jnp.sum(w.reshape(BLOCK // 8, 8, rows), axis=0)
            inverse = 1.0 / jnp.sum(total, axis=0, keepdims=True)
            if pair < GROUP // 2 - 1:
                top = score(pair + 1)
            for l in range(LISTED):
                at = slice(l * BLOCK, (l + 1) * BLOCK)
                p_scr[at, cols] = (s_scr[now, at, :] * inverse).astype(jnp.bfloat16)
            o_t = jnp.dot(vt[...], p_scr[:, cols], preferred_element_type=jnp.float32)
            do = dos[cols, :]
            do_t = do.astype(jnp.float32).T
            o_round = o_t.astype(jnp.bfloat16).astype(jnp.float32)
            row_dot = jnp.sum(o_round * do_t, axis=0, keepdims=True)
            scaled = inverse * scale
            for l in range(LISTED):
                at = slice(l * BLOCK, (l + 1) * BLOCK)
                dp = lax.dot_general(
                    vc[at, :], do, contract_last, preferred_element_type=jnp.float32
                )
                ds = ((s_scr[now, at, :] * scaled) * (dp - row_dot)).astype(jnp.bfloat16)
                d_scr[at, cols] = ds
            dq_t = jnp.dot(kt[...], d_scr[:, cols], preferred_element_type=jnp.float32)
            o = o_t.T.astype(jnp.bfloat16)
            dq = dq_t.T.astype(jnp.bfloat16)
            for i in range(2):
                at = slice(i * BLOCK, (i + 1) * BLOCK)
                out[quarters, 0, 2 * pair + i] = o[at].reshape(4, QUARTER, WIDTH)
                out[quarters, 1, 2 * pair + i] = dq[at].reshape(4, QUARTER, WIDTH)

        here = pl.ds(b * LISTED, LISTED)
        dk[here] = jnp.dot(d_scr[...], qs[...], preferred_element_type=jnp.float32).reshape(LISTED, BLOCK, WIDTH)
        dv[here] = jnp.dot(p_scr[...], dos[...], preferred_element_type=jnp.float32).reshape(LISTED, BLOCK, WIDTH)

        out_copy(b).start()

    @pl.loop(LISTED, ENTRIES)
    def _(e):
        *_, fresh, f = fields(code[base + e])

        @pl.when(fresh == 0)
        def _():
            dk[f] += dk[e]
            dv[f] += dv[e]

    def back_copies(e, act):
        _, _, owner_x, sl, fresh, _ = fields(code[base + e])
        away = (x - owner_x) & (X - 1)
        for k, buf in ((0, g0), (1, g1), (2, g2), (3, g3)):

            @pl.when((fresh == 1) & (away == k))
            def _(buf=buf):
                act(pltpu.make_async_copy(tiles.at[e], buf.at[sl], back_sem.at[e]))

    @pl.loop(0, ENTRIES)
    def _(e):
        parts = [dk[e].reshape(4, 1, QUARTER, WIDTH), dv[e].reshape(4, 1, QUARTER, WIDTH)]
        tile = jnp.concatenate(parts, axis=1).astype(jnp.bfloat16)
        tiles[e] = tile.reshape(2 * BLOCK, WIDTH)
        back_copies(e, lambda copy: copy.start())

    @pl.loop(0, ENTRIES)
    def _(e):
        back_copies(e, lambda copy: copy.wait())

    @pl.loop(0, 2)
    def _(b):
        out_copy(b).wait()


def blocks(count):
    return jax.ShapeDtypeStruct((count, 2 * BLOCK, WIDTH), jnp.bfloat16)


def shift(array, axis, by):
    size = lax.axis_size(axis)
    return lax.ppermute(array, axis, [(i, (i + by) % size) for i in range(size)])


def params(mib):
    return pltpu.CompilerParams(vmem_limit_bytes=mib * MIB)


def exchange(array, axis):
    return lax.all_to_all(array, axis, split_axis=0, concat_axis=0, tiled=True)


def gather(slots, *operands):
    return pl.pallas_call(
        gather_kernel,
        out_shape=[blocks(slots)] * 3,
        in_specs=[SMEM] * 2 + [HBM] * 2,
        out_specs=[HBM] * 3,
        scratch_shapes=[DMA((3 * ENTRIES,))],
        compiler_params=params(4),
    )(*operands)


def scatter(*operands):
    return pl.pallas_call(
        scatter_kernel,
        out_shape=[blocks(ENTRIES)] * 2,
        in_specs=[SMEM] * 2 + [VMEM] * 4,
        out_specs=[VMEM] * 2,
        scratch_shapes=[pltpu.VMEM((2 * ENTRIES, 2 * BLOCK, WIDTH), jnp.float32)],
        compiler_params=params(14),
    )(*operands)


def add_kernel(left, right, total):
    total[...] = (left[...].astype(jnp.float32) + right[...].astype(jnp.float32)).astype(jnp.bfloat16)


def add(*operands):
    return pl.pallas_call(
        add_kernel,
        out_shape=blocks(ENTRIES),
        in_specs=[VMEM] * 2,
        out_specs=VMEM,
        compiler_params=params(8),
    )(*operands)


def masks(*operands):
    return pl.pallas_call(
        mask_kernel,
        out_shape=jax.ShapeDtypeStruct((ENTRIES, BLOCK, BLOCK), jnp.float32),
        in_specs=[SMEM] * 3 + [VMEM],
        out_specs=VMEM,
        compiler_params=params(4),
        cost_estimate=pl.CostEstimate(flops=ENTRIES * BLOCK * BLOCK * 8, bytes_accessed=MIB, transcendentals=0),
    )(*operands)


def attend(slots, *operands):
    outs = jax.ShapeDtypeStruct((HEAD, 2, GROUP, QUARTER, WIDTH), jnp.bfloat16)
    return pl.pallas_call(
        attend_kernel,
        out_shape=[outs, blocks(ENTRIES)] + [blocks(slots)] * 3,
        in_specs=[SMEM] * 2 + [HBM] * 7,
        out_specs=[HBM] * 5,
        scratch_shapes=[
            pltpu.VMEM((HEAD, 2, GROUP, QUARTER, WIDTH), jnp.bfloat16),
            pltpu.VMEM((ENTRIES, 2 * BLOCK, WIDTH), jnp.bfloat16),
            pltpu.VMEM((ENTRIES, BLOCK, BLOCK), jnp.float32),
            pltpu.VMEM((HEAD, 2, GROUP, QUARTER, WIDTH), jnp.bfloat16),
            pltpu.VMEM((LISTED * BLOCK, WIDTH), jnp.bfloat16),
            pltpu.VMEM((LISTED * BLOCK, WIDTH), jnp.bfloat16),
            pltpu.VMEM((WIDTH, LISTED * BLOCK), jnp.bfloat16),
            pltpu.VMEM((WIDTH, LISTED * BLOCK), jnp.bfloat16),
            pltpu.VMEM((GROUP * BLOCK, WIDTH), jnp.bfloat16),
            pltpu.VMEM((GROUP * BLOCK, WIDTH), jnp.bfloat16),
            pltpu.VMEM((2, LISTED * BLOCK, 2 * BLOCK), jnp.float32),
            pltpu.VMEM((LISTED * BLOCK, GROUP * BLOCK), jnp.bfloat16),
            pltpu.VMEM((LISTED * BLOCK, GROUP * BLOCK), jnp.bfloat16),
            pltpu.VMEM((ENTRIES, BLOCK, WIDTH), jnp.float32),
            pltpu.VMEM((ENTRIES, BLOCK, WIDTH), jnp.float32),
            DMA((ENTRIES,)),
            DMA((2, 2)),
            DMA((2,)),
            DMA((ENTRIES,)),
        ],
        compiler_params=params(60),
        cost_estimate=pl.CostEstimate(
            flops=5 * 2 * 2048 * 1024 * 128, bytes_accessed=8 * MIB, transcendentals=2048 * 1024
        ),
    )(*operands)


def between(slots, place, code, own, qd, mask):
    other = shift(own, "core", 1)
    sends = gather(slots, place, code, own, other)
    fetched = [shift(sends[k - 1], "x", k) for k in (1, 2, 3)]
    qd = exchange(qd, "head")
    out, g0, g1, g2, g3 = attend(
        slots, place, code, qd, own, other, *fetched, mask
    )

    returned = [shift(g, "x", -k) for k, g in ((1, g1), (2, g2), (3, g3))]
    out = exchange(out, "head")
    *returned, out = lax.optimization_barrier((*returned, out))
    own_sum, other_sum = scatter(place, code, g0, *returned)
    from_core = shift(other_sum, "core", 1)
    column_sum = add(own_sum, from_core)
    return out, column_sum


def per_device(queries, keys, values, output_gradient, kv_list, kv_type, session_id):
    where = [lax.axis_index(axis) for axis in ("z", "x", "core")]
    place = jnp.stack(where).astype(jnp.int32)

    code, most = coded(kv_list)
    sess = session_id.astype(jnp.float32).reshape(-1, BLOCK)

    code, most = lax.optimization_barrier((code, most))

    kv = jnp.stack([keys, values]).transpose(2, 0, 1, 3)
    kv = jnp.broadcast_to(kv, (Z, HEAD, 2, QUARTER, WIDTH))
    own = exchange(kv.reshape(Z * HEAD, 2, QUARTER, WIDTH), ("z", "head"))
    own = own.reshape(ENTRIES, 2 * BLOCK, WIDTH)

    qd = jnp.stack([queries, output_gradient]).reshape(2, QUARTER, HEAD, GROUP, WIDTH)
    qd = qd.transpose(2, 0, 3, 1, 4)
    mask = masks(place, kv_list.T, kv_type.T, sess)
    qd, mask = lax.optimization_barrier((qd, mask))

    out, column_sum = lax.switch(
        sum((most > few).astype(jnp.int32) for few in SLOTS[:-1]),
        [functools.partial(between, slots) for slots in SLOTS],
        place, code, own, qd, mask,
    )

    parts = exchange(column_sum.reshape(Z * HEAD, 2, QUARTER, WIDTH), ("z", "head"))
    parts = parts.reshape(Z, HEAD, 2, QUARTER, WIDTH)
    total = jnp.sum(parts.astype(jnp.float32), axis=0).astype(jnp.bfloat16)
    total = total.transpose(1, 2, 0, 3)

    out = out.transpose(1, 3, 0, 2, 4).reshape(2, QUARTER, HEAD * GROUP, WIDTH)
    return out[0], out[1], total[0], total[1]


def solution(mesh):
    fine = Mesh(mesh.devices.reshape(Z, X, CORE, HEAD), ("z", "x", "core", "head"))
    split = P(("z", "x", "core", "head"), None, None)
    return jax.shard_map(
        per_device,
        mesh=fine,
        in_specs=(split,) * 4 + (P(),) * 3,
        out_specs=(split,) * 4,
        check_vma=False,
    )
```

```python
import functools

import jax
import jax.numpy as jnp
from jax import lax
from jax.experimental import pallas as pl
from jax.experimental.pallas import tpu as pltpu
from jax.sharding import Mesh, PartitionSpec as P

BLOCK = 128
WIDTH = 128
LISTED = 8
ENTRIES = 16
Z, X, CORE, HEAD = 8, 4, 2, 8
CTX = Z * X * CORE
GROUP = 8
QUARTER = 32
SLOTS = (7, 8, 9, 14)
LOG2E = 1.4426950408889634
MIB = 1 << 20

SMEM = pl.BlockSpec(memory_space=pltpu.SMEM)
VMEM = pl.BlockSpec(memory_space=pltpu.VMEM)
HBM = pl.BlockSpec(memory_space=pltpu.HBM)
DMA = pltpu.SemaphoreType.DMA


def fields(code):
    bits, parts = (4, 1, 2, 4, 1), []
    for bit in bits:
        parts.append(code & ((1 << bit) - 1))
        code = lax.shift_right_logical(code, bit)
    return (*parts, code)


def coded(kv_list):
    ent = kv_list.reshape(CTX, ENTRIES)
    order = jnp.arange(ENTRIES, dtype=jnp.int32)
    equal = ent[:, :, None] == ent[:, None, :]
    first = jnp.min(jnp.where(equal, order[None, None, :], ENTRIES), axis=2)
    fresh = first == order[None, :]
    column = lax.rem(ent // 4, X)
    before = (
        fresh[:, None, :]
        & (column[:, :, None] == column[:, None, :])
        & (order[None, None, :] < first[:, :, None])
    )
    slot = jnp.sum(before.astype(jnp.int32), axis=2)
    home = lax.rem(jnp.arange(CTX, dtype=jnp.int32) // CORE, X)
    most = jnp.max(jnp.where(column == home[:, None], 0, slot + 1))
    row = ent // 16 * 2 + lax.rem(ent, 2)
    core = lax.rem(ent // 2, CORE)
    code = slot + 16 * (fresh.astype(jnp.int32) + 2 * first)
    code = row + 16 * (core + CORE * (column + X * code))
    return code.reshape(-1), most


def neighbour_lists(place, code):
    z, x, core = place
    index = [(z * X + lax.rem(x + k, X)) * CORE + core for k in range(X)]
    code = code.reshape(CTX, ENTRIES)
    lines = jnp.stack([lax.dynamic_index_in_dim(code, d, 0, keepdims=False) for d in index])
    row, owner_core, owner_x, slot, fresh, _ = fields(lines)
    mine = (fresh == 1) & (owner_x == x)
    at = row + jnp.where(owner_core == core, 0, ENTRIES)
    slots = jnp.arange(ENTRIES, dtype=jnp.int32)[None, :, None]
    here = mine[:, None, :] & (slot[:, None, :] == slots)
    listed = jnp.sum(jnp.where(here, at[:, None, :], 0), axis=2)
    count = jnp.sum(mine.astype(jnp.int32), axis=1)
    return jnp.concatenate([listed.reshape(-1), count])


def gather_kernel(lists, own, oth, s1, s2, s3, sem):
    for k, out in ((2, s2), (1, s1), (3, s3)):

        @pl.loop(0, lists[X * ENTRIES + k])
        def _(sl, k=k, out=out):
            at = lists[k * ENTRIES + sl]

            @pl.when(at < ENTRIES)
            def _():
                pltpu.make_async_copy(own.at[at], out.at[sl], sem.at[k * ENTRIES + sl]).start()

            @pl.when(at >= ENTRIES)
            def _():
                source = oth.at[at - ENTRIES]
                pltpu.make_async_copy(source, out.at[sl], sem.at[k * ENTRIES + sl]).start()

    for k, out in ((2, s2), (1, s1), (3, s3)):

        @pl.loop(0, lists[X * ENTRIES + k])
        def _(sl, k=k, out=out):
            pltpu.make_async_copy(own.at[0], out.at[sl], sem.at[k * ENTRIES + sl]).wait()


def scatter_kernel(lists, g0, g1, g2, g3, own_out, oth_out, acc):
    acc[...] = jnp.zeros_like(acc)
    for k, buf in ((0, g0), (1, g1), (2, g2), (3, g3)):

        @pl.loop(0, lists[X * ENTRIES + k])
        def _(sl, k=k, buf=buf):
            acc[lists[k * ENTRIES + sl]] += buf[sl].astype(jnp.float32)

    own_out[...] = acc[:ENTRIES].astype(jnp.bfloat16)
    oth_out[...] = acc[ENTRIES:].astype(jnp.bfloat16)


def mask_kernel(place, ent, kind, sess, mask):
    me = (place[0] * X + place[1]) * CORE + place[2]
    key_iota = lax.broadcasted_iota(jnp.int32, (BLOCK, BLOCK), 0)
    query_iota = lax.broadcasted_iota(jnp.int32, (BLOCK, BLOCK), 1)

    @pl.loop(0, ENTRIES)
    def _(e):
        index = me * 2 + e // LISTED
        block, t = ent[e % LISTED, index], kind[e % LISTED, index]
        sess_q = sess[pl.ds(index, 1), :]
        sess_k = jnp.broadcast_to(sess[pl.ds(block, 1), :], (BLOCK, BLOCK)).T
        needs = jnp.where((t == 0) | (t == 2), 1.0, 0.0)
        shift = jnp.where(t == 0, (block - index) * BLOCK, jnp.where(t == 3, 0, -(1 << 20)))
        seen = ((sess_k - sess_q) * needs == 0.0) & (key_iota + shift <= query_iota)
        mask[e] = jnp.where(seen, jnp.inf, -jnp.inf)


def attend_kernel(
    place, code, qd_in, own, oth, r1, r2, r3, mask_in,
    out_to, g0, g1, g2, g3,
    qd, tiles, mask, out, kc, vc, kt, vt, qs, dos, s_scr, p_scr, d_scr, dk, dv,
    tile_sem, part_sem, out_sem, back_sem,
):
    z, x, core = place[0], place[1], place[2]
    base = ((z * X + x) * CORE + core) * ENTRIES
    scale = WIDTH**-0.5
    rows = 2 * BLOCK
    contract_last = (((1,), (1,)), ((), ()))

    def query_copy(b):
        half = pl.ds(b * 4, 4)
        return pltpu.make_async_copy(qd_in.at[half], qd.at[half], part_sem.at[0, b])

    def mask_copy(b):
        half = pl.ds(b * LISTED, LISTED)
        return pltpu.make_async_copy(mask_in.at[half], mask.at[half], part_sem.at[1, b])

    def out_copy(b):
        half = pl.ds(b * 4, 4)
        return pltpu.make_async_copy(out.at[half], out_to.at[half], out_sem.at[b])

    @pl.loop(0, 2)
    def _(b):
        query_copy(b).start()
        mask_copy(b).start()

        @pl.loop(0, LISTED)
        def _(l):
            e = b * LISTED + l
            row, owner_core, owner_x, sl, _, _ = fields(code[base + e])
            away = (x - owner_x) & (X - 1)
            here = (away == 0) & (owner_core == core)
            beside = (away == 0) & (owner_core != core)
            sources = ((own, row, here), (oth, row, beside), (r1, sl, away == 1))
            sources += ((r2, sl, away == 2), (r3, sl, away == 3))
            for source, at, chosen in sources:

                @pl.when(chosen)
                def _(source=source, at=at):
                    pltpu.make_async_copy(source.at[at], tiles.at[e], tile_sem.at[e]).start()

    @pl.loop(0, 2)
    def _(b):
        query_copy(b).wait()
        mask_copy(b).wait()

        @pl.loop(0, LISTED)
        def _(l):
            e = b * LISTED + l
            pltpu.make_async_copy(own.at[0], tiles.at[e], tile_sem.at[e]).wait()

        for l in range(LISTED):
            at = slice(l * BLOCK, (l + 1) * BLOCK)
            tile = tiles[b * LISTED + l].reshape(4, 2, QUARTER, WIDTH)
            kc[at, :] = tile[:, 0].reshape(BLOCK, WIDTH)
            vc[at, :] = tile[:, 1].reshape(BLOCK, WIDTH)

        for l in range(LISTED):
            at = slice(l * BLOCK, (l + 1) * BLOCK)
            kt[:, at] = kc[at, :].astype(jnp.float32).T.astype(jnp.bfloat16)
            vt[:, at] = vc[at, :].astype(jnp.float32).T.astype(jnp.bfloat16)

        quarters = pl.ds(b * 4, 4)
        for g in range(GROUP):
            at = slice(g * BLOCK, (g + 1) * BLOCK)
            qs[at, :] = qd[quarters, 0, g].reshape(BLOCK, WIDTH)
            dos[at, :] = qd[quarters, 1, g].reshape(BLOCK, WIDTH)

        def score(pair):
            q = qs[pair * rows : (pair + 1) * rows, :]
            top = jnp.full((8, rows), -jnp.inf, jnp.float32)
            for l in range(LISTED):
                at = slice(l * BLOCK, (l + 1) * BLOCK)
                s = lax.dot_general(
                    kc[at, :], q, contract_last, preferred_element_type=jnp.float32
                )
                m = mask[b * LISTED + l]
                s = jnp.minimum(s, jnp.concatenate([m, m], axis=1))
                s_scr[pair % 2, at, :] = s
                top = jnp.maximum(top, jnp.max(s.reshape(BLOCK // 8, 8, rows), axis=0))
            return jnp.max(top, axis=0, keepdims=True)

        top = score(0)
        for pair in range(GROUP // 2):
            cols = slice(pair * rows, (pair + 1) * rows)
            now = pair % 2
            total = jnp.zeros((8, rows), jnp.float32)
            for l in range(LISTED):
                at = slice(l * BLOCK, (l + 1) * BLOCK)
                w = jnp.exp2((s_scr[now, at, :] - top) * (scale * LOG2E))
                s_scr[now, at, :] = w
                total = total + jnp.sum(w.reshape(BLOCK // 8, 8, rows), axis=0)
            inverse = 1.0 / jnp.sum(total, axis=0, keepdims=True)
            if pair < GROUP // 2 - 1:
                top = score(pair + 1)
            for l in range(LISTED):
                at = slice(l * BLOCK, (l + 1) * BLOCK)
                p_scr[at, cols] = (s_scr[now, at, :] * inverse).astype(jnp.bfloat16)
            o_t = jnp.dot(vt[...], p_scr[:, cols], preferred_element_type=jnp.float32)
            do = dos[cols, :]
            do_t = do.astype(jnp.float32).T
            o_round = o_t.astype(jnp.bfloat16).astype(jnp.float32)
            row_dot = jnp.sum(o_round * do_t, axis=0, keepdims=True)
            scaled = inverse * scale
            for l in range(LISTED):
                at = slice(l * BLOCK, (l + 1) * BLOCK)
                dp = lax.dot_general(
                    vc[at, :], do, contract_last, preferred_element_type=jnp.float32
                )
                ds = ((s_scr[now, at, :] * scaled) * (dp - row_dot)).astype(jnp.bfloat16)
                d_scr[at, cols] = ds
            dq_t = jnp.dot(kt[...], d_scr[:, cols], preferred_element_type=jnp.float32)
            o = o_t.T.astype(jnp.bfloat16)
            dq = dq_t.T.astype(jnp.bfloat16)
            for i in range(2):
                at = slice(i * BLOCK, (i + 1) * BLOCK)
                out[quarters, 0, 2 * pair + i] = o[at].reshape(4, QUARTER, WIDTH)
                out[quarters, 1, 2 * pair + i] = dq[at].reshape(4, QUARTER, WIDTH)

        here = pl.ds(b * LISTED, LISTED)
        dk[here] = jnp.dot(d_scr[...], qs[...], preferred_element_type=jnp.float32).reshape(LISTED, BLOCK, WIDTH)
        dv[here] = jnp.dot(p_scr[...], dos[...], preferred_element_type=jnp.float32).reshape(LISTED, BLOCK, WIDTH)

        out_copy(b).start()

    @pl.loop(LISTED, ENTRIES)
    def _(e):
        *_, fresh, f = fields(code[base + e])

        @pl.when(fresh == 0)
        def _():
            dk[f] += dk[e]
            dv[f] += dv[e]

    def back_copies(e, act):
        _, _, owner_x, sl, fresh, _ = fields(code[base + e])
        away = (x - owner_x) & (X - 1)
        for k, buf in ((0, g0), (1, g1), (2, g2), (3, g3)):

            @pl.when((fresh == 1) & (away == k))
            def _(buf=buf):
                act(pltpu.make_async_copy(tiles.at[e], buf.at[sl], back_sem.at[e]))

    @pl.loop(0, ENTRIES)
    def _(e):
        parts = [dk[e].reshape(4, 1, QUARTER, WIDTH), dv[e].reshape(4, 1, QUARTER, WIDTH)]
        tile = jnp.concatenate(parts, axis=1).astype(jnp.bfloat16)
        tiles[e] = tile.reshape(2 * BLOCK, WIDTH)
        back_copies(e, lambda copy: copy.start())

    @pl.loop(0, ENTRIES)
    def _(e):
        back_copies(e, lambda copy: copy.wait())

    @pl.loop(0, 2)
    def _(b):
        out_copy(b).wait()


def blocks(count):
    return jax.ShapeDtypeStruct((count, 2 * BLOCK, WIDTH), jnp.bfloat16)


def shift(array, axis, by):
    size = lax.axis_size(axis)
    return lax.ppermute(array, axis, [(i, (i + by) % size) for i in range(size)])


def params(mib):
    return pltpu.CompilerParams(vmem_limit_bytes=mib * MIB)


def exchange(array, axis):
    return lax.all_to_all(array, axis, split_axis=0, concat_axis=0, tiled=True)


def gather(slots, *operands):
    return pl.pallas_call(
        gather_kernel,
        out_shape=[blocks(slots)] * 3,
        in_specs=[SMEM] + [HBM] * 2,
        out_specs=[HBM] * 3,
        scratch_shapes=[DMA((X * ENTRIES,))],
        compiler_params=params(4),
    )(*operands)


def scatter(*operands):
    return pl.pallas_call(
        scatter_kernel,
        out_shape=[blocks(ENTRIES)] * 2,
        in_specs=[SMEM] + [VMEM] * 4,
        out_specs=[VMEM] * 2,
        scratch_shapes=[pltpu.VMEM((2 * ENTRIES, 2 * BLOCK, WIDTH), jnp.float32)],
        compiler_params=params(14),
    )(*operands)


def add_kernel(left, right, total):
    total[...] = (left[...].astype(jnp.float32) + right[...].astype(jnp.float32)).astype(jnp.bfloat16)


def add(*operands):
    return pl.pallas_call(
        add_kernel,
        out_shape=blocks(ENTRIES),
        in_specs=[VMEM] * 2,
        out_specs=VMEM,
        compiler_params=params(8),
    )(*operands)


def masks(*operands):
    return pl.pallas_call(
        mask_kernel,
        out_shape=jax.ShapeDtypeStruct((ENTRIES, BLOCK, BLOCK), jnp.float32),
        in_specs=[SMEM] * 3 + [VMEM],
        out_specs=VMEM,
        compiler_params=params(4),
        cost_estimate=pl.CostEstimate(flops=ENTRIES * BLOCK * BLOCK * 8, bytes_accessed=MIB, transcendentals=0),
    )(*operands)


def attend(slots, *operands):
    outs = jax.ShapeDtypeStruct((HEAD, 2, GROUP, QUARTER, WIDTH), jnp.bfloat16)
    return pl.pallas_call(
        attend_kernel,
        out_shape=[outs, blocks(ENTRIES)] + [blocks(slots)] * 3,
        in_specs=[SMEM] * 2 + [HBM] * 7,
        out_specs=[HBM] * 5,
        scratch_shapes=[
            pltpu.VMEM((HEAD, 2, GROUP, QUARTER, WIDTH), jnp.bfloat16),
            pltpu.VMEM((ENTRIES, 2 * BLOCK, WIDTH), jnp.bfloat16),
            pltpu.VMEM((ENTRIES, BLOCK, BLOCK), jnp.float32),
            pltpu.VMEM((HEAD, 2, GROUP, QUARTER, WIDTH), jnp.bfloat16),
            pltpu.VMEM((LISTED * BLOCK, WIDTH), jnp.bfloat16),
            pltpu.VMEM((LISTED * BLOCK, WIDTH), jnp.bfloat16),
            pltpu.VMEM((WIDTH, LISTED * BLOCK), jnp.bfloat16),
            pltpu.VMEM((WIDTH, LISTED * BLOCK), jnp.bfloat16),
            pltpu.VMEM((GROUP * BLOCK, WIDTH), jnp.bfloat16),
            pltpu.VMEM((GROUP * BLOCK, WIDTH), jnp.bfloat16),
            pltpu.VMEM((2, LISTED * BLOCK, 2 * BLOCK), jnp.float32),
            pltpu.VMEM((LISTED * BLOCK, GROUP * BLOCK), jnp.bfloat16),
            pltpu.VMEM((LISTED * BLOCK, GROUP * BLOCK), jnp.bfloat16),
            pltpu.VMEM((ENTRIES, BLOCK, WIDTH), jnp.float32),
            pltpu.VMEM((ENTRIES, BLOCK, WIDTH), jnp.float32),
            DMA((ENTRIES,)),
            DMA((2, 2)),
            DMA((2,)),
            DMA((ENTRIES,)),
        ],
        compiler_params=params(60),
        cost_estimate=pl.CostEstimate(
            flops=5 * 2 * 2048 * 1024 * 128, bytes_accessed=8 * MIB, transcendentals=2048 * 1024
        ),
    )(*operands)


def between(slots, place, code, lists, own, qd, mask):
    other = shift(own, "core", 1)
    sends = gather(slots, lists, own, other)
    r2, r1, r3 = [shift(sends[k - 1], "x", k) for k in (2, 1, 3)]
    qd = exchange(qd, "head")
    out, g0, g1, g2, g3 = attend(
        slots, place, code, qd, own, other, r1, r2, r3, mask
    )

    g2, g1, g3 = [shift(g, "x", -k) for k, g in ((2, g2), (1, g1), (3, g3))]
    out = exchange(out, "head")
    g1, g2, g3, out = lax.optimization_barrier((g1, g2, g3, out))
    own_sum, other_sum = scatter(lists, g0, g1, g2, g3)
    from_core = shift(other_sum, "core", 1)
    column_sum = add(own_sum, from_core)
    return out, column_sum


def per_device(queries, keys, values, output_gradient, kv_list, kv_type, session_id):
    where = [lax.axis_index(axis).astype(jnp.int32) for axis in ("z", "x", "core")]
    place = jnp.stack(where)

    code, most = coded(kv_list)
    sess = session_id.astype(jnp.float32).reshape(-1, BLOCK)

    lists = neighbour_lists(where, code)
    code, most, lists = lax.optimization_barrier((code, most, lists))

    kv = jnp.stack([keys, values]).transpose(2, 0, 1, 3)
    kv = jnp.broadcast_to(kv, (Z, HEAD, 2, QUARTER, WIDTH))
    own = exchange(kv.reshape(Z * HEAD, 2, QUARTER, WIDTH), ("z", "head"))
    own = own.reshape(ENTRIES, 2 * BLOCK, WIDTH)

    qd = jnp.stack([queries, output_gradient]).reshape(2, QUARTER, HEAD, GROUP, WIDTH)
    qd = qd.transpose(2, 0, 3, 1, 4)
    mask = masks(place, kv_list.T, kv_type.T, sess)
    qd, mask = lax.optimization_barrier((qd, mask))

    out, column_sum = lax.switch(
        sum((most > few).astype(jnp.int32) for few in SLOTS[:-1]),
        [functools.partial(between, slots) for slots in SLOTS],
        place, code, lists, own, qd, mask,
    )

    parts = exchange(column_sum.reshape(Z * HEAD, 2, QUARTER, WIDTH), ("z", "head"))
    parts = parts.reshape(Z, HEAD, 2, QUARTER, WIDTH)
    total = jnp.sum(parts.astype(jnp.float32), axis=0).astype(jnp.bfloat16)
    total = total.transpose(1, 2, 0, 3)

    out = out.transpose(1, 3, 0, 2, 4).reshape(2, QUARTER, HEAD * GROUP, WIDTH)
    return out[0], out[1], total[0], total[1]


def solution(mesh):
    fine = Mesh(mesh.devices.reshape(Z, X, CORE, HEAD), ("z", "x", "core", "head"))
    split = P(("z", "x", "core", "head"), None, None)
    return jax.shard_map(
        per_device,
        mesh=fine,
        in_specs=(split,) * 4 + (P(),) * 3,
        out_specs=(split,) * 4,
        check_vma=False,
    )
```

```python
import functools

import jax
import jax.numpy as jnp
from jax import lax
from jax.experimental import pallas as pl
from jax.experimental.pallas import tpu as pltpu
from jax.sharding import Mesh, PartitionSpec as P

BLOCK = 128
WIDTH = 128
LISTED = 8
ENTRIES = 16
Z, X, CORE, HEAD = 8, 4, 2, 8
CTX = Z * X * CORE
GROUP = 8
QUARTER = 32
SLOTS = (7, 8, 9, 14)
LOG2E = 1.4426950408889634
MIB = 1 << 20

SMEM = pl.BlockSpec(memory_space=pltpu.SMEM)
VMEM = pl.BlockSpec(memory_space=pltpu.VMEM)
HBM = pl.BlockSpec(memory_space=pltpu.HBM)
DMA = pltpu.SemaphoreType.DMA


def fields(code):
    bits, parts = (4, 1, 2, 4, 1), []
    for bit in bits:
        parts.append(code & ((1 << bit) - 1))
        code = lax.shift_right_logical(code, bit)
    return (*parts, code)


def coded(kv_list):
    ent = kv_list.reshape(CTX, ENTRIES)
    order = jnp.arange(ENTRIES, dtype=jnp.int32)
    equal = ent[:, :, None] == ent[:, None, :]
    first = jnp.min(jnp.where(equal, order[None, None, :], ENTRIES), axis=2)
    fresh = first == order[None, :]
    column = lax.rem(ent // 4, X)
    before = (
        fresh[:, None, :]
        & (column[:, :, None] == column[:, None, :])
        & (order[None, None, :] < first[:, :, None])
    )
    slot = jnp.sum(before.astype(jnp.int32), axis=2)
    home = lax.rem(jnp.arange(CTX, dtype=jnp.int32) // CORE, X)
    most = jnp.max(jnp.where(column == home[:, None], 0, slot + 1))
    row = ent // 16 * 2 + lax.rem(ent, 2)
    core = lax.rem(ent // 2, CORE)
    code = slot + 16 * (fresh.astype(jnp.int32) + 2 * first)
    code = row + 16 * (core + CORE * (column + X * code))
    return code.reshape(-1), most


def neighbour_lists(place, code):
    z, x, core = place
    index = [(z * X + lax.rem(x + k, X)) * CORE + core for k in range(X)]
    code = code.reshape(CTX, ENTRIES)
    lines = jnp.stack([lax.dynamic_index_in_dim(code, d, 0, keepdims=False) for d in index])
    row, owner_core, owner_x, slot, fresh, _ = fields(lines)
    mine = (fresh == 1) & (owner_x == x)
    at = row + jnp.where(owner_core == core, 0, ENTRIES)
    slots = jnp.arange(ENTRIES, dtype=jnp.int32)[None, :, None]
    here = mine[:, None, :] & (slot[:, None, :] == slots)
    listed = jnp.sum(jnp.where(here, at[:, None, :], 0), axis=2)
    count = jnp.sum(mine.astype(jnp.int32), axis=1)
    return jnp.concatenate([listed.reshape(-1), count])


def gather_kernel(lists, own, oth, s1, s2, s3, sem):
    for k, out in ((2, s2), (1, s1), (3, s3)):

        @pl.loop(0, lists[X * ENTRIES + k])
        def _(sl, k=k, out=out):
            at = lists[k * ENTRIES + sl]

            @pl.when(at < ENTRIES)
            def _():
                pltpu.make_async_copy(own.at[at], out.at[sl], sem.at[k * ENTRIES + sl]).start()

            @pl.when(at >= ENTRIES)
            def _():
                source = oth.at[at - ENTRIES]
                pltpu.make_async_copy(source, out.at[sl], sem.at[k * ENTRIES + sl]).start()

    for k, out in ((2, s2), (1, s1), (3, s3)):

        @pl.loop(0, lists[X * ENTRIES + k])
        def _(sl, k=k, out=out):
            pltpu.make_async_copy(own.at[0], out.at[sl], sem.at[k * ENTRIES + sl]).wait()


def scatter_kernel(lists, g0, g1, g2, g3, own_out, oth_out, acc):
    acc[...] = jnp.zeros_like(acc)
    for k, buf in ((0, g0), (1, g1), (2, g2), (3, g3)):

        @pl.loop(0, lists[X * ENTRIES + k])
        def _(sl, k=k, buf=buf):
            acc[lists[k * ENTRIES + sl]] += buf[sl].astype(jnp.float32)

    own_out[...] = acc[:ENTRIES].astype(jnp.bfloat16)
    oth_out[...] = acc[ENTRIES:].astype(jnp.bfloat16)


def mask_kernel(place, ent, kind, sess, mask):
    me = (place[0] * X + place[1]) * CORE + place[2]
    key_iota = lax.broadcasted_iota(jnp.int32, (BLOCK, BLOCK), 0)
    query_iota = lax.broadcasted_iota(jnp.int32, (BLOCK, BLOCK), 1)

    @pl.loop(0, ENTRIES)
    def _(e):
        index = me * 2 + e // LISTED
        block, t = ent[e % LISTED, index], kind[e % LISTED, index]
        sess_q = sess[pl.ds(index, 1), :]
        sess_k = jnp.broadcast_to(sess[pl.ds(block, 1), :], (BLOCK, BLOCK)).T
        needs = jnp.where((t == 0) | (t == 2), 1.0, 0.0)
        shift = jnp.where(t == 0, (block - index) * BLOCK, jnp.where(t == 3, 0, -(1 << 20)))
        seen = ((sess_k - sess_q) * needs == 0.0) & (key_iota + shift <= query_iota)
        mask[e] = jnp.where(seen, jnp.inf, -jnp.inf)


def attend_kernel(
    place, code, qd_in, own, oth, r1, r2, r3, mask_in,
    out_to, g0, g1, g2, g3,
    qd, tiles, mask, out, kc, vc, kt, vt, qs, dos, s_scr, p_scr, d_scr, dk, dv,
    tile_sem, part_sem, out_sem, back_sem,
):
    z, x, core = place[0], place[1], place[2]
    base = ((z * X + x) * CORE + core) * ENTRIES
    scale = WIDTH**-0.5
    rows = 2 * BLOCK
    contract_last = (((1,), (1,)), ((), ()))

    def query_copy(b):
        half = pl.ds(b * 4, 4)
        return pltpu.make_async_copy(qd_in.at[half], qd.at[half], part_sem.at[0, b])

    def mask_copy(b):
        half = pl.ds(b * LISTED, LISTED)
        return pltpu.make_async_copy(mask_in.at[half], mask.at[half], part_sem.at[1, b])

    def out_copy(b):
        half = pl.ds(b * 4, 4)
        return pltpu.make_async_copy(out.at[half], out_to.at[half], out_sem.at[b])

    @pl.loop(0, 2)
    def _(b):
        query_copy(b).start()
        mask_copy(b).start()

        @pl.loop(0, LISTED)
        def _(l):
            e = b * LISTED + l
            row, owner_core, owner_x, sl, _, _ = fields(code[base + e])
            away = (x - owner_x) & (X - 1)
            here = (away == 0) & (owner_core == core)
            beside = (away == 0) & (owner_core != core)
            sources = ((own, row, here), (oth, row, beside), (r1, sl, away == 1))
            sources += ((r2, sl, away == 2), (r3, sl, away == 3))
            for source, at, chosen in sources:

                @pl.when(chosen)
                def _(source=source, at=at):
                    pltpu.make_async_copy(source.at[at], tiles.at[e], tile_sem.at[e]).start()

    @pl.loop(0, 2)
    def _(b):
        query_copy(b).wait()
        mask_copy(b).wait()

        @pl.loop(0, LISTED)
        def _(l):
            e = b * LISTED + l
            pltpu.make_async_copy(own.at[0], tiles.at[e], tile_sem.at[e]).wait()

        for l in range(LISTED):
            at = slice(l * BLOCK, (l + 1) * BLOCK)
            tile = tiles[b * LISTED + l].reshape(4, 2, QUARTER, WIDTH)
            kc[at, :] = tile[:, 0].reshape(BLOCK, WIDTH)
            vc[at, :] = tile[:, 1].reshape(BLOCK, WIDTH)

        for l in range(LISTED):
            at = slice(l * BLOCK, (l + 1) * BLOCK)
            kt[:, at] = kc[at, :].astype(jnp.float32).T.astype(jnp.bfloat16)
            vt[:, at] = vc[at, :].astype(jnp.float32).T.astype(jnp.bfloat16)

        quarters = pl.ds(b * 4, 4)
        for g in range(GROUP):
            at = slice(g * BLOCK, (g + 1) * BLOCK)
            qs[at, :] = qd[quarters, 0, g].reshape(BLOCK, WIDTH)
            dos[at, :] = qd[quarters, 1, g].reshape(BLOCK, WIDTH)

        def score(pair):
            q = qs[pair * rows : (pair + 1) * rows, :]
            top = jnp.full((8, rows), -jnp.inf, jnp.float32)
            for l in range(LISTED):
                at = slice(l * BLOCK, (l + 1) * BLOCK)
                s = lax.dot_general(
                    kc[at, :], q, contract_last, preferred_element_type=jnp.float32
                )
                m = mask[b * LISTED + l]
                s = jnp.minimum(s, jnp.concatenate([m, m], axis=1))
                s_scr[pair % 2, at, :] = s
                top = jnp.maximum(top, jnp.max(s.reshape(BLOCK // 8, 8, rows), axis=0))
            return jnp.max(top, axis=0, keepdims=True)

        top = score(0)
        for pair in range(GROUP // 2):
            cols = slice(pair * rows, (pair + 1) * rows)
            now = pair % 2
            total = jnp.zeros((8, rows), jnp.float32)
            for l in range(LISTED):
                at = slice(l * BLOCK, (l + 1) * BLOCK)
                w = jnp.exp2((s_scr[now, at, :] - top) * (scale * LOG2E))
                s_scr[now, at, :] = w
                total = total + jnp.sum(w.reshape(BLOCK // 8, 8, rows), axis=0)
            inverse = 1.0 / jnp.sum(total, axis=0, keepdims=True)
            if pair < GROUP // 2 - 1:
                top = score(pair + 1)
            for l in range(LISTED):
                at = slice(l * BLOCK, (l + 1) * BLOCK)
                p_scr[at, cols] = (s_scr[now, at, :] * inverse).astype(jnp.bfloat16)
            o_t = jnp.dot(vt[...], p_scr[:, cols], preferred_element_type=jnp.float32)
            do = dos[cols, :]
            do_t = do.astype(jnp.float32).T
            o_round = o_t.astype(jnp.bfloat16).astype(jnp.float32)
            row_dot = jnp.sum(o_round * do_t, axis=0, keepdims=True)
            scaled = inverse * scale
            for l in range(LISTED):
                at = slice(l * BLOCK, (l + 1) * BLOCK)
                dp = lax.dot_general(
                    vc[at, :], do, contract_last, preferred_element_type=jnp.float32
                )
                ds = ((s_scr[now, at, :] * scaled) * (dp - row_dot)).astype(jnp.bfloat16)
                d_scr[at, cols] = ds
            dq_t = jnp.dot(kt[...], d_scr[:, cols], preferred_element_type=jnp.float32)
            o = o_t.T.astype(jnp.bfloat16)
            dq = dq_t.T.astype(jnp.bfloat16)
            for i in range(2):
                at = slice(i * BLOCK, (i + 1) * BLOCK)
                out[quarters, 0, 2 * pair + i] = o[at].reshape(4, QUARTER, WIDTH)
                out[quarters, 1, 2 * pair + i] = dq[at].reshape(4, QUARTER, WIDTH)

        here = pl.ds(b * LISTED, LISTED)
        dk[here] = jnp.dot(d_scr[...], qs[...], preferred_element_type=jnp.float32).reshape(LISTED, BLOCK, WIDTH)
        dv[here] = jnp.dot(p_scr[...], dos[...], preferred_element_type=jnp.float32).reshape(LISTED, BLOCK, WIDTH)

        out_copy(b).start()

    @pl.loop(LISTED, ENTRIES)
    def _(e):
        *_, fresh, f = fields(code[base + e])

        @pl.when(fresh == 0)
        def _():
            dk[f] += dk[e]
            dv[f] += dv[e]

    def back_copies(e, act):
        _, _, owner_x, sl, fresh, _ = fields(code[base + e])
        away = (x - owner_x) & (X - 1)
        for k, buf in ((0, g0), (1, g1), (2, g2), (3, g3)):

            @pl.when((fresh == 1) & (away == k))
            def _(buf=buf):
                act(pltpu.make_async_copy(tiles.at[e], buf.at[sl], back_sem.at[e]))

    @pl.loop(0, ENTRIES)
    def _(e):
        parts = [dk[e].reshape(4, 1, QUARTER, WIDTH), dv[e].reshape(4, 1, QUARTER, WIDTH)]
        tile = jnp.concatenate(parts, axis=1).astype(jnp.bfloat16)
        tiles[e] = tile.reshape(2 * BLOCK, WIDTH)
        back_copies(e, lambda copy: copy.start())

    @pl.loop(0, ENTRIES)
    def _(e):
        back_copies(e, lambda copy: copy.wait())

    @pl.loop(0, 2)
    def _(b):
        out_copy(b).wait()


def blocks(count):
    return jax.ShapeDtypeStruct((count, 2 * BLOCK, WIDTH), jnp.bfloat16)


def shift(array, axis, by):
    size = lax.axis_size(axis)
    return lax.ppermute(array, axis, [(i, (i + by) % size) for i in range(size)])


def params(mib):
    return pltpu.CompilerParams(vmem_limit_bytes=mib * MIB)


def exchange(array, axis):
    return lax.all_to_all(array, axis, split_axis=0, concat_axis=0, tiled=True)


def gather(slots, *operands):
    return pl.pallas_call(
        gather_kernel,
        out_shape=[blocks(slots)] * 3,
        in_specs=[SMEM] + [HBM] * 2,
        out_specs=[HBM] * 3,
        scratch_shapes=[DMA((X * ENTRIES,))],
        compiler_params=params(4),
    )(*operands)


def scatter(*operands):
    return pl.pallas_call(
        scatter_kernel,
        out_shape=[blocks(ENTRIES)] * 2,
        in_specs=[SMEM] + [VMEM] * 4,
        out_specs=[VMEM] * 2,
        scratch_shapes=[pltpu.VMEM((2 * ENTRIES, 2 * BLOCK, WIDTH), jnp.float32)],
        compiler_params=params(14),
    )(*operands)


def add_kernel(left, right, total):
    total[...] = (left[...].astype(jnp.float32) + right[...].astype(jnp.float32)).astype(jnp.bfloat16)


def add(*operands):
    return pl.pallas_call(
        add_kernel,
        out_shape=blocks(ENTRIES),
        in_specs=[VMEM] * 2,
        out_specs=VMEM,
        compiler_params=params(8),
    )(*operands)


def masks(*operands):
    return pl.pallas_call(
        mask_kernel,
        out_shape=jax.ShapeDtypeStruct((ENTRIES, BLOCK, BLOCK), jnp.float32),
        in_specs=[SMEM] * 3 + [VMEM],
        out_specs=VMEM,
        compiler_params=params(4),
        cost_estimate=pl.CostEstimate(flops=ENTRIES * BLOCK * BLOCK * 8, bytes_accessed=MIB, transcendentals=0),
    )(*operands)


def attend(slots, *operands):
    outs = jax.ShapeDtypeStruct((HEAD, 2, GROUP, QUARTER, WIDTH), jnp.bfloat16)
    return pl.pallas_call(
        attend_kernel,
        out_shape=[outs, blocks(ENTRIES)] + [blocks(slots)] * 3,
        in_specs=[SMEM] * 2 + [HBM] * 7,
        out_specs=[HBM] * 5,
        scratch_shapes=[
            pltpu.VMEM((HEAD, 2, GROUP, QUARTER, WIDTH), jnp.bfloat16),
            pltpu.VMEM((ENTRIES, 2 * BLOCK, WIDTH), jnp.bfloat16),
            pltpu.VMEM((ENTRIES, BLOCK, BLOCK), jnp.float32),
            pltpu.VMEM((HEAD, 2, GROUP, QUARTER, WIDTH), jnp.bfloat16),
            pltpu.VMEM((LISTED * BLOCK, WIDTH), jnp.bfloat16),
            pltpu.VMEM((LISTED * BLOCK, WIDTH), jnp.bfloat16),
            pltpu.VMEM((WIDTH, LISTED * BLOCK), jnp.bfloat16),
            pltpu.VMEM((WIDTH, LISTED * BLOCK), jnp.bfloat16),
            pltpu.VMEM((GROUP * BLOCK, WIDTH), jnp.bfloat16),
            pltpu.VMEM((GROUP * BLOCK, WIDTH), jnp.bfloat16),
            pltpu.VMEM((2, LISTED * BLOCK, 2 * BLOCK), jnp.float32),
            pltpu.VMEM((LISTED * BLOCK, GROUP * BLOCK), jnp.bfloat16),
            pltpu.VMEM((LISTED * BLOCK, GROUP * BLOCK), jnp.bfloat16),
            pltpu.VMEM((ENTRIES, BLOCK, WIDTH), jnp.float32),
            pltpu.VMEM((ENTRIES, BLOCK, WIDTH), jnp.float32),
            DMA((ENTRIES,)),
            DMA((2, 2)),
            DMA((2,)),
            DMA((ENTRIES,)),
        ],
        compiler_params=params(50),
        cost_estimate=pl.CostEstimate(
            flops=5 * 2 * 2048 * 1024 * 128, bytes_accessed=8 * MIB, transcendentals=2048 * 1024
        ),
    )(*operands)


def between(slots, place, code, lists, own, qd, mask):
    other = shift(own, "core", 1)
    sends = gather(slots, lists, own, other)
    r2, r1, r3 = [shift(sends[k - 1], "x", k) for k in (2, 1, 3)]
    qd = exchange(qd, "head")
    out, g0, g1, g2, g3 = attend(
        slots, place, code, qd, own, other, r1, r2, r3, mask
    )

    g2, g1, g3 = [shift(g, "x", -k) for k, g in ((2, g2), (1, g1), (3, g3))]
    out = exchange(out, "head")
    g1, g2, g3, out = lax.optimization_barrier((g1, g2, g3, out))
    own_sum, other_sum = scatter(lists, g0, g1, g2, g3)
    from_core = shift(other_sum, "core", 1)
    column_sum = add(own_sum, from_core)
    return out, column_sum


def per_device(queries, keys, values, output_gradient, kv_list, kv_type, session_id):
    where = [lax.axis_index(axis).astype(jnp.int32) for axis in ("z", "x", "core")]
    place = jnp.stack(where)

    code, most = coded(kv_list)
    sess = session_id.astype(jnp.float32).reshape(-1, BLOCK)

    lists = neighbour_lists(where, code)
    code, most, lists = lax.optimization_barrier((code, most, lists))

    kv = jnp.stack([keys, values]).transpose(2, 0, 1, 3)
    kv = jnp.broadcast_to(kv, (Z, HEAD, 2, QUARTER, WIDTH))
    own = exchange(kv.reshape(Z * HEAD, 2, QUARTER, WIDTH), ("z", "head"))
    own = own.reshape(ENTRIES, 2 * BLOCK, WIDTH)

    qd = jnp.stack([queries, output_gradient]).reshape(2, QUARTER, HEAD, GROUP, WIDTH)
    qd = qd.transpose(2, 0, 3, 1, 4)
    mask = masks(place, kv_list.T, kv_type.T, sess)
    qd, mask = lax.optimization_barrier((qd, mask))

    out, column_sum = lax.switch(
        sum((most > few).astype(jnp.int32) for few in SLOTS[:-1]),
        [functools.partial(between, slots) for slots in SLOTS],
        place, code, lists, own, qd, mask,
    )

    parts = exchange(column_sum.reshape(Z * HEAD, 2, QUARTER, WIDTH), ("z", "head"))
    parts = parts.reshape(Z, HEAD, 2, QUARTER, WIDTH)
    total = jnp.sum(parts.astype(jnp.float32), axis=0).astype(jnp.bfloat16)
    total = total.transpose(1, 2, 0, 3)

    out = out.transpose(1, 3, 0, 2, 4).reshape(2, QUARTER, HEAD * GROUP, WIDTH)
    return out[0], out[1], total[0], total[1]


def solution(mesh):
    fine = Mesh(mesh.devices.reshape(Z, X, CORE, HEAD), ("z", "x", "core", "head"))
    split = P(("z", "x", "core", "head"), None, None)
    return jax.shard_map(
        per_device,
        mesh=fine,
        in_specs=(split,) * 4 + (P(),) * 3,
        out_specs=(split,) * 4,
        check_vma=False,
    )
```
